128 devices in a mesh: member: 8 (over y, x_hi), grid: 16 (over x_lo, z, core).
Axes of the slice: x: 4 (x_hi: 2, x_lo: 2; x = x_hi * 2 + x_lo), y: 4, z: 4, core: 2. Of those that a mesh axis runs over, the one named last changes fastest.
Arguments:
- latents: bfloat16 [8, 32768, 1024], P('member', 'grid'), may hold values from -6 to 6
- hidden_weight: bfloat16 [1024, 1024], replicated, may hold values from -0.1875 to 0.1875
- output_weight: bfloat16 [1024, 100], replicated, may hold values from -0.1875 to 0.1875
- observed: float32 [100, 32768], P(None, 'grid'), may hold values from -6 to 6
- node_area_weight: float32 [32768], P('grid'), may hold values from 0.3 to 3
Outputs:
- grad_latents: bfloat16 [8, 32768, 1024], P('member', 'grid')
- grad_first: float32 [1024, 1024], P('grid')
- grad_second: float32 [1024, 100], P('grid')
The draws below stay inside these ranges and needn't reach their ends.
All inputs are finite; a program needn't handle non-finite values.
Results may differ from the reference program's by a relative error of at most 0.018.
Values may be sent and summed in bfloat16 or wider, within the bound.
No kernel may reach another device: no remote copies, remote signals or barrier semaphores. Data moves between devices by JAX's collectives and lax.ppermute only.
A program may use at most 128 MiB of HBM per device.

```python
import math
import jax
import jax.numpy as jnp
from jax import lax

D = 1024
V = 100
MEMBERS = 8
NODES = 32768


def strengthened(entries, own_key, source, target, shards_of, factor):
    owner, partner = [(jnp.arange(entries.shape[axis_at]) // (entries.shape[axis_at] // shards_of)).reshape([-1 if axis == axis_at else 1 for axis in range(entries.ndim)]) for axis_at in (source, target)]
    chosen = jax.random.permutation(own_key, shards_of)[partner]
    strong = (owner == chosen) | (owner == (partner + shards_of // 2) % shards_of)
    return jnp.where(strong, factor * entries, entries)


def steps_of(key, extent, cuts, low, top_value):
    def one(dim, parts):
        draws = jax.random.uniform(jax.random.fold_in(jax.random.fold_in(key, 6), dim), (parts,), jnp.float32, low / len(cuts), top_value / len(cuts))
        return jnp.repeat(jnp.exp(draws), extent[dim] // parts).reshape((-1,) + (1,) * (len(extent) - dim - 1))

    gain = one(*cuts[0])
    for cut in cuts[1:]:
        gain = gain * one(*cut)
    return gain


def bell_draw(own_key, dims, scale, bound, shards=(), dtype=jnp.bfloat16):
    result = jax.random.normal(own_key, dims, jnp.float32) * scale
    if len(shards) > 0:
        result = steps_of(own_key, dims, shards, -0.22, 0.18) * result
    return jnp.clip(result, min=-bound, max=bound).astype(dtype)


def bell_draw_with(rng, dims, scale, bound, split, heavy, dtype=jnp.bfloat16):
    result = scale * jax.random.normal(rng, dims, jnp.float32)
    if split:
        result = result * steps_of(rng, dims, split, -0.22, 0.18)
    return jnp.clip(strengthened(result, jax.random.fold_in(rng, 3), *heavy), -bound, bound).astype(dtype)


def setup_inputs(seed: int = 0) -> dict:
    seeds = jax.random.split(jax.random.key(seed), 6)
    latents = bell_draw_with(seeds[0], (MEMBERS, NODES, D), 1.0, 6.0, ((0, 8), (1, 16)), (1, 2, 16, 2.0))
    hidden_weight = bell_draw(seeds[1], (D, D), D ** -0.5, 0.1875)
    output_weight = bell_draw(seeds[2], (D, V), D ** -0.5, 0.1875)
    observed = bell_draw(seeds[3], (V, NODES), 1.0, 6.0, ((1, 16),), jnp.float32)
    node_area_weight = jnp.clip(jnp.exp(math.log(3.0) - 2.3025851 * jax.random.uniform(seeds[4], (NODES,), jnp.float32) ** steps_of(seeds[4], (NODES,), ((0, 16),), -0.2, 0.2)), 0.3, 3.0)
    return dict(latents=latents, hidden_weight=hidden_weight, output_weight=output_weight, observed=observed, node_area_weight=node_area_weight)


smooth_sq = 0.0025

def slope_function(diff):
    return diff / jnp.sqrt(diff * diff + smooth_sq)

def forward_decode(latent_state, hidden_weight, output_weight):
    pre_activation = jnp.dot(latent_state, hidden_weight, preferred_element_type=jnp.float32)
    gate_sigmoid = jax.nn.sigmoid(pre_activation)
    hidden_activation = (pre_activation * gate_sigmoid).astype(jnp.bfloat16)
    single_prediction = lax.dot_general(output_weight, hidden_activation, (((0,), (1,)), ((), ())), preferred_element_type=jnp.float32)
    return (pre_activation, gate_sigmoid, hidden_activation, single_prediction)

def backward(latent_state, grad_low, hidden_weight, output_weight):
    pre_activation, gate_sigmoid, hidden_activation, unused = forward_decode(latent_state, hidden_weight, output_weight)
    grad_hidden = lax.dot_general(grad_low, output_weight, (((0,), (1,)), ((), ())), preferred_element_type=jnp.float32)
    grad_pre = (grad_hidden * gate_sigmoid * (1.0 + pre_activation * (1.0 - gate_sigmoid))).astype(jnp.bfloat16)
    part_second = lax.dot_general(hidden_activation, grad_low, (((0,), (1,)), ((), ())), preferred_element_type=jnp.float32)
    part_first = lax.dot_general(latent_state, grad_pre, (((0,), (0,)), ((), ())), preferred_element_type=jnp.float32)
    grad_latent = lax.dot_general(grad_pre, hidden_weight, (((1,), (1,)), ((), ())), preferred_element_type=jnp.float32).astype(jnp.bfloat16)
    return (part_first, part_second, grad_latent)

def reference(latents, hidden_weight, output_weight, observed, node_area_weight):
    ensemble_predictions = lax.map(lambda latent_state: forward_decode(latent_state, hidden_weight, output_weight)[3], latents)
    member_list = latents.shape[0]
    pairwise_sum = jnp.zeros_like(ensemble_predictions)
    for other_member in range(member_list):
        pairwise_sum = pairwise_sum + slope_function(ensemble_predictions - ensemble_predictions[other_member][None])
    field_gradient = node_area_weight[None, None, :] * (slope_function(ensemble_predictions - observed[None]) - pairwise_sum / (member_list - 1))
    grad_low = field_gradient.astype(jnp.bfloat16)

    def step_member(carry, items):
        latent_state, low = items
        part_first, part_second, grad_latent = backward(latent_state, low, hidden_weight, output_weight)
        return ((carry[0] + part_first, carry[1] + part_second), grad_latent)
    init = (jnp.zeros((D, D), jnp.float32), jnp.zeros((D, V), jnp.float32))
    sums, grad_latents = lax.scan(step_member, init, (latents, grad_low))
    factor = 1.0 / math.sqrt(member_list * NODES)
    return (grad_latents, sums[0] * factor, sums[1] * factor)
```

```python
import math

import jax
import jax.numpy as jnp
from jax import lax
from jax.sharding import PartitionSpec as P

smooth_sq = 0.0025
bf16 = jnp.bfloat16
f32 = jnp.float32


def slope_function(diff):
    return diff * lax.rsqrt(diff * diff + smooth_sq)


def moved(value, move):
    pairs = []
    for member in range(8):
        for grid in range(16):
            y, x_hi, x_lo, z, core = member // 2, member % 2, grid // 8, (grid // 2) % 4, grid % 2
            y, x, z, core = move(y, x_hi * 2 + x_lo, z, core)
            target = (y * 2 + x // 2) * 16 + ((x % 2) * 4 + z) * 2 + core
            pairs.append((member * 16 + grid, target))
    return lax.ppermute(value, ("member", "grid"), pairs)


def summed(own, others):
    total = own.astype(f32)
    for other in others:
        total = total + other.astype(f32)
    return total


def reduced(part):
    grid = lax.axis_index("grid")
    x_lo, z, core = grid // 8, (grid // 2) % 4, grid % 2
    columns = part.shape[1]
    blocks = part.reshape(2, 4, 2, 64, columns)

    def pick(array, index, axis):
        return lax.dynamic_index_in_dim(array, index, axis, keepdims=False)

    got = moved(pick(blocks, 1 - core, 2), lambda y, x, z, c: (y, x, z, 1 - c))
    blocks = summed(pick(blocks, core, 2), [got]).astype(bf16)
    got = [
        moved(pick(blocks, (z + k) % 4, 1), lambda y, x, z, c, k=k: (y, x, (z + k) % 4, c))
        for k in (1, 2, 3)
    ]
    blocks = summed(pick(blocks, z, 1), got).astype(bf16)
    mine, theirs = pick(blocks, x_lo, 0), pick(blocks, 1 - x_lo, 0)
    got = [
        moved(mine if k == 2 else theirs, lambda y, x, z, c, k=k: (y, x ^ k, z, c))
        for k in (1, 2, 3)
    ]
    block = summed(mine, got).astype(bf16)
    got = [moved(block, lambda y, x, z, c, k=k: ((y + k) % 4, x, z, c)) for k in (1, 2, 3)]
    return summed(block, got)


def body(latents, hidden_weight, output_weight, observed, node_area_weight):
    latent_state = latents[0]
    member_list = lax.axis_size("member")
    groups = lax.axis_size("grid")
    node_count = latent_state.shape[0]
    variables = output_weight.shape[1]
    pre_activation = jnp.dot(latent_state, hidden_weight, preferred_element_type=f32)
    gate_sigmoid = jax.nn.sigmoid(pre_activation)
    hidden_activation = (pre_activation * gate_sigmoid).astype(bf16)
    forecast = lax.dot_general(
        output_weight, hidden_activation, (((0,), (1,)), ((), ())), preferred_element_type=f32
    )
    share = node_count // member_list
    blocks = forecast.reshape(variables, member_list, share).transpose(1, 0, 2)
    blocks = (0.25 * blocks).astype(jnp.float16)
    blocks = lax.all_to_all(blocks, "member", 0, 0, tiled=True)
    blocks = 4.0 * blocks.astype(f32)
    place = lax.axis_index("member") * share
    here = lax.dynamic_slice_in_dim(observed, place, share, 1)
    weight = lax.dynamic_slice_in_dim(node_area_weight, place, share, 0)
    pairwise = [0.0] * member_list
    for a in range(member_list):
        for b in range(a + 1, member_list):
            slope = slope_function(blocks[a] - blocks[b])
            pairwise[a] = pairwise[a] + slope
            pairwise[b] = pairwise[b] - slope
    low = jnp.stack(
        [
            weight[None, :] * (slope_function(blocks[a] - here) - pairwise[a] / (member_list - 1))
            for a in range(member_list)
        ]
    ).astype(bf16)
    low = lax.all_to_all(low, "member", 0, 0, tiled=True)
    grad_low = low.transpose(1, 0, 2).reshape(variables, node_count)
    grad_hidden = lax.dot_general(
        grad_low, output_weight, (((0,), (1,)), ((), ())), preferred_element_type=f32
    )
    grad_pre = (grad_hidden * gate_sigmoid * (1.0 + pre_activation * (1.0 - gate_sigmoid))).astype(
        bf16
    )
    part_second = lax.dot_general(
        hidden_activation, grad_low, (((0,), (1,)), ((), ())), preferred_element_type=f32
    )
    part_first = lax.dot_general(
        latent_state, grad_pre, (((0,), (0,)), ((), ())), preferred_element_type=f32
    )
    part = jnp.concatenate(
        [part_first.astype(bf16), jnp.pad(part_second.astype(bf16), ((0, 0), (0, 128 - variables)))], axis=1
    )
    total = reduced(part)
    grad_latent = lax.dot_general(
        grad_pre, hidden_weight, (((1,), (1,)), ((), ())), preferred_element_type=f32
    ).astype(bf16)
    factor = 1.0 / math.sqrt(member_list * node_count * groups)
    width = part_first.shape[1]
    return (grad_latent[None], total[:, :width] * factor, total[:, width : width + variables] * factor)


def solution(mesh):
    in_specs = (P("member", "grid", None), P(), P(), P(None, "grid"), P("grid"))
    out_specs = (P("member", "grid", None), P("grid", None), P("grid", None))
    return jax.shard_map(body, mesh=mesh, in_specs=in_specs, out_specs=out_specs, check_vma=False)
```

```python
import functools
import math

import jax
import jax.numpy as jnp
from jax import lax
from jax.experimental import pallas as pl
from jax.experimental.pallas import tpu as pltpu
from jax.sharding import PartitionSpec as P

smooth_sq = 0.0025
bf16 = jnp.bfloat16
f16 = jnp.float16
f32 = jnp.float32

NT = (((1,), (1,)), ((), ()))
WIDE = 128
TALL = 112
SHARE = 256


def params(mib):
    return pltpu.CompilerParams(vmem_limit_bytes=mib * 1024 * 1024)


def cost(flops, nbytes, trans=0):
    return pl.CostEstimate(flops=flops, bytes_accessed=nbytes, transcendentals=trans)


def forward_kernel(latent_ref, weight_ref, out_weight_ref, forecast_ref, hidden_ref, slope_ref, padded_ref):
    rows, width = latent_ref.shape
    variables = out_weight_ref.shape[1]

    @pl.when(pl.program_id(0) == 0)
    def _():
        padded_ref[...] = jnp.concatenate(
            [out_weight_ref[...], jnp.zeros((width, WIDE - variables), bf16)], axis=1
        )

    for start in range(0, width, 256):
        columns = slice(start, start + 256)
        pre = jnp.dot(latent_ref[...], weight_ref[:, columns], preferred_element_type=f32)
        sig = 1.0 / (1.0 + jnp.exp(-pre))
        hidden_ref[:, columns] = (pre * sig).astype(bf16)
        slope_ref[:, columns] = (sig * (1.0 + pre * (1.0 - sig))).astype(bf16)
    for share in range(rows // SHARE):
        forecast = jnp.dot(
            hidden_ref[share * SHARE : (share + 1) * SHARE, :], padded_ref[...], preferred_element_type=f32
        )
        forecast_ref[share] = forecast.T[:TALL].astype(forecast_ref.dtype)


def forward(latent, weight, out_weight):
    nodes, width = latent.shape
    variables = out_weight.shape[1]
    rows = 512
    return pl.pallas_call(
        forward_kernel,
        grid=(nodes // rows,),
        in_specs=[
            pl.BlockSpec((rows, width), lambda i: (i, 0)),
            pl.BlockSpec((width, width), lambda i: (0, 0)),
            pl.BlockSpec((width, variables), lambda i: (0, 0)),
        ],
        out_specs=[
            pl.BlockSpec((rows // SHARE, TALL, SHARE), lambda i: (i, 0, 0)),
            pl.BlockSpec((rows, width), lambda i: (i, 0)),
            pl.BlockSpec((rows, width), lambda i: (i, 0)),
            pl.BlockSpec((width, WIDE), lambda i: (0, 0)),
        ],
        out_shape=[
            jax.ShapeDtypeStruct((nodes // SHARE, TALL, SHARE), f32),
            jax.ShapeDtypeStruct((nodes, width), bf16),
            jax.ShapeDtypeStruct((nodes, width), bf16),
            jax.ShapeDtypeStruct((width, WIDE), bf16),
        ],
        compiler_params=params(32),
        cost_estimate=cost(2 * nodes * width * (width + WIDE), 20 << 20),
        name="forward",
    )(latent, weight, out_weight)


def slope_function(diff):
    return diff * lax.rsqrt(diff * diff + smooth_sq)


def pair_kernel(place_ref, blocks_ref, observed_ref, area_ref, low_ref):
    members = blocks_ref.shape[0]
    variables = observed_ref.shape[0]
    for start in range(0, TALL, 16):
        rows = slice(start, start + 16)
        real = min(16, variables - start)
        observed = observed_ref[start : start + real, :]
        if real < 16:
            observed = jnp.concatenate([observed, jnp.zeros((16 - real, SHARE), f32)], axis=0)
        values = [blocks_ref[a, rows, :] for a in range(members)]
        totals = [0.0] * members
        for a in range(members):
            for b in range(a + 1, members):
                slope = slope_function(values[a] - values[b])
                totals[a] = totals[a] + slope
                totals[b] = totals[b] - slope
        for a in range(members):
            field = area_ref[...] * (slope_function(values[a] - observed) - totals[a] * (1.0 / (members - 1)))
            low_ref[a, rows, :] = field.astype(bf16)


def pairs(place, blocks, observed, area):
    members = blocks.shape[0]
    variables = observed.shape[0]
    return pl.pallas_call(
        pair_kernel,
        grid_spec=pltpu.PrefetchScalarGridSpec(
            num_scalar_prefetch=1,
            grid=(1,),
            in_specs=[
                pl.BlockSpec((members, TALL, SHARE), lambda i, place: (0, 0, 0)),
                pl.BlockSpec((variables, SHARE), lambda i, place: (0, place[0])),
                pl.BlockSpec((1, SHARE), lambda i, place: (0, place[0])),
            ],
            out_specs=pl.BlockSpec((members, TALL, SHARE), lambda i, place: (0, 0, 0)),
        ),
        out_shape=jax.ShapeDtypeStruct((members, TALL, SHARE), bf16),
        compiler_params=params(16),
        cost_estimate=cost(4 << 20, 2 << 20),
        name="pairs",
    )(place, blocks, observed, area)


def place_rows(order_ref, group, block, store):
    core = order_ref[8]
    at = order_ref[group] * 64
    store(pl.multiple_of(core * 512 + at, 64), block[:64])
    store(pl.multiple_of((1 - core) * 512 + at, 64), block[64:])


def turn_kernel(order_ref, latent_ref, turned_ref):
    def store(at, value):
        turned_ref[pl.ds(at, 64), :] = value

    for group in range(8):
        block = latent_ref[:, group * 128 : (group + 1) * 128].T
        place_rows(order_ref, group, block, store)


def turned(order, latent):
    nodes, width = latent.shape
    rows = 512
    return pl.pallas_call(
        turn_kernel,
        grid_spec=pltpu.PrefetchScalarGridSpec(
            num_scalar_prefetch=1,
            grid=(nodes // rows,),
            in_specs=[pl.BlockSpec((rows, width), lambda i, order: (i, 0))],
            out_specs=pl.BlockSpec((width, rows), lambda i, order: (0, i)),
        ),
        out_shape=jax.ShapeDtypeStruct((width, nodes), bf16),
        compiler_params=params(16),
        cost_estimate=cost(0, 8 << 20),
        name="turned",
    )(order, latent)


def backward_kernel(
    order_ref, low_ref, turned_ref, slope_ref, hidden_ref, padded_ref, pre_ref, send_ref, keep_ref, turn_ref, flat_ref, second_ref
):
    step = pl.program_id(0)
    steps = pl.num_programs(0)
    nodes = turn_ref.shape[0]
    width = turned_ref.shape[0]
    shares = low_ref.shape[0]
    half = width // 2

    @pl.when(step == 0)
    def _():
        for share in range(shares):
            columns = slice(share * SHARE, (share + 1) * SHARE)
            low = jnp.concatenate([low_ref[share], jnp.zeros((WIDE - TALL, SHARE), bf16)], axis=0)
            flat_ref[:, columns] = low
            turn_ref[columns, :] = low.T

    for start in range(0, nodes, 512):
        rows = slice(start, start + 512)
        grad_hidden = lax.dot_general(turn_ref[rows, :], padded_ref[...], NT, preferred_element_type=f32)
        pre_ref[rows, :] = (grad_hidden * slope_ref[rows, :].astype(f32)).astype(bf16)
    for out_ref, base in ((send_ref, 0), (keep_ref, half)):
        for start in range(0, half, 256):
            rows = slice(start, start + 256)
            part = jnp.dot(turned_ref[base + start : base + start + 256, :], pre_ref[...], preferred_element_type=f32)
            out_ref[rows, pl.ds(pl.multiple_of(step * 256, 256), 256)] = part.astype(bf16)
    second_ref[step] = jnp.dot(flat_ref[...], hidden_ref[...], preferred_element_type=f32).T

    @pl.when(step == steps - 1)
    def _():
        for group in range(8):
            block = second_ref[group // 2, (group % 2) * 128 : (group % 2 + 1) * 128, :].astype(bf16)
            at = pl.multiple_of(order_ref[group] * 64, 64)
            first_core = order_ref[8] == 1
            mine = jnp.where(first_core, block[:64], block[64:])
            other = jnp.where(first_core, block[64:], block[:64])
            keep_ref[pl.ds(at, 64), width : width + WIDE] = mine
            send_ref[pl.ds(at, 64), width : width + WIDE] = other


def backward(order, low, turned_latent, slope, hidden, padded):
    nodes, width = slope.shape
    half = width // 2
    total = width + WIDE
    return pl.pallas_call(
        backward_kernel,
        grid_spec=pltpu.PrefetchScalarGridSpec(
            num_scalar_prefetch=1,
            grid=(width // 256,),
            in_specs=[
                pl.BlockSpec(low.shape, lambda i, order: (0, 0, 0)),
                pl.BlockSpec((width, nodes), lambda i, order: (0, 0)),
                pl.BlockSpec((nodes, 256), lambda i, order: (0, i)),
                pl.BlockSpec((nodes, 256), lambda i, order: (0, i)),
                pl.BlockSpec((256, WIDE), lambda i, order: (i, 0)),
            ],
            out_specs=[
                pl.BlockSpec((nodes, 256), lambda i, order: (0, i)),
                pl.BlockSpec((half, total), lambda i, order: (0, 0)),
                pl.BlockSpec((half, total), lambda i, order: (0, 0)),
            ],
            scratch_shapes=[
                pltpu.VMEM((nodes, WIDE), bf16),
                pltpu.VMEM((WIDE, nodes), bf16),
                pltpu.VMEM((width // 256, 256, WIDE), f32),
            ],
        ),
        out_shape=[
            jax.ShapeDtypeStruct((nodes, width), bf16),
            jax.ShapeDtypeStruct((half, total), bf16),
            jax.ShapeDtypeStruct((half, total), bf16),
        ],
        compiler_params=params(36),
        cost_estimate=cost(2 * nodes * width * (width + 2 * WIDE), 20 << 20),
        name="backward",
    )(order, low, turned_latent, slope, hidden, padded)


def latent_kernel(pre_ref, weight_ref, out_ref):
    rows, width = pre_ref.shape
    for start in range(0, width, 256):
        columns = slice(start, start + 256)
        out_ref[:, columns] = lax.dot_general(
            pre_ref[...], weight_ref[columns, :], NT, preferred_element_type=f32
        ).astype(bf16)


def latent_gradient(grad_pre, weight):
    nodes, width = grad_pre.shape
    rows = 512
    return pl.pallas_call(
        latent_kernel,
        grid=(nodes // rows,),
        in_specs=[
            pl.BlockSpec((rows, width), lambda i: (i, 0)),
            pl.BlockSpec((width, width), lambda i: (0, 0)),
        ],
        out_specs=pl.BlockSpec((rows, width), lambda i: (i, 0)),
        out_shape=jax.ShapeDtypeStruct((nodes, width), bf16),
        compiler_params=params(24),
        cost_estimate=cost(2 * nodes * width * width, 10 << 20),
        name="latent_gradient",
    )(grad_pre, weight)


def moved(value, move):
    moves = []
    for member in range(8):
        for grid in range(16):
            y, x_hi, x_lo, z, core = member // 2, member % 2, grid // 8, (grid // 2) % 4, grid % 2
            y, x, z, core = move(y, x_hi * 2 + x_lo, z, core)
            target = (y * 2 + x // 2) * 16 + ((x % 2) * 4 + z) * 2 + core
            moves.append((member * 16 + grid, target))
    return lax.ppermute(value, ("member", "grid"), moves)


def summed(own, others):
    total = own.astype(f32)
    for other in others:
        total = total + other.astype(f32)
    return total


def reduced(send, keep):
    columns = send.shape[1]
    got = moved(send, lambda y, x, z, c: (y, x, z, 1 - c))
    blocks = summed(keep, [got]).astype(bf16).reshape(4, 2, 64, columns)
    got = [moved(blocks[k], lambda y, x, z, c, k=k: (y, x, (z + k) % 4, c)) for k in (1, 3, 2)]
    blocks = summed(blocks[0], got).astype(bf16)
    got = [
        moved(blocks[0] if k == 2 else blocks[1], lambda y, x, z, c, k=k: (y, x ^ k, z, c))
        for k in (1, 3, 2)
    ]
    block = summed(blocks[0], got).astype(bf16)
    got = [moved(block, lambda y, x, z, c, k=k: ((y + k) % 4, x, z, c)) for k in (1, 3, 2)]
    return summed(block, got)


def body(latents, hidden_weight, output_weight, observed, node_area_weight):
    latent = latents[0]
    members = lax.axis_size("member")
    groups = lax.axis_size("grid")
    nodes, width = latent.shape
    variables = output_weight.shape[1]
    member = lax.axis_index("member")
    grid = lax.axis_index("grid")
    x_lo, z, core = grid // 8, (grid // 2) % 4, grid % 2
    order = jnp.stack(
        [((g % 4 - z) % 4) * 2 + jnp.abs(g // 4 - x_lo) for g in range(8)] + [1 - core]
    ).astype(jnp.int32)
    place = member.astype(jnp.int32).reshape(1)

    forecast, hidden, slope, padded = forward(latent, hidden_weight, output_weight)
    blocks = lax.all_to_all((0.25 * forecast).astype(f16), "member", 0, 0, tiled=True)
    low = pairs(place, 4.0 * blocks.astype(f32), observed, node_area_weight.reshape(1, nodes))
    low = lax.all_to_all(low, "member", 0, 0, tiled=True)
    turned_latent = turned(order, latent)
    grad_pre, send, keep = backward(order, low, turned_latent, slope, hidden, padded)
    total = reduced(send, keep)
    grad_latent = latent_gradient(grad_pre, hidden_weight)
    factor = 1.0 / math.sqrt(members * nodes * groups)
    return (grad_latent[None], total[:, :width] * factor, total[:, width : width + variables] * factor)


def solution(mesh):
    in_specs = (P("member", "grid", None), P(), P(), P(None, "grid"), P("grid"))
    out_specs = (P("member", "grid", None), P("grid", None), P("grid", None))
    return jax.shard_map(body, mesh=mesh, in_specs=in_specs, out_specs=out_specs, check_vma=False)
```

```python
import functools
import math

import jax
import jax.numpy as jnp
from jax import lax
from jax.experimental import pallas as pl
from jax.experimental.pallas import tpu as pltpu
from jax.sharding import PartitionSpec as P

smooth_sq = 0.0025
bf16 = jnp.bfloat16
f16 = jnp.float16
f32 = jnp.float32

NT = (((1,), (1,)), ((), ()))
WIDE = 128
TALL = 112
SHARE = 256
ROWS = 512
COLS = 256

vmem = pl.BlockSpec(memory_space=pltpu.VMEM)
smem = pl.BlockSpec(memory_space=pltpu.SMEM)
anywhere = pl.BlockSpec(memory_space=pltpu.HBM)


def params(mib):
    return pltpu.CompilerParams(vmem_limit_bytes=mib * 1024 * 1024)


def cost(flops, nbytes, trans=0):
    return pl.CostEstimate(flops=flops, bytes_accessed=nbytes, transcendentals=trans)


CHUNKS = (512, 512, 1024)
FCOLS = 512


def forward_kernel(
    latent_ref, weight_ref, out_weight_ref, forecast_ref, hidden_ref, slope_ref, latent_copy, weight_copy, padded_ref, out_weight_copy, latent_sems, weight_sems, out_weight_sem
):
    nodes, width = latent_ref.shape
    variables = out_weight_ref.shape[0]
    out_weight_load = pltpu.make_async_copy(out_weight_ref, out_weight_copy, out_weight_sem)
    spans = []
    for size in CHUNKS:
        begin = spans[-1].stop if spans else 0
        spans.append(slice(begin, begin + size))
    weight_loads = [
        pltpu.make_async_copy(
            weight_ref.at[:, pl.ds(start, FCOLS)], weight_copy.at[:, pl.ds(start, FCOLS)], weight_sems.at[start // FCOLS]
        )
        for start in range(0, width, FCOLS)
    ]
    latent_loads = [
        pltpu.make_async_copy(
            latent_ref.at[pl.ds(rows.start, rows.stop - rows.start)],
            latent_copy.at[pl.ds(rows.start, rows.stop - rows.start)],
            latent_sems.at[index],
        )
        for index, rows in enumerate(spans)
    ]
    weight_loads[0].start()
    latent_loads[0].start()
    for load in weight_loads[1:] + latent_loads[1:]:
        load.start()
    out_weight_load.start()
    out_weight_load.wait()
    turned_weight = jnp.concatenate(
        [out_weight_copy[...], jnp.zeros((WIDE - variables, width), bf16)], axis=0
    )
    padded_ref[...] = turned_weight.T

    for index, rows in enumerate(spans):
        latent_loads[index].wait()
        for start in range(0, width, FCOLS):
            columns = slice(start, start + FCOLS)
            if index == 0:
                weight_loads[start // FCOLS].wait()
            pre = jnp.dot(latent_copy[rows, :], weight_copy[:, columns], preferred_element_type=f32)
            sig = 0.5 * jnp.tanh(0.5 * pre) + 0.5
            hidden = pre * sig
            hidden_ref[rows, columns] = hidden.astype(bf16)
            slope_ref[rows, columns] = (sig + hidden * (1.0 - sig)).astype(bf16)
        for share in range(rows.start // SHARE, rows.stop // SHARE):
            forecast_ref[share] = lax.dot_general(
                turned_weight[:TALL],
                hidden_ref[share * SHARE : (share + 1) * SHARE, :],
                NT,
                preferred_element_type=f32,
            )


def forward(latent, weight, out_weight):
    nodes, width = latent.shape
    latent = pltpu.with_memory_space_constraint(latent, pltpu.HBM)
    weight = pltpu.with_memory_space_constraint(weight, pltpu.HBM)
    out_weight = pltpu.with_memory_space_constraint(out_weight, pltpu.HBM)
    return pl.pallas_call(
        forward_kernel,
        in_specs=[anywhere] * 3,
        out_specs=[vmem] * 6,
        out_shape=[
            jax.ShapeDtypeStruct((nodes // SHARE, TALL, SHARE), f32),
            jax.ShapeDtypeStruct((nodes, width), bf16),
            jax.ShapeDtypeStruct((nodes, width), bf16),
            jax.ShapeDtypeStruct((nodes, width), bf16),
            jax.ShapeDtypeStruct((width, width), bf16),
            jax.ShapeDtypeStruct((width, WIDE), bf16),
        ],
        scratch_shapes=[
            pltpu.VMEM(out_weight.shape, bf16),
            pltpu.SemaphoreType.DMA((len(CHUNKS),)),
            pltpu.SemaphoreType.DMA((width // FCOLS,)),
            pltpu.SemaphoreType.DMA,
        ],
        compiler_params=params(12),
        cost_estimate=cost(2 * nodes * width * (width + WIDE), 20 << 20),
        name="forward",
    )(latent, weight, out_weight)


def slope_function(diff):
    return diff * lax.rsqrt(diff * diff + smooth_sq)


def pair_kernel(place_ref, blocks_ref, observed_ref, area_ref, low_ref, here_ref, weight_ref, sems):
    members = blocks_ref.shape[0]
    variables = observed_ref.shape[0]
    at = pl.multiple_of(place_ref[0] * SHARE, SHARE)
    loads = [
        pltpu.make_async_copy(observed_ref.at[:, pl.ds(at, SHARE)], here_ref, sems.at[0]),
        pltpu.make_async_copy(area_ref.at[:, pl.ds(at, SHARE)], weight_ref, sems.at[1]),
    ]
    for load in loads:
        load.start()
    for load in loads:
        load.wait()
    area = weight_ref[...]
    for start in range(0, TALL, 16):
        rows = slice(start, start + 16)
        real = min(16, variables - start)
        observed = here_ref[start : start + real, :]
        if real < 16:
            observed = jnp.concatenate([observed, jnp.zeros((16 - real, SHARE), f32)], axis=0)
        values = [blocks_ref[a, rows, :] for a in range(members)]
        totals = [0.0] * members
        for a in range(members):
            for b in range(a + 1, members):
                slope = slope_function(values[a] - values[b])
                totals[a] = totals[a] + slope
                totals[b] = totals[b] - slope
        for a in range(members):
            field = area * (slope_function(values[a] - observed) - totals[a] * (1.0 / (members - 1)))
            low_ref[a, rows, :] = field.astype(bf16)


def pairs(place, blocks, observed, area):
    members = blocks.shape[0]
    variables = observed.shape[0]
    return pl.pallas_call(
        pair_kernel,
        in_specs=[smem, vmem, anywhere, anywhere],
        out_specs=vmem,
        out_shape=jax.ShapeDtypeStruct((members, TALL, SHARE), bf16),
        scratch_shapes=[
            pltpu.VMEM((variables, SHARE), f32),
            pltpu.VMEM((1, SHARE), f32),
            pltpu.SemaphoreType.DMA((2,)),
        ],
        compiler_params=params(8),
        cost_estimate=cost(4 << 20, 2 << 20),
        name="pairs",
    )(place, blocks, observed, area)


def turn_kernel(order_ref, latent_ref, turned_ref):
    nodes, width = latent_ref.shape
    half = width // 2
    core = order_ref[8]
    for group in range(8):
        at = order_ref[group] * 64
        first = pl.multiple_of(core * half + at, 64)
        second = pl.multiple_of((1 - core) * half + at, 64)
        for row in range(0, nodes, ROWS):
            columns = slice(row, row + ROWS)
            block = latent_ref[columns, group * 128 : (group + 1) * 128].T
            turned_ref[pl.ds(first, 64), columns] = block[:64]
            turned_ref[pl.ds(second, 64), columns] = block[64:]


def turned(order, latent):
    nodes, width = latent.shape
    return pl.pallas_call(
        turn_kernel,
        in_specs=[smem, vmem],
        out_specs=vmem,
        out_shape=jax.ShapeDtypeStruct((width, nodes), bf16),
        compiler_params=params(8),
        cost_estimate=cost(0, 8 << 20),
        name="turned",
    )(order, latent)


def first_product(turned_ref, slope_ref, padded_ref, turn_ref, pre_ref, send_ref, keep_ref, begin):
    nodes, span = pre_ref.shape
    half = turned_ref.shape[0] // 2
    for column in range(0, span, COLS):
        columns = slice(column, column + COLS)
        source = slice(begin + column, begin + column + COLS)
        for start in range(0, nodes, ROWS):
            rows = slice(start, start + ROWS)
            grad_hidden = lax.dot_general(turn_ref[rows, :], padded_ref[source, :], NT, preferred_element_type=f32)
            pre_ref[rows, columns] = (grad_hidden * slope_ref[rows, source].astype(f32)).astype(bf16)
        for out_ref, base in ((send_ref, 0), (keep_ref, half)):
            part = jnp.dot(turned_ref[base : base + half, :], pre_ref[:, columns], preferred_element_type=f32)
            out_ref[:, columns] = part.astype(bf16)


def backward_a_kernel(low_ref, turned_ref, slope_ref, padded_ref, pre_ref, send_ref, keep_ref, turn_ref, flat_ref):
    for share in range(low_ref.shape[0]):
        columns = slice(share * SHARE, (share + 1) * SHARE)
        low = jnp.concatenate([low_ref[share], jnp.zeros((WIDE - TALL, SHARE), bf16)], axis=0)
        flat_ref[:, columns] = low
        turn_ref[columns, :] = low.T
    first_product(turned_ref, slope_ref, padded_ref, turn_ref, pre_ref, send_ref, keep_ref, 0)


def backward_b_kernel(
    order_ref, turned_ref, slope_ref, hidden_ref, padded_ref, turn_ref, flat_ref, pre_ref, send_ref, keep_ref, second_ref
):
    width = hidden_ref.shape[1]
    span = pre_ref.shape[1]
    first_product(turned_ref, slope_ref, padded_ref, turn_ref, pre_ref, send_ref, keep_ref, width - span)
    for column in range(0, width, COLS):
        columns = slice(column, column + COLS)
        second_ref[columns, :] = jnp.dot(flat_ref[...], hidden_ref[:, columns], preferred_element_type=f32).T.astype(bf16)
    core = order_ref[8]
    for group in range(8):
        at = pl.multiple_of(order_ref[group] * 64, 64)
        mine = pl.multiple_of(group * 128 + 64 * (1 - core), 64)
        other = pl.multiple_of(group * 128 + 64 * core, 64)
        keep_ref[pl.ds(at, 64), span:] = second_ref[pl.ds(mine, 64), :]
        send_ref[pl.ds(at, 64), span:] = second_ref[pl.ds(other, 64), :]


def backward_a(low, turned_latent, slope, padded):
    nodes, width = slope.shape
    half = width // 2
    return pl.pallas_call(
        backward_a_kernel,
        in_specs=[vmem] * 4,
        out_specs=[vmem] * 5,
        out_shape=[
            jax.ShapeDtypeStruct((nodes, half), bf16),
            jax.ShapeDtypeStruct((half, half), bf16),
            jax.ShapeDtypeStruct((half, half), bf16),
            jax.ShapeDtypeStruct((nodes, WIDE), bf16),
            jax.ShapeDtypeStruct((WIDE, nodes), bf16),
        ],
        compiler_params=params(12),
        cost_estimate=cost(nodes * width * (width + WIDE), 8 << 20),
        name="backward_a",
    )(low, turned_latent, slope, padded)


def backward_b(order, turned_latent, slope, hidden, padded, turn, flat):
    nodes, width = slope.shape
    half = width // 2
    return pl.pallas_call(
        backward_b_kernel,
        in_specs=[smem] + [vmem] * 6,
        out_specs=[vmem] * 3,
        out_shape=[
            jax.ShapeDtypeStruct((nodes, half), bf16),
            jax.ShapeDtypeStruct((half, half + WIDE), bf16),
            jax.ShapeDtypeStruct((half, half + WIDE), bf16),
        ],
        scratch_shapes=[pltpu.VMEM((width, WIDE), bf16)],
        compiler_params=params(12),
        cost_estimate=cost(nodes * width * (width + 3 * WIDE), 8 << 20),
        name="backward_b",
    )(order, turned_latent, slope, hidden, padded, turn, flat)


def latent_kernel(left_ref, right_ref, weight_ref, out_ref, result_ref, sems):
    nodes, half = left_ref.shape
    width = weight_ref.shape[1]
    stores = []
    for row in range(0, nodes, ROWS):
        rows = slice(row, row + ROWS)
        for start in range(0, width, COLS):
            columns = slice(start, start + COLS)
            left = lax.dot_general(left_ref[rows, :], weight_ref[columns, :half], NT, preferred_element_type=f32)
            right = lax.dot_general(right_ref[rows, :], weight_ref[columns, half:], NT, preferred_element_type=f32)
            result_ref[rows, columns] = (left + right).astype(bf16)
        store = pltpu.make_async_copy(
            result_ref.at[pl.ds(row, ROWS)], out_ref.at[pl.ds(row, ROWS)], sems.at[row // ROWS]
        )
        store.start()
        stores.append(store)
    for store in stores:
        store.wait()


def latent_gradient(left, right, weight):
    nodes = left.shape[0]
    width = weight.shape[1]
    return pl.pallas_call(
        latent_kernel,
        in_specs=[vmem] * 3,
        out_specs=anywhere,
        out_shape=jax.ShapeDtypeStruct((nodes, width), bf16),
        scratch_shapes=[pltpu.VMEM((nodes, width), bf16), pltpu.SemaphoreType.DMA((nodes // ROWS,))],
        compiler_params=params(12),
        cost_estimate=cost(2 * nodes * width * width, 10 << 20),
        name="latent_gradient",
    )(left, right, weight)


def moved(value, move):
    moves = []
    for member in range(8):
        for grid in range(16):
            y, x_hi, x_lo, z, core = member // 2, member % 2, grid // 8, (grid // 2) % 4, grid % 2
            y, x, z, core = move(y, x_hi * 2 + x_lo, z, core)
            target = (y * 2 + x // 2) * 16 + ((x % 2) * 4 + z) * 2 + core
            moves.append((member * 16 + grid, target))
    return lax.ppermute(value, ("member", "grid"), moves)


def summed(own, others):
    total = own.astype(f32)
    for other in others:
        total = total + other.astype(f32)
    return total


def reduced(send, keep):
    columns = send.shape[1]
    got = moved(send, lambda y, x, z, c: (y, x, z, 1 - c))
    blocks = summed(keep, [got]).astype(bf16).reshape(4, 2, 64, columns)
    got = [moved(blocks[k], lambda y, x, z, c, k=k: (y, x, (z + k) % 4, c)) for k in (1, 3, 2)]
    blocks = summed(blocks[0], got).astype(bf16)
    got = [
        moved(blocks[0] if k == 2 else blocks[1], lambda y, x, z, c, k=k: (y, x ^ k, z, c))
        for k in (1, 3, 2)
    ]
    block = summed(blocks[0], got).astype(bf16)
    got = [moved(block, lambda y, x, z, c, k=k: ((y + k) % 4, x, z, c)) for k in (1, 3, 2)]
    return summed(block, got)


def body(latents, hidden_weight, output_weight, observed, node_area_weight):
    latent = latents[0]
    members = lax.axis_size("member")
    groups = lax.axis_size("grid")
    nodes, width = latent.shape
    variables = output_weight.shape[1]
    member = lax.axis_index("member")
    grid = lax.axis_index("grid")
    x_lo, z, core = grid // 8, (grid // 2) % 4, grid % 2
    order = jnp.stack(
        [((g % 4 - z) % 4) * 2 + jnp.abs(g // 4 - x_lo) for g in range(8)] + [1 - core]
    ).astype(jnp.int32)
    place = member.astype(jnp.int32).reshape(1)

    forecast, hidden, slope, latent_copy, weight_copy, padded = forward(latent, hidden_weight, output_weight.T)
    blocks = lax.all_to_all((0.25 * forecast).astype(f16), "member", 0, 0, tiled=True)
    low = pairs(place, 4.0 * blocks.astype(f32), observed, node_area_weight.reshape(1, nodes))
    low = lax.all_to_all(low, "member", 0, 0, tiled=True)
    turned_latent = turned(order, latent_copy)
    pre_a, send_a, keep_a, turn, flat = backward_a(low, turned_latent, slope, padded)
    pre_b, send_b, keep_b = backward_b(order, turned_latent, slope, hidden, padded, turn, flat)
    total_a = reduced(send_a, keep_a)
    total_b = reduced(send_b, keep_b)
    grad_latent = latent_gradient(pre_a, pre_b, weight_copy)
    factor = 1.0 / math.sqrt(members * nodes * groups)
    half = width // 2
    first = jnp.concatenate([total_a, total_b[:, :half]], axis=1)
    return (grad_latent[None], first * factor, total_b[:, half : half + variables] * factor)


def solution(mesh):
    in_specs = (P("member", "grid", None), P(), P(), P(None, "grid"), P("grid"))
    out_specs = (P("member", "grid", None), P("grid", None), P("grid", None))
    return jax.shard_map(body, mesh=mesh, in_specs=in_specs, out_specs=out_specs, check_vma=False)
```

```python
import functools
import math

import jax
import jax.numpy as jnp
from jax import lax
from jax.experimental import pallas as pl
from jax.experimental.pallas import tpu as pltpu
from jax.sharding import PartitionSpec as P

smooth_sq = 0.0025
bf16 = jnp.bfloat16
f16 = jnp.float16
f32 = jnp.float32

NT = (((1,), (1,)), ((), ()))
WIDE = 128
TALL = 112
SHARE = 256
ROWS = 512
COLS = 256

vmem = pl.BlockSpec(memory_space=pltpu.VMEM)
smem = pl.BlockSpec(memory_space=pltpu.SMEM)
anywhere = pl.BlockSpec(memory_space=pltpu.HBM)


def params(mib):
    return pltpu.CompilerParams(vmem_limit_bytes=mib * 1024 * 1024)


def cost(flops, nbytes, trans=0):
    return pl.CostEstimate(flops=flops, bytes_accessed=nbytes, transcendentals=trans)


CHUNKS = (512, 512, 512, 512)
FCOLS = 512


def forward_kernel(
    latent_ref,
    weight_ref,
    out_weight_ref,
    forecast_ref,
    hidden_out,
    slope_out,
    padded_ref,
    hidden_ref,
    slope_ref,
    latent_copy,
    weight_copy,
    out_weight_copy,
    latent_sems,
    weight_sems,
    out_weight_sem,
    hidden_sems,
    slope_sems,
):
    nodes, width = latent_ref.shape
    variables = out_weight_ref.shape[0]
    out_weight_load = pltpu.make_async_copy(out_weight_ref, out_weight_copy, out_weight_sem)
    spans = []
    for size in CHUNKS:
        begin = spans[-1].stop if spans else 0
        spans.append(slice(begin, begin + size))
    weight_loads = [
        pltpu.make_async_copy(
            weight_ref.at[:, pl.ds(start, FCOLS)], weight_copy.at[:, pl.ds(start, FCOLS)], weight_sems.at[start // FCOLS]
        )
        for start in range(0, width, FCOLS)
    ]

    def chunk(ref, rows):
        return ref.at[pl.ds(rows.start, rows.stop - rows.start)]

    latent_loads = [
        pltpu.make_async_copy(chunk(latent_ref, rows), chunk(latent_copy, rows), latent_sems.at[index])
        for index, rows in enumerate(spans)
    ]
    weight_loads[0].start()
    latent_loads[0].start()
    for load in weight_loads[1:] + latent_loads[1:]:
        load.start()
    out_weight_load.start()
    out_weight_load.wait()
    turned_weight = jnp.concatenate(
        [out_weight_copy[...], jnp.zeros((WIDE - variables, width), bf16)], axis=0
    )
    padded_ref[...] = turned_weight.T
    stores = []
    for index, rows in enumerate(spans):
        latent_loads[index].wait()
        for start in range(0, width, FCOLS):
            columns = slice(start, start + FCOLS)
            if index == 0:
                weight_loads[start // FCOLS].wait()
            pre = jnp.dot(latent_copy[rows, :], weight_copy[:, columns], preferred_element_type=f32)
            sig = 0.5 * jnp.tanh(0.5 * pre) + 0.5
            hidden = pre * sig
            hidden_ref[rows, columns] = hidden.astype(bf16)
            slope_ref[rows, columns] = (sig + hidden * (1.0 - sig)).astype(bf16)
        for made, out, sems in ((hidden_ref, hidden_out, hidden_sems), (slope_ref, slope_out, slope_sems)):
            store = pltpu.make_async_copy(chunk(made, rows), chunk(out, rows), sems.at[index])
            store.start()
            stores.append(store)
        for share in range(rows.start // SHARE, rows.stop // SHARE):
            forecast_ref[share] = lax.dot_general(
                turned_weight[:TALL],
                hidden_ref[share * SHARE : (share + 1) * SHARE, :],
                NT,
                preferred_element_type=f32,
            )
    for store in stores:
        store.wait()


def pinned(value):
    return pltpu.with_memory_space_constraint(value, pltpu.HBM)


def forward(latent, weight, out_weight):
    nodes, width = latent.shape
    return pl.pallas_call(
        forward_kernel,
        in_specs=[anywhere] * 3,
        out_specs=[vmem, anywhere, anywhere, vmem],
        out_shape=[
            jax.ShapeDtypeStruct((nodes // SHARE, TALL, SHARE), f32),
            pltpu.HBM((nodes, width), bf16),
            pltpu.HBM((nodes, width), bf16),
            jax.ShapeDtypeStruct((width, WIDE), bf16),
        ],
        scratch_shapes=[
            pltpu.VMEM((nodes, width), bf16),
            pltpu.VMEM((nodes, width), bf16),
            pltpu.VMEM((nodes, width), bf16),
            pltpu.VMEM((width, width), bf16),
            pltpu.VMEM(out_weight.shape, bf16),
            pltpu.SemaphoreType.DMA((len(CHUNKS),)),
            pltpu.SemaphoreType.DMA((width // FCOLS,)),
            pltpu.SemaphoreType.DMA,
            pltpu.SemaphoreType.DMA((len(CHUNKS),)),
            pltpu.SemaphoreType.DMA((len(CHUNKS),)),
        ],
        compiler_params=params(32),
        cost_estimate=cost(2 * nodes * width * (width + WIDE), 20 << 20),
        name="forward",
    )(pinned(latent), pinned(weight), pinned(out_weight))


def slope_function(diff):
    return diff * lax.rsqrt(diff * diff + smooth_sq)


def pair_kernel(place_ref, blocks_ref, observed_ref, area_ref, low_ref, here_ref, weight_ref, sems):
    members = blocks_ref.shape[0]
    variables = observed_ref.shape[0]
    at = pl.multiple_of(place_ref[0] * SHARE, SHARE)
    loads = [
        pltpu.make_async_copy(observed_ref.at[:, pl.ds(at, SHARE)], here_ref, sems.at[0]),
        pltpu.make_async_copy(area_ref.at[:, pl.ds(at, SHARE)], weight_ref, sems.at[1]),
    ]
    for load in loads:
        load.start()
    for load in loads:
        load.wait()
    area = weight_ref[...]
    for start in range(0, TALL, 16):
        rows = slice(start, start + 16)
        real = min(16, variables - start)
        observed = here_ref[start : start + real, :]
        if real < 16:
            observed = jnp.concatenate([observed, jnp.zeros((16 - real, SHARE), f32)], axis=0)
        values = [blocks_ref[a, rows, :] for a in range(members)]
        totals = [0.0] * members
        for a in range(members):
            for b in range(a + 1, members):
                slope = slope_function(values[a] - values[b])
                totals[a] = totals[a] + slope
                totals[b] = totals[b] - slope
        for a in range(members):
            field = area * (slope_function(values[a] - observed) - totals[a] * (1.0 / (members - 1)))
            low_ref[a, rows, :] = field.astype(bf16)


def pairs(place, blocks, observed, area):
    members = blocks.shape[0]
    variables = observed.shape[0]
    return pl.pallas_call(
        pair_kernel,
        in_specs=[smem, vmem, anywhere, anywhere],
        out_specs=vmem,
        out_shape=jax.ShapeDtypeStruct((members, TALL, SHARE), bf16),
        scratch_shapes=[
            pltpu.VMEM((variables, SHARE), f32),
            pltpu.VMEM((1, SHARE), f32),
            pltpu.SemaphoreType.DMA((2,)),
        ],
        compiler_params=params(8),
        cost_estimate=cost(4 << 20, 2 << 20),
        name="pairs",
    )(place, blocks, observed, area)


def position(grid_ref):
    grid = grid_ref[0]
    return grid >> 3, (grid >> 1) & 3, grid & 1


def slot(group, x_lo, z):
    return (((group - z) & 3) * 2 + ((group >> 2) ^ x_lo)) * 64


def turn_kernel(grid_ref, latent_ref, turned_ref):
    nodes, width = latent_ref.shape
    half = width // 2
    x_lo, z, core = position(grid_ref)
    for group in range(8):
        at = slot(group, x_lo, z)
        first = pl.multiple_of((1 - core) * half + at, 64)
        second = pl.multiple_of(core * half + at, 64)
        for row in range(0, nodes, ROWS):
            columns = slice(row, row + ROWS)
            block = latent_ref[columns, group * 128 : (group + 1) * 128].T
            turned_ref[pl.ds(first, 64), columns] = block[:64]
            turned_ref[pl.ds(second, 64), columns] = block[64:]


def turned(grid, latent):
    nodes, width = latent.shape
    return pl.pallas_call(
        turn_kernel,
        in_specs=[smem, vmem],
        out_specs=vmem,
        out_shape=jax.ShapeDtypeStruct((width, nodes), bf16),
        compiler_params=params(8),
        cost_estimate=cost(0, 8 << 20),
        name="turned",
    )(grid, latent)


def first_product(turned_ref, slope_ref, padded_ref, turn_ref, pre_ref, send_ref, keep_ref, begin, ready):
    nodes, span = pre_ref.shape
    half = turned_ref.shape[0] // 2
    for column in range(0, span, COLS):
        columns = slice(column, column + COLS)
        source = slice(begin + column, begin + column + COLS)
        for start in range(0, nodes, ROWS):
            rows = slice(start, start + ROWS)
            grad_hidden = lax.dot_general(turn_ref[rows, :], padded_ref[source, :], NT, preferred_element_type=f32)
            pre_ref[rows, columns] = (grad_hidden * slope_ref[rows, columns].astype(f32)).astype(bf16)
    ready()
    for column in range(0, span, COLS):
        columns = slice(column, column + COLS)
        for out_ref, base in ((send_ref, 0), (keep_ref, half)):
            part = jnp.dot(turned_ref[base : base + half, :], pre_ref[:, columns], preferred_element_type=f32)
            out_ref[:, columns] = part.astype(bf16)


def backward_a_kernel(
    low_ref,
    turned_hbm,
    slope_hbm,
    padded_ref,
    pre_ref,
    send_ref,
    keep_ref,
    turn_ref,
    flat_ref,
    turned_ref,
    slope_ref,
    turned_sem,
    slope_sem,
):
    span = pre_ref.shape[1]
    slope_load = pltpu.make_async_copy(slope_hbm.at[:, pl.ds(0, span)], slope_ref, slope_sem)
    turned_load = pltpu.make_async_copy(turned_hbm, turned_ref, turned_sem)
    slope_load.start()
    turned_load.start()
    for share in range(low_ref.shape[0]):
        columns = slice(share * SHARE, (share + 1) * SHARE)
        low = jnp.concatenate([low_ref[share], jnp.zeros((WIDE - TALL, SHARE), bf16)], axis=0)
        flat_ref[:, columns] = low
        turn_ref[columns, :] = low.T
    slope_load.wait()
    first_product(
        turned_ref, slope_ref, padded_ref, turn_ref, pre_ref, send_ref, keep_ref, 0, turned_load.wait
    )


def backward_b_kernel(
    grid_ref,
    turned_ref,
    slope_hbm,
    hidden_hbm,
    padded_ref,
    turn_ref,
    flat_ref,
    pre_ref,
    send_ref,
    keep_ref,
    second_ref,
    slope_ref,
    hidden_ref,
    slope_sem,
    hidden_sem,
):
    width = hidden_ref.shape[1]
    span = pre_ref.shape[1]
    slope_load = pltpu.make_async_copy(slope_hbm.at[:, pl.ds(width - span, span)], slope_ref, slope_sem)
    hidden_load = pltpu.make_async_copy(hidden_hbm, hidden_ref, hidden_sem)
    slope_load.start()
    hidden_load.start()
    slope_load.wait()
    first_product(
        turned_ref, slope_ref, padded_ref, turn_ref, pre_ref, send_ref, keep_ref, width - span, lambda: None
    )
    hidden_load.wait()
    for column in range(0, width, COLS):
        columns = slice(column, column + COLS)
        second_ref[columns, :] = jnp.dot(flat_ref[...], hidden_ref[:, columns], preferred_element_type=f32).T.astype(bf16)
    x_lo, z, core = position(grid_ref)
    for group in range(8):
        at = pl.multiple_of(slot(group, x_lo, z), 64)
        mine = pl.multiple_of(group * 128 + 64 * core, 64)
        other = pl.multiple_of(group * 128 + 64 * (1 - core), 64)
        keep_ref[pl.ds(at, 64), span:] = second_ref[pl.ds(mine, 64), :]
        send_ref[pl.ds(at, 64), span:] = second_ref[pl.ds(other, 64), :]


def backward_a(low, turned_latent, slope, padded):
    nodes, width = slope.shape
    half = width // 2
    return pl.pallas_call(
        backward_a_kernel,
        in_specs=[vmem, anywhere, anywhere, vmem],
        out_specs=[vmem] * 6,
        out_shape=[
            jax.ShapeDtypeStruct((nodes, half), bf16),
            jax.ShapeDtypeStruct((half, half), bf16),
            jax.ShapeDtypeStruct((half, half), bf16),
            jax.ShapeDtypeStruct((nodes, WIDE), bf16),
            jax.ShapeDtypeStruct((WIDE, nodes), bf16),
            jax.ShapeDtypeStruct((width, nodes), bf16),
        ],
        scratch_shapes=[
            pltpu.VMEM((nodes, half), bf16),
            pltpu.SemaphoreType.DMA,
            pltpu.SemaphoreType.DMA,
        ],
        compiler_params=params(16),
        cost_estimate=cost(nodes * width * (width + WIDE), 8 << 20),
        name="backward_a",
    )(low, pinned(turned_latent), pinned(slope), padded)


def backward_b(grid, turned_latent, slope, hidden, padded, turn, flat):
    nodes, width = slope.shape
    half = width // 2
    return pl.pallas_call(
        backward_b_kernel,
        in_specs=[smem, vmem, anywhere, anywhere] + [vmem] * 3,
        out_specs=[vmem] * 3,
        out_shape=[
            jax.ShapeDtypeStruct((nodes, half), bf16),
            jax.ShapeDtypeStruct((half, half + WIDE), bf16),
            jax.ShapeDtypeStruct((half, half + WIDE), bf16),
        ],
        scratch_shapes=[
            pltpu.VMEM((width, WIDE), bf16),
            pltpu.VMEM((nodes, half), bf16),
            pltpu.VMEM((nodes, width), bf16),
            pltpu.SemaphoreType.DMA,
            pltpu.SemaphoreType.DMA,
        ],
        compiler_params=params(16),
        cost_estimate=cost(nodes * width * (width + 3 * WIDE), 8 << 20),
        name="backward_b",
    )(grid, turned_latent, pinned(slope), pinned(hidden), padded, turn, flat)


def latent_kernel(left_ref, right_ref, weight_hbm, *refs, begin):
    out_ref, weight_ref, result_ref, weight_sem, sems = refs[-5:]
    nodes, half = left_ref.shape
    width = weight_ref.shape[1]
    load = pltpu.make_async_copy(weight_hbm, weight_ref, weight_sem)
    load.start()
    load.wait()
    stores = []
    for row in range(0, nodes // 2, ROWS):
        rows = slice(begin + row, begin + row + ROWS)
        for start in range(0, width, COLS):
            columns = slice(start, start + COLS)
            left = lax.dot_general(left_ref[rows, :], weight_ref[columns, :half], NT, preferred_element_type=f32)
            right = lax.dot_general(right_ref[rows, :], weight_ref[columns, half:], NT, preferred_element_type=f32)
            result_ref[row : row + ROWS, columns] = (left + right).astype(bf16)
        store = pltpu.make_async_copy(
            result_ref.at[pl.ds(row, ROWS)], out_ref.at[pl.ds(begin + row, ROWS)], sems.at[row // ROWS]
        )
        store.start()
        stores.append(store)
    for store in stores:
        store.wait()


def latent_gradient(left, right, weight, begin, so_far=None):
    nodes = left.shape[0]
    width = weight.shape[1]
    more = [] if so_far is None else [so_far]
    return pl.pallas_call(
        functools.partial(latent_kernel, begin=begin),
        in_specs=[vmem, vmem, anywhere] + [anywhere] * len(more),
        out_specs=anywhere,
        out_shape=pltpu.HBM((nodes, width), bf16),
        input_output_aliases={3: 0} if more else {},
        scratch_shapes=[
            pltpu.VMEM((width, width), bf16),
            pltpu.VMEM((nodes // 2, width), bf16),
            pltpu.SemaphoreType.DMA,
            pltpu.SemaphoreType.DMA((nodes // 2 // ROWS,)),
        ],
        compiler_params=params(12),
        cost_estimate=cost(nodes * width * width, 5 << 20),
        name="latent_gradient",
    )(left, right, pinned(weight), *more)


def moved(value, move):
    moves = []
    for member in range(8):
        for grid in range(16):
            y, x_hi, x_lo, z, core = member // 2, member % 2, grid // 8, (grid // 2) % 4, grid % 2
            y, x, z, core = move(y, x_hi * 2 + x_lo, z, core)
            target = (y * 2 + x // 2) * 16 + ((x % 2) * 4 + z) * 2 + core
            moves.append((member * 16 + grid, target))
    return lax.ppermute(value, ("member", "grid"), moves)


def summed(own, others):
    total = own.astype(f32)
    for other in others:
        total = total + other.astype(f32)
    return total


def over_core(send, keep):
    got = moved(send, lambda y, x, z, c: (y, x, z, 1 - c))
    return summed(keep, [got]).astype(bf16)


def over_chips(rows):
    blocks = rows.reshape(4, 2, 64, rows.shape[1])
    got = [moved(blocks[k], lambda y, x, z, c, k=k: (y, x, (z + k) % 4, c)) for k in (1, 3, 2)]
    blocks = summed(blocks[0], got).astype(bf16)
    got = [
        moved(blocks[0] if k == 2 else blocks[1], lambda y, x, z, c, k=k: (y, x ^ k, z, c))
        for k in (1, 3, 2)
    ]
    block = summed(blocks[0], got).astype(bf16)
    got = [moved(block, lambda y, x, z, c, k=k: ((y + k) % 4, x, z, c)) for k in (1, 3, 2)]
    return summed(block, got)


def body(latents, hidden_weight, output_weight, observed, node_area_weight):
    latent = latents[0]
    members = lax.axis_size("member")
    groups = lax.axis_size("grid")
    nodes, width = latent.shape
    variables = output_weight.shape[1]
    place = lax.axis_index("member").astype(jnp.int32).reshape(1)
    grid = lax.axis_index("grid").astype(jnp.int32).reshape(1)

    forecast, hidden, slope, padded = forward(latent, hidden_weight, output_weight.T)
    blocks, late_grid = lax.optimization_barrier(((0.25 * forecast).astype(f16), grid))
    blocks = lax.all_to_all(blocks, "member", 0, 0, tiled=True)
    turned_latent = turned(late_grid, latent)
    low = pairs(place, 4.0 * blocks.astype(f32), observed, node_area_weight.reshape(1, nodes))
    low = lax.all_to_all(low, "member", 0, 0, tiled=True)
    pre_a, send_a, keep_a, turn, flat, turned_latent = backward_a(low, turned_latent, slope, padded)
    pre_b, send_b, keep_b = backward_b(grid, turned_latent, slope, hidden, padded, turn, flat)
    rows_a, pre_a = lax.optimization_barrier((over_core(send_a, keep_a), pre_a))
    grad_latent = latent_gradient(pre_a, pre_b, hidden_weight, 0)
    rows_b, pre_b = lax.optimization_barrier((over_core(send_b, keep_b), pre_b))
    grad_latent = latent_gradient(pre_a, pre_b, hidden_weight, nodes // 2, grad_latent)
    total_a = over_chips(rows_a)
    total_b = over_chips(rows_b)
    factor = 1.0 / math.sqrt(members * nodes * groups)
    half = width // 2
    first = jnp.concatenate([total_a, total_b[:, :half]], axis=1)
    return (grad_latent[None], first * factor, total_b[:, half : half + variables] * factor)


def solution(mesh):
    in_specs = (P("member", "grid", None), P(), P(), P(None, "grid"), P("grid"))
    out_specs = (P("member", "grid", None), P("grid", None), P("grid", None))
    return jax.shard_map(body, mesh=mesh, in_specs=in_specs, out_specs=out_specs, check_vma=False)
```

```python
import functools
import math

import jax
import jax.numpy as jnp
from jax import lax
from jax.experimental import pallas as pl
from jax.experimental.pallas import tpu as pltpu
from jax.sharding import PartitionSpec as P

smooth_sq = 0.0025
bf16 = jnp.bfloat16
f16 = jnp.float16
f32 = jnp.float32

NT = (((1,), (1,)), ((), ()))
WIDE = 128
TALL = 112
SHARE = 256
ROWS = 512
COLS = 256

vmem = pl.BlockSpec(memory_space=pltpu.VMEM)
smem = pl.BlockSpec(memory_space=pltpu.SMEM)
anywhere = pl.BlockSpec(memory_space=pltpu.HBM)


def params(mib):
    return pltpu.CompilerParams(vmem_limit_bytes=mib * 1024 * 1024)


def cost(flops, nbytes, trans=0):
    return pl.CostEstimate(flops=flops, bytes_accessed=nbytes, transcendentals=trans)


CHUNKS = (512, 512, 512, 256, 256)
FCOLS = 512


def forward_kernel(
    latent_ref,
    weight_ref,
    out_weight_ref,
    forecast_ref,
    hidden_out,
    slope_out,
    padded_ref,
    hidden_ref,
    slope_ref,
    latent_copy,
    weight_copy,
    out_weight_copy,
    latent_sems,
    weight_sems,
    out_weight_sem,
    hidden_sems,
    slope_sems,
):
    nodes, width = latent_ref.shape
    variables = out_weight_ref.shape[0]
    out_weight_load = pltpu.make_async_copy(out_weight_ref, out_weight_copy, out_weight_sem)
    spans = []
    for size in CHUNKS:
        begin = spans[-1].stop if spans else 0
        spans.append(slice(begin, begin + size))
    weight_loads = [
        pltpu.make_async_copy(
            weight_ref.at[:, pl.ds(start, FCOLS)], weight_copy.at[:, pl.ds(start, FCOLS)], weight_sems.at[start // FCOLS]
        )
        for start in range(0, width, FCOLS)
    ]

    def chunk(ref, rows):
        return ref.at[pl.ds(rows.start, rows.stop - rows.start)]

    latent_loads = [
        pltpu.make_async_copy(chunk(latent_ref, rows), chunk(latent_copy, rows), latent_sems.at[index])
        for index, rows in enumerate(spans)
    ]
    weight_loads[0].start()
    latent_loads[0].start()
    for load in weight_loads[1:] + latent_loads[1:]:
        load.start()
    out_weight_load.start()
    out_weight_load.wait()
    turned_weight = jnp.concatenate(
        [out_weight_copy[...], jnp.zeros((WIDE - variables, width), bf16)], axis=0
    )
    padded_ref[...] = turned_weight.T
    stores = []
    for index, rows in enumerate(spans):
        latent_loads[index].wait()
        for start in range(0, width, FCOLS):
            columns = slice(start, start + FCOLS)
            if index == 0:
                weight_loads[start // FCOLS].wait()
            pre = jnp.dot(latent_copy[rows, :], weight_copy[:, columns], preferred_element_type=f32)
            sig = 0.5 * jnp.tanh(0.5 * pre) + 0.5
            hidden = pre * sig
            hidden_ref[rows, columns] = hidden.astype(bf16)
            slope_ref[rows, columns] = (sig + hidden * (1.0 - sig)).astype(bf16)
        for made, out, sems in ((hidden_ref, hidden_out, hidden_sems), (slope_ref, slope_out, slope_sems)):
            store = pltpu.make_async_copy(chunk(made, rows), chunk(out, rows), sems.at[index])
            store.start()
            stores.append(store)
        for share in range(rows.start // SHARE, rows.stop // SHARE):
            forecast_ref[share] = lax.dot_general(
                turned_weight[:TALL],
                hidden_ref[share * SHARE : (share + 1) * SHARE, :],
                NT,
                preferred_element_type=f32,
            )
    for store in stores:
        store.wait()


def pinned(value):
    return pltpu.with_memory_space_constraint(value, pltpu.HBM)


def forward(latent, weight, out_weight):
    nodes, width = latent.shape
    return pl.pallas_call(
        forward_kernel,
        in_specs=[anywhere] * 3,
        out_specs=[vmem, anywhere, anywhere, vmem],
        out_shape=[
            jax.ShapeDtypeStruct((nodes // SHARE, TALL, SHARE), f32),
            pltpu.HBM((nodes, width), bf16),
            pltpu.HBM((nodes, width), bf16),
            jax.ShapeDtypeStruct((width, WIDE), bf16),
        ],
        scratch_shapes=[
            pltpu.VMEM((nodes, width), bf16),
            pltpu.VMEM((nodes, width), bf16),
            pltpu.VMEM((nodes, width), bf16),
            pltpu.VMEM((width, width), bf16),
            pltpu.VMEM(out_weight.shape, bf16),
            pltpu.SemaphoreType.DMA((len(CHUNKS),)),
            pltpu.SemaphoreType.DMA((width // FCOLS,)),
            pltpu.SemaphoreType.DMA,
            pltpu.SemaphoreType.DMA((len(CHUNKS),)),
            pltpu.SemaphoreType.DMA((len(CHUNKS),)),
        ],
        compiler_params=params(32),
        cost_estimate=cost(2 * nodes * width * (width + WIDE), 20 << 20),
        name="forward",
    )(pinned(latent), pinned(weight), pinned(out_weight))


def slope_function(diff):
    return diff * lax.rsqrt(diff * diff + smooth_sq)


def pair_kernel(place_ref, blocks_ref, observed_ref, area_ref, low_ref, here_ref, weight_ref, sems):
    members = blocks_ref.shape[0]
    variables = observed_ref.shape[0]
    at = pl.multiple_of(place_ref[0] * SHARE, SHARE)
    loads = [
        pltpu.make_async_copy(observed_ref.at[:, pl.ds(at, SHARE)], here_ref, sems.at[0]),
        pltpu.make_async_copy(area_ref.at[:, pl.ds(at, SHARE)], weight_ref, sems.at[1]),
    ]
    for load in loads:
        load.start()
    for load in loads:
        load.wait()
    area = weight_ref[...]
    for start in range(0, TALL, 16):
        rows = slice(start, start + 16)
        real = min(16, variables - start)
        observed = here_ref[start : start + real, :]
        if real < 16:
            observed = jnp.concatenate([observed, jnp.zeros((16 - real, SHARE), f32)], axis=0)
        values = [blocks_ref[a, rows, :] for a in range(members)]
        totals = [0.0] * members
        for a in range(members):
            for b in range(a + 1, members):
                slope = slope_function(values[a] - values[b])
                totals[a] = totals[a] + slope
                totals[b] = totals[b] - slope
        for a in range(members):
            field = area * (slope_function(values[a] - observed) - totals[a] * (1.0 / (members - 1)))
            low_ref[a, rows, :] = field.astype(bf16)


def pairs(place, blocks, observed, area):
    members = blocks.shape[0]
    variables = observed.shape[0]
    return pl.pallas_call(
        pair_kernel,
        in_specs=[smem, vmem, anywhere, anywhere],
        out_specs=vmem,
        out_shape=jax.ShapeDtypeStruct((members, TALL, SHARE), bf16),
        scratch_shapes=[
            pltpu.VMEM((variables, SHARE), f32),
            pltpu.VMEM((1, SHARE), f32),
            pltpu.SemaphoreType.DMA((2,)),
        ],
        compiler_params=params(8),
        cost_estimate=cost(4 << 20, 2 << 20),
        name="pairs",
    )(place, blocks, observed, area)


def position(grid_ref):
    grid = grid_ref[0]
    return grid >> 3, (grid >> 1) & 3, grid & 1


def slot(group, x_lo, z):
    return (((group - z) & 3) * 2 + ((group >> 2) ^ x_lo)) * 64


def turn_kernel(grid_ref, latent_ref, turned_ref):
    nodes, width = latent_ref.shape
    half = width // 2
    x_lo, z, core = position(grid_ref)
    for group in range(8):
        at = slot(group, x_lo, z)
        first = pl.multiple_of((1 - core) * half + at, 64)
        second = pl.multiple_of(core * half + at, 64)
        for row in range(0, nodes, ROWS):
            columns = slice(row, row + ROWS)
            block = latent_ref[columns, group * 128 : (group + 1) * 128].T
            turned_ref[pl.ds(first, 64), columns] = block[:64]
            turned_ref[pl.ds(second, 64), columns] = block[64:]


def turned(grid, latent):
    nodes, width = latent.shape
    return pl.pallas_call(
        turn_kernel,
        in_specs=[smem, vmem],
        out_specs=vmem,
        out_shape=jax.ShapeDtypeStruct((width, nodes), bf16),
        compiler_params=params(8),
        cost_estimate=cost(0, 8 << 20),
        name="turned",
    )(grid, latent)


def gradient_of_pre(slope_ref, padded_ref, turn_ref, pre_ref, columns, begin):
    for start in range(0, pre_ref.shape[0], ROWS):
        rows = slice(start, start + ROWS)
        grad_hidden = lax.dot_general(turn_ref[rows, :], padded_ref[columns, :], NT, preferred_element_type=f32)
        grad_pre = (grad_hidden * slope_ref[rows, columns].astype(f32)).astype(bf16)
        pre_ref[rows, columns.start - begin : columns.stop - begin] = grad_pre


def first_product(turned_ref, pre_ref, send_ref, keep_ref, rows):
    span = pre_ref.shape[1]
    half = turned_ref.shape[0] // 2
    out_ref = send_ref if rows.start < half else keep_ref
    at = rows.start % half
    part = jnp.dot(turned_ref[rows, :], pre_ref[...], preferred_element_type=f32)
    out_ref[at : at + rows.stop - rows.start, :span] = part.astype(bf16)


def backward_a_kernel(
    low_ref,
    turned_hbm,
    slope_hbm,
    padded_ref,
    pre_ref,
    send_ref,
    keep_ref,
    turn_ref,
    flat_ref,
    turned_ref,
    slope_ref,
    turned_sems,
    slope_sems,
):
    span = pre_ref.shape[1]
    width = slope_ref.shape[1]
    column_parts = [slice(start, start + COLS) for start in range(0, width, COLS)]
    row_parts = [slice(start, start + 256) for start in range(0, width, 256)]
    slope_loads = [
        pltpu.make_async_copy(
            slope_hbm.at[:, pl.ds(part.start, COLS)], slope_ref.at[:, pl.ds(part.start, COLS)], slope_sems.at[index]
        )
        for index, part in enumerate(column_parts)
    ]
    turned_loads = [
        pltpu.make_async_copy(
            turned_hbm.at[pl.ds(part.start, 256)], turned_ref.at[pl.ds(part.start, 256)], turned_sems.at[index]
        )
        for index, part in enumerate(row_parts)
    ]
    now = span // COLS
    for load in slope_loads[:now] + turned_loads + slope_loads[now:]:
        load.start()
    for share in range(low_ref.shape[0]):
        columns = slice(share * SHARE, (share + 1) * SHARE)
        low = jnp.concatenate([low_ref[share], jnp.zeros((WIDE - TALL, SHARE), bf16)], axis=0)
        flat_ref[:, columns] = low
        turn_ref[columns, :] = low.T
    for load, columns in zip(slope_loads[:now], column_parts):
        load.wait()
        gradient_of_pre(slope_ref, padded_ref, turn_ref, pre_ref, columns, 0)
    for load, rows in zip(turned_loads, row_parts):
        load.wait()
        first_product(turned_ref, pre_ref, send_ref, keep_ref, rows)
    for load in slope_loads[now:]:
        load.wait()


def backward_b_kernel(
    grid_ref,
    turned_ref,
    slope_ref,
    hidden_hbm,
    weight_hbm,
    padded_ref,
    turn_ref,
    flat_ref,
    pre_ref,
    send_ref,
    keep_ref,
    weight_ref,
    second_ref,
    hidden_ref,
    hidden_sem,
    weight_sem,
):
    width = hidden_ref.shape[1]
    span = pre_ref.shape[1]
    hidden_load = pltpu.make_async_copy(hidden_hbm, hidden_ref, hidden_sem)
    weight_load = pltpu.make_async_copy(weight_hbm, weight_ref, weight_sem)
    hidden_load.start()
    weight_load.start()
    for start in range(width - span, width, COLS):
        gradient_of_pre(slope_ref, padded_ref, turn_ref, pre_ref, slice(start, start + COLS), width - span)
    for start in range(0, width, 512):
        first_product(turned_ref, pre_ref, send_ref, keep_ref, slice(start, start + 512))
    hidden_load.wait()
    for column in range(0, width, COLS):
        columns = slice(column, column + COLS)
        second_ref[columns, :] = jnp.dot(flat_ref[...], hidden_ref[:, columns], preferred_element_type=f32).T.astype(bf16)
    x_lo, z, core = position(grid_ref)
    for group in range(8):
        at = pl.multiple_of(slot(group, x_lo, z), 64)
        mine = pl.multiple_of(group * 128 + 64 * core, 64)
        other = pl.multiple_of(group * 128 + 64 * (1 - core), 64)
        keep_ref[pl.ds(at, 64), span:] = second_ref[pl.ds(mine, 64), :]
        send_ref[pl.ds(at, 64), span:] = second_ref[pl.ds(other, 64), :]
    weight_load.wait()


def backward_a(low, turned_latent, slope, padded):
    nodes, width = slope.shape
    half = width // 2
    return pl.pallas_call(
        backward_a_kernel,
        in_specs=[vmem, anywhere, anywhere, vmem],
        out_specs=[vmem] * 7,
        out_shape=[
            jax.ShapeDtypeStruct((nodes, half), bf16),
            jax.ShapeDtypeStruct((half, half), bf16),
            jax.ShapeDtypeStruct((half, half), bf16),
            jax.ShapeDtypeStruct((nodes, WIDE), bf16),
            jax.ShapeDtypeStruct((WIDE, nodes), bf16),
            jax.ShapeDtypeStruct((width, nodes), bf16),
            jax.ShapeDtypeStruct((nodes, width), bf16),
        ],
        scratch_shapes=[
            pltpu.SemaphoreType.DMA((width // 256,)),
            pltpu.SemaphoreType.DMA((width // COLS,)),
        ],
        compiler_params=params(16),
        cost_estimate=cost(nodes * width * (width + WIDE), 8 << 20),
        name="backward_a",
    )(low, pinned(turned_latent), pinned(slope), padded)


def backward_b(grid, turned_latent, slope, hidden, weight, padded, turn, flat):
    nodes, width = slope.shape
    half = width // 2
    return pl.pallas_call(
        backward_b_kernel,
        in_specs=[smem, vmem, vmem, anywhere, anywhere] + [vmem] * 3,
        out_specs=[vmem] * 4,
        out_shape=[
            jax.ShapeDtypeStruct((nodes, half), bf16),
            jax.ShapeDtypeStruct((half, half + WIDE), bf16),
            jax.ShapeDtypeStruct((half, half + WIDE), bf16),
            jax.ShapeDtypeStruct((width, width), bf16),
        ],
        scratch_shapes=[
            pltpu.VMEM((width, WIDE), bf16),
            pltpu.VMEM((nodes, width), bf16),
            pltpu.SemaphoreType.DMA,
            pltpu.SemaphoreType.DMA,
        ],
        compiler_params=params(16),
        cost_estimate=cost(nodes * width * (width + 3 * WIDE), 8 << 20),
        name="backward_b",
    )(grid, turned_latent, slope, pinned(hidden), pinned(weight), padded, turn, flat)


def latent_kernel(left_ref, right_ref, weight_ref, out_ref, result_ref, sems):
    nodes, half = left_ref.shape
    width = weight_ref.shape[1]
    stores = []
    for row in range(0, nodes, ROWS):
        rows = slice(row, row + ROWS)
        for start in range(0, width, COLS):
            columns = slice(start, start + COLS)
            left = lax.dot_general(left_ref[rows, :], weight_ref[columns, :half], NT, preferred_element_type=f32)
            right = lax.dot_general(right_ref[rows, :], weight_ref[columns, half:], NT, preferred_element_type=f32)
            result_ref[rows, columns] = (left + right).astype(bf16)
        store = pltpu.make_async_copy(
            result_ref.at[pl.ds(row, ROWS)], out_ref.at[pl.ds(row, ROWS)], sems.at[row // ROWS]
        )
        store.start()
        stores.append(store)
    for store in stores:
        store.wait()


def latent_gradient(left, right, weight):
    nodes = left.shape[0]
    width = weight.shape[1]
    return pl.pallas_call(
        latent_kernel,
        in_specs=[vmem] * 3,
        out_specs=anywhere,
        out_shape=pltpu.HBM((nodes, width), bf16),
        scratch_shapes=[pltpu.VMEM((nodes, width), bf16), pltpu.SemaphoreType.DMA((nodes // ROWS,))],
        compiler_params=params(12),
        cost_estimate=cost(2 * nodes * width * width, 10 << 20),
        name="latent_gradient",
    )(left, right, weight)


def moved(value, move):
    moves = []
    for member in range(8):
        for grid in range(16):
            y, x_hi, x_lo, z, core = member // 2, member % 2, grid // 8, (grid // 2) % 4, grid % 2
            y, x, z, core = move(y, x_hi * 2 + x_lo, z, core)
            target = (y * 2 + x // 2) * 16 + ((x % 2) * 4 + z) * 2 + core
            moves.append((member * 16 + grid, target))
    return lax.ppermute(value, ("member", "grid"), moves)


def summed(own, others):
    total = own.astype(f32)
    for other in others:
        total = total + other.astype(f32)
    return total


def over_core(send, keep):
    got = moved(send, lambda y, x, z, c: (y, x, z, 1 - c))
    return summed(keep, [got]).astype(bf16)


def over_z(rows):
    blocks = rows.reshape(4, 2, 64, rows.shape[1])
    got = [moved(blocks[k], lambda y, x, z, c, k=k: (y, x, (z + k) % 4, c)) for k in (1, 3, 2)]
    return summed(blocks[0], got).astype(bf16)


def over_x_and_y(blocks):
    got = [
        moved(blocks[0] if k == 2 else blocks[1], lambda y, x, z, c, k=k: (y, x ^ k, z, c))
        for k in (1, 3, 2)
    ]
    block = summed(blocks[0], got).astype(bf16)
    got = [moved(block, lambda y, x, z, c, k=k: (y ^ k, x, z, c)) for k in (1, 3, 2)]
    return summed(block, got)


def body(latents, hidden_weight, output_weight, observed, node_area_weight):
    latent = latents[0]
    members = lax.axis_size("member")
    groups = lax.axis_size("grid")
    nodes, width = latent.shape
    variables = output_weight.shape[1]
    place = lax.axis_index("member").astype(jnp.int32).reshape(1)
    grid = lax.axis_index("grid").astype(jnp.int32).reshape(1)

    forecast, hidden, slope, padded = forward(latent, hidden_weight, output_weight.T)
    blocks, late_grid = lax.optimization_barrier(((0.25 * forecast).astype(f16), grid))
    blocks = lax.all_to_all(blocks, "member", 0, 0, tiled=True)
    turned_latent = turned(late_grid, latent)
    low = pairs(place, 4.0 * blocks.astype(f32), observed, node_area_weight.reshape(1, nodes))
    low = lax.all_to_all(low, "member", 0, 0, tiled=True)
    pre_a, send_a, keep_a, turn, flat, turned_latent, slope = backward_a(low, turned_latent, slope, padded)
    pre_b, send_b, keep_b, weight_copy = backward_b(
        grid, turned_latent, slope, hidden, hidden_weight, padded, turn, flat
    )
    rows_a = over_core(send_a, keep_a)
    rows_b, pre_b = lax.optimization_barrier((over_core(send_b, keep_b), pre_b))
    grad_latent = latent_gradient(pre_a, pre_b, weight_copy)
    blocks = jnp.concatenate([over_z(rows_a), over_z(rows_b)], axis=2)
    blocks, grad_latent = lax.optimization_barrier((blocks, grad_latent))
    total = over_x_and_y(blocks)
    factor = 1.0 / math.sqrt(members * nodes * groups)
    return (grad_latent[None], total[:, :width] * factor, total[:, width : width + variables] * factor)


def solution(mesh):
    in_specs = (P("member", "grid", None), P(), P(), P(None, "grid"), P("grid"))
    out_specs = (P("member", "grid", None), P("grid", None), P("grid", None))
    return jax.shard_map(body, mesh=mesh, in_specs=in_specs, out_specs=out_specs, check_vma=False)
```

```python
import functools
import math

import jax
import jax.numpy as jnp
from jax import lax
from jax.experimental import pallas as pl
from jax.experimental.pallas import tpu as pltpu
from jax.sharding import PartitionSpec as P

smooth_sq = 0.0025
bf16 = jnp.bfloat16
f16 = jnp.float16
f32 = jnp.float32

NT = (((1,), (1,)), ((), ()))
WIDE = 128
TALL = 112
SHARE = 256
ROWS = 512
COLS = 256

vmem = pl.BlockSpec(memory_space=pltpu.VMEM)
smem = pl.BlockSpec(memory_space=pltpu.SMEM)
anywhere = pl.BlockSpec(memory_space=pltpu.HBM)


def params(mib):
    return pltpu.CompilerParams(vmem_limit_bytes=mib * 1024 * 1024)


def cost(flops, nbytes, trans=0):
    return pl.CostEstimate(flops=flops, bytes_accessed=nbytes, transcendentals=trans)


CHUNKS = (512, 512, 512, 256, 256)
FCOLS = 512


def forward_kernel(
    latent_ref,
    weight_ref,
    out_weight_ref,
    forecast_ref,
    hidden_out,
    slope_out,
    padded_ref,
    hidden_ref,
    slope_ref,
    latent_copy,
    weight_copy,
    out_weight_copy,
    latent_sems,
    weight_sems,
    out_weight_sem,
    hidden_sems,
    slope_sems,
):
    nodes, width = latent_ref.shape
    variables = out_weight_ref.shape[0]
    out_weight_load = pltpu.make_async_copy(out_weight_ref, out_weight_copy, out_weight_sem)
    spans = []
    for size in CHUNKS:
        begin = spans[-1].stop if spans else 0
        spans.append(slice(begin, begin + size))
    weight_loads = [
        pltpu.make_async_copy(
            weight_ref.at[:, pl.ds(start, FCOLS)], weight_copy.at[:, pl.ds(start, FCOLS)], weight_sems.at[start // FCOLS]
        )
        for start in range(0, width, FCOLS)
    ]

    def chunk(ref, rows):
        return ref.at[pl.ds(rows.start, rows.stop - rows.start)]

    latent_loads = [
        pltpu.make_async_copy(chunk(latent_ref, rows), chunk(latent_copy, rows), latent_sems.at[index])
        for index, rows in enumerate(spans)
    ]
    weight_loads[0].start()
    latent_loads[0].start()
    for load in weight_loads[1:] + latent_loads[1:]:
        load.start()
    out_weight_load.start()
    out_weight_load.wait()
    turned_weight = jnp.concatenate(
        [out_weight_copy[...], jnp.zeros((WIDE - variables, width), bf16)], axis=0
    )
    padded_ref[...] = turned_weight.T
    stores = []
    for index, rows in enumerate(spans):
        latent_loads[index].wait()
        for start in range(0, width, FCOLS):
            columns = slice(start, start + FCOLS)
            if index == 0:
                weight_loads[start // FCOLS].wait()
            pre = jnp.dot(latent_copy[rows, :], weight_copy[:, columns], preferred_element_type=f32)
            sig = 0.5 * jnp.tanh(0.5 * pre) + 0.5
            hidden = pre * sig
            hidden_ref[rows, columns] = hidden.astype(bf16)
            slope_ref[rows, columns] = (sig + hidden * (1.0 - sig)).astype(bf16)
        for made, out, sems in ((hidden_ref, hidden_out, hidden_sems), (slope_ref, slope_out, slope_sems)):
            store = pltpu.make_async_copy(chunk(made, rows), chunk(out, rows), sems.at[index])
            store.start()
            stores.append(store)
        for share in range(rows.start // SHARE, rows.stop // SHARE):
            forecast_ref[share] = lax.dot_general(
                turned_weight[:TALL],
                hidden_ref[share * SHARE : (share + 1) * SHARE, :],
                NT,
                preferred_element_type=f32,
            )
    for store in stores:
        store.wait()


def pinned(value):
    return pltpu.with_memory_space_constraint(value, pltpu.HBM)


def forward(latent, weight, out_weight):
    nodes, width = latent.shape
    return pl.pallas_call(
        forward_kernel,
        in_specs=[anywhere] * 3,
        out_specs=[vmem, anywhere, anywhere, vmem],
        out_shape=[
            jax.ShapeDtypeStruct((nodes // SHARE, TALL, SHARE), f32),
            pltpu.HBM((nodes, width), bf16),
            pltpu.HBM((nodes, width), bf16),
            jax.ShapeDtypeStruct((width, WIDE), bf16),
        ],
        scratch_shapes=[
            pltpu.VMEM((nodes, width), bf16),
            pltpu.VMEM((nodes, width), bf16),
            pltpu.VMEM((nodes, width), bf16),
            pltpu.VMEM((width, width), bf16),
            pltpu.VMEM(out_weight.shape, bf16),
            pltpu.SemaphoreType.DMA((len(CHUNKS),)),
            pltpu.SemaphoreType.DMA((width // FCOLS,)),
            pltpu.SemaphoreType.DMA,
            pltpu.SemaphoreType.DMA((len(CHUNKS),)),
            pltpu.SemaphoreType.DMA((len(CHUNKS),)),
        ],
        compiler_params=params(32),
        cost_estimate=cost(2 * nodes * width * (width + WIDE), 20 << 20),
        name="forward",
    )(pinned(latent), pinned(weight), pinned(out_weight))


def slope_function(diff):
    return diff * lax.rsqrt(diff * diff + smooth_sq)


def pair_kernel(place_ref, blocks_ref, observed_ref, area_ref, low_ref, here_ref, weight_ref, sems):
    members = blocks_ref.shape[0]
    variables = observed_ref.shape[0]
    at = pl.multiple_of(place_ref[0] * SHARE, SHARE)
    loads = [
        pltpu.make_async_copy(observed_ref.at[:, pl.ds(at, SHARE)], here_ref, sems.at[0]),
        pltpu.make_async_copy(area_ref.at[:, pl.ds(at, SHARE)], weight_ref, sems.at[1]),
    ]
    for load in loads:
        load.start()
    for start in range(0, TALL, 16):
        rows = slice(start, start + 16)
        values = [blocks_ref[a, rows, :] for a in range(members)]
        totals = [0.0] * members
        for a in range(members):
            for b in range(a + 1, members):
                slope = slope_function(values[a] - values[b])
                totals[a] = totals[a] + slope
                totals[b] = totals[b] - slope
        if start == 0:
            for load in loads:
                load.wait()
        area = weight_ref[...]
        real = min(16, variables - start)
        observed = here_ref[start : start + real, :]
        if real < 16:
            observed = jnp.concatenate([observed, jnp.zeros((16 - real, SHARE), f32)], axis=0)
        for a in range(members):
            field = area * (slope_function(values[a] - observed) - totals[a] * (1.0 / (members - 1)))
            low_ref[a, rows, :] = field.astype(bf16)


def pairs(place, blocks, observed, area):
    members = blocks.shape[0]
    variables = observed.shape[0]
    return pl.pallas_call(
        pair_kernel,
        in_specs=[smem, vmem, anywhere, anywhere],
        out_specs=vmem,
        out_shape=jax.ShapeDtypeStruct((members, TALL, SHARE), bf16),
        scratch_shapes=[
            pltpu.VMEM((variables, SHARE), f32),
            pltpu.VMEM((1, SHARE), f32),
            pltpu.SemaphoreType.DMA((2,)),
        ],
        compiler_params=params(8),
        cost_estimate=cost(4 << 20, 2 << 20),
        name="pairs",
    )(place, blocks, observed, area)


def position(grid_ref):
    grid = grid_ref[0]
    return grid >> 3, (grid >> 1) & 3, grid & 1


STEPS = ((1, 3), (2, 0))


def owner(block, steps, x_lo, z):
    return ((block & 1) ^ x_lo) * 4 + ((z + steps[block >> 1]) & 3)


def turn_kernel(grid_ref, latent_ref, turned_ref):
    nodes, width = latent_ref.shape
    x_lo, z, core = position(grid_ref)
    for group in range(8):
        step = (group - z) & 3
        odd = step & 1
        place = odd * (step >> 1) + (1 - odd) * (3 - (step >> 1))
        at = (place >> 1) * 512 + (place & 1) * 128 + ((group >> 2) ^ x_lo) * 64
        first = pl.multiple_of(at + (1 - core) * 256, 64)
        second = pl.multiple_of(at + core * 256, 64)
        for row in range(0, nodes, ROWS):
            columns = slice(row, row + ROWS)
            block = latent_ref[columns, group * 128 : (group + 1) * 128].T
            turned_ref[pl.ds(first, 64), columns] = block[:64]
            turned_ref[pl.ds(second, 64), columns] = block[64:]


def turned(grid, latent):
    nodes, width = latent.shape
    return pl.pallas_call(
        turn_kernel,
        in_specs=[smem, vmem],
        out_specs=vmem,
        out_shape=jax.ShapeDtypeStruct((width, nodes), bf16),
        compiler_params=params(8),
        cost_estimate=cost(0, 8 << 20),
        name="turned",
    )(grid, latent)


class PartLoads:
    def __init__(self, part, grid_ref, turned_hbm, hidden_hbm, turned_ref, hidden_ref, turned_sems, hidden_sems):
        x_lo, z, self.core = position(grid_ref)
        self.turned_ref, self.hidden_ref = turned_ref, hidden_ref
        self.turned = [
            pltpu.make_async_copy(
                turned_hbm.at[pl.ds(part * 512 + start, 256)], turned_ref.at[pl.ds(start, 256)], turned_sems.at[start // 256]
            )
            for start in (0, 256)
        ]
        self.hidden = [
            pltpu.make_async_copy(
                hidden_hbm.at[:, pl.ds(pl.multiple_of(owner(block, STEPS[part], x_lo, z) * 128, 128), 128)],
                hidden_ref.at[:, pl.ds(block * 128, 128)],
                hidden_sems.at[block],
            )
            for block in range(4)
        ]

    def start(self):
        for load in self.turned + self.hidden:
            load.start()

    def products(self, pre_ref, flat_ref, send_ref, keep_ref, second_ref):
        width = pre_ref.shape[1]
        for load, out_ref, start in zip(self.turned, (send_ref, keep_ref), (0, 256)):
            load.wait()
            for column in range(0, width, 512):
                columns = slice(column, column + 512)
                part = jnp.dot(self.turned_ref[start : start + 256, :], pre_ref[:, columns], preferred_element_type=f32)
                out_ref[:, columns] = part.astype(bf16)
        for load in self.hidden:
            load.wait()
        for start in (0, 256):
            rows = slice(start, start + 256)
            second = jnp.dot(flat_ref[...], self.hidden_ref[:, rows], preferred_element_type=f32)
            second_ref[rows, :] = second.T.astype(bf16)
        for block in range(4):
            rows = slice(block * 64, (block + 1) * 64)
            mine = pl.multiple_of(block * 128 + self.core * 64, 64)
            other = pl.multiple_of(block * 128 + (1 - self.core) * 64, 64)
            keep_ref[rows, width:] = second_ref[pl.ds(mine, 64), :]
            send_ref[rows, width:] = second_ref[pl.ds(other, 64), :]


def backward_a_kernel(
    grid_ref,
    low_ref,
    turned_hbm,
    slope_hbm,
    hidden_hbm,
    padded_ref,
    pre_ref,
    send_ref,
    keep_ref,
    flat_ref,
    turn_ref,
    turned_ref,
    hidden_ref,
    second_ref,
    slope_ref,
    turned_sems,
    hidden_sems,
    slope_sems,
):
    nodes, width = pre_ref.shape
    loads = PartLoads(0, grid_ref, turned_hbm, hidden_hbm, turned_ref, hidden_ref, turned_sems, hidden_sems)
    slope_loads = [
        pltpu.make_async_copy(
            slope_hbm.at[:, pl.ds(start, COLS)], slope_ref.at[:, pl.ds(start, COLS)], slope_sems.at[start // COLS]
        )
        for start in range(0, width, COLS)
    ]
    for load in slope_loads:
        load.start()
    loads.start()
    for share in range(low_ref.shape[0]):
        columns = slice(share * SHARE, (share + 1) * SHARE)
        low = jnp.concatenate([low_ref[share], jnp.zeros((WIDE - TALL, SHARE), bf16)], axis=0)
        flat_ref[:, columns] = low
        turn_ref[columns, :] = low.T
    for column in range(0, width, COLS):
        columns = slice(column, column + COLS)
        slope_loads[column // COLS].wait()
        for start in range(0, nodes, ROWS):
            rows = slice(start, start + ROWS)
            grad_hidden = lax.dot_general(turn_ref[rows, :], padded_ref[columns, :], NT, preferred_element_type=f32)
            pre_ref[rows, columns] = (grad_hidden * slope_ref[rows, columns].astype(f32)).astype(bf16)
    loads.products(pre_ref, flat_ref, send_ref, keep_ref, second_ref)


def backward_b_kernel(
    grid_ref,
    turned_hbm,
    hidden_hbm,
    pre_ref,
    flat_ref,
    send_ref,
    keep_ref,
    turned_ref,
    hidden_ref,
    second_ref,
    turned_sems,
    hidden_sems,
):
    loads = PartLoads(1, grid_ref, turned_hbm, hidden_hbm, turned_ref, hidden_ref, turned_sems, hidden_sems)
    loads.start()
    loads.products(pre_ref, flat_ref, send_ref, keep_ref, second_ref)


def part_shapes(nodes, width):
    out = [jax.ShapeDtypeStruct((256, width + WIDE), bf16)] * 2
    scratch = [
        pltpu.VMEM((512, nodes), bf16),
        pltpu.VMEM((nodes, 512), bf16),
        pltpu.VMEM((512, WIDE), bf16),
    ]
    sems = [pltpu.SemaphoreType.DMA((2,)), pltpu.SemaphoreType.DMA((4,))]
    return out, scratch, sems


def backward_a(grid, low, turned_latent, slope, hidden, padded):
    nodes, width = slope.shape
    out, scratch, sems = part_shapes(nodes, width)
    return pl.pallas_call(
        backward_a_kernel,
        in_specs=[smem, vmem, anywhere, anywhere, anywhere, vmem],
        out_specs=[vmem] * 4,
        out_shape=[jax.ShapeDtypeStruct((nodes, width), bf16)] + out + [jax.ShapeDtypeStruct((WIDE, nodes), bf16)],
        scratch_shapes=[pltpu.VMEM((nodes, WIDE), bf16)]
        + scratch
        + [pltpu.VMEM((nodes, width), bf16)]
        + sems
        + [pltpu.SemaphoreType.DMA((width // COLS,))],
        compiler_params=params(20),
        cost_estimate=cost(nodes * width * (width + 3 * WIDE), 8 << 20),
        name="backward_a",
    )(grid, low, pinned(turned_latent), pinned(slope), pinned(hidden), padded)


def backward_b(grid, turned_latent, hidden, grad_pre, flat):
    nodes, width = hidden.shape
    out, scratch, sems = part_shapes(nodes, width)
    return pl.pallas_call(
        backward_b_kernel,
        in_specs=[smem, anywhere, anywhere, vmem, vmem],
        out_specs=[vmem] * 2,
        out_shape=out,
        scratch_shapes=scratch + sems,
        compiler_params=params(16),
        cost_estimate=cost(nodes * width * (width + WIDE), 4 << 20),
        name="backward_b",
    )(grid, pinned(turned_latent), pinned(hidden), grad_pre, flat)


def latent_kernel(pre_ref, weight_hbm, out_ref, weight_ref, result_ref, weight_sems, sems):
    nodes, width = pre_ref.shape
    loads = [
        pltpu.make_async_copy(
            weight_hbm.at[pl.ds(start, COLS)], weight_ref.at[pl.ds(start, COLS)], weight_sems.at[start // COLS]
        )
        for start in range(0, width, COLS)
    ]
    for load in loads:
        load.start()
    stores = []
    for row in range(0, nodes, ROWS):
        rows = slice(row, row + ROWS)
        for start in range(0, width, COLS):
            if row == 0:
                loads[start // COLS].wait()
            columns = slice(start, start + COLS)
            result_ref[rows, columns] = lax.dot_general(
                pre_ref[rows, :], weight_ref[columns, :], NT, preferred_element_type=f32
            ).astype(bf16)
        store = pltpu.make_async_copy(
            result_ref.at[pl.ds(row, ROWS)], out_ref.at[pl.ds(row, ROWS)], sems.at[row // ROWS]
        )
        store.start()
        stores.append(store)
    for store in stores:
        store.wait()


def latent_gradient(grad_pre, weight):
    nodes, width = grad_pre.shape
    return pl.pallas_call(
        latent_kernel,
        in_specs=[vmem, anywhere],
        out_specs=anywhere,
        out_shape=pltpu.HBM((nodes, width), bf16),
        scratch_shapes=[
            pltpu.VMEM((width, width), bf16),
            pltpu.VMEM((nodes, width), bf16),
            pltpu.SemaphoreType.DMA((width // COLS,)),
            pltpu.SemaphoreType.DMA((nodes // ROWS,)),
        ],
        compiler_params=params(12),
        cost_estimate=cost(2 * nodes * width * width, 10 << 20),
        name="latent_gradient",
    )(grad_pre, pinned(weight))


def finish_kernel(own_ref, *refs, factor):
    *others, first_ref, second_ref = refs
    width, variables = first_ref.shape[1], second_ref.shape[1]
    total = own_ref[...].astype(f32)
    for other in others:
        total = total + other[...].astype(f32)
    total = total * factor
    first_ref[...] = total[:, :width]
    second_ref[...] = total[:, width : width + variables]


def finish(own, others, width, variables, factor):
    rows = own.shape[0]
    return pl.pallas_call(
        functools.partial(finish_kernel, factor=factor),
        in_specs=[vmem] * (1 + len(others)),
        out_specs=[vmem] * 2,
        out_shape=[jax.ShapeDtypeStruct((rows, width), f32), jax.ShapeDtypeStruct((rows, variables), f32)],
        compiler_params=params(8),
        cost_estimate=cost(0, 1 << 20),
        name="finish",
    )(own, *others)


def moved(value, move):
    moves = []
    for member in range(8):
        for grid in range(16):
            y, x_hi, x_lo, z, core = member // 2, member % 2, grid // 8, (grid // 2) % 4, grid % 2
            y, x, z, core = move(y, x_hi * 2 + x_lo, z, core)
            target = (y * 2 + x // 2) * 16 + ((x % 2) * 4 + z) * 2 + core
            moves.append((member * 16 + grid, target))
    return lax.ppermute(value, ("member", "grid"), moves)


def summed(own, others):
    total = own.astype(f32)
    for other in others:
        total = total + other.astype(f32)
    return total


def over_core(send, keep):
    got = moved(send, lambda y, x, z, c: (y, x, z, 1 - c))
    return summed(keep, [got]).astype(bf16)


def over_z(part, rows):
    blocks = rows.reshape(2, 2, 64, rows.shape[1])
    return [
        moved(block, lambda y, x, z, c, k=k: (y, x, (z + k) % 4, c)) if k else block
        for k, block in zip(STEPS[part], blocks)
    ]


def over_x(blocks):
    got = [
        moved(blocks[0] if k == 2 else blocks[1], lambda y, x, z, c, k=k: (y, x ^ k, z, c))
        for k in (1, 3, 2)
    ]
    return summed(blocks[0], got).astype(bf16)


def over_y(block):
    return [moved(block, lambda y, x, z, c, k=k: (y ^ k, x, z, c)) for k in (1, 3, 2)]


def body(latents, hidden_weight, output_weight, observed, node_area_weight):
    latent = latents[0]
    members = lax.axis_size("member")
    groups = lax.axis_size("grid")
    nodes, width = latent.shape
    variables = output_weight.shape[1]
    place = lax.axis_index("member").astype(jnp.int32).reshape(1)
    grid = lax.axis_index("grid").astype(jnp.int32).reshape(1)

    forecast, hidden, slope, padded = forward(latent, hidden_weight, output_weight.T)
    blocks, late_grid = lax.optimization_barrier(((0.25 * forecast).astype(f16), grid))
    blocks = lax.all_to_all(blocks, "member", 0, 0, tiled=True)
    turned_latent = turned(late_grid, latent)
    low = pairs(place, 4.0 * blocks.astype(f32), observed, node_area_weight.reshape(1, nodes))
    low = lax.all_to_all(low, "member", 0, 0, tiled=True)
    grad_pre, send_a, keep_a, flat = backward_a(grid, low, turned_latent, slope, hidden, padded)
    send_b, keep_b = backward_b(grid, turned_latent, hidden, grad_pre, flat)
    rows_a, send_b = lax.optimization_barrier((over_core(send_a, keep_a), send_b))
    rows_b, grad_pre = lax.optimization_barrier((over_core(send_b, keep_b), grad_pre))
    grad_latent = latent_gradient(grad_pre, hidden_weight)
    plus, minus = over_z(0, rows_a)
    across, own = over_z(1, rows_b)
    blocks = summed(own, [plus, minus, across]).astype(bf16)
    blocks, grad_latent = lax.optimization_barrier((blocks, grad_latent))
    block = over_x(blocks)
    factor = 1.0 / math.sqrt(members * nodes * groups)
    first, second = finish(block, over_y(block), width, variables, factor)
    return grad_latent[None], first, second


def solution(mesh):
    in_specs = (P("member", "grid", None), P(), P(), P(None, "grid"), P("grid"))
    out_specs = (P("member", "grid", None), P("grid", None), P("grid", None))
    return jax.shard_map(body, mesh=mesh, in_specs=in_specs, out_specs=out_specs, check_vma=False)
```

```python
import functools
import math

import jax
import jax.numpy as jnp
from jax import lax
from jax.experimental import pallas as pl
from jax.experimental.pallas import tpu as pltpu
from jax.sharding import PartitionSpec as P

smooth_sq = 0.0025
bf16 = jnp.bfloat16
f16 = jnp.float16
f32 = jnp.float32

NT = (((1,), (1,)), ((), ()))
WIDE = 128
TALL = 112
SHARE = 256
ROWS = 512
COLS = 256

vmem = pl.BlockSpec(memory_space=pltpu.VMEM)
smem = pl.BlockSpec(memory_space=pltpu.SMEM)
anywhere = pl.BlockSpec(memory_space=pltpu.HBM)


def params(mib):
    return pltpu.CompilerParams(vmem_limit_bytes=mib * 1024 * 1024)


def cost(flops, nbytes, trans=0):
    return pl.CostEstimate(flops=flops, bytes_accessed=nbytes, transcendentals=trans)


CHUNKS = (512, 512, 512, 256, 256)
FCOLS = 512


def forward_kernel(
    latent_ref,
    weight_ref,
    out_weight_ref,
    forecast_ref,
    hidden_out,
    slope_out,
    padded_ref,
    hidden_ref,
    slope_ref,
    latent_copy,
    weight_copy,
    out_weight_copy,
    latent_sems,
    weight_sems,
    out_weight_sem,
    hidden_sems,
    slope_sems,
):
    nodes, width = latent_ref.shape
    variables = out_weight_ref.shape[0]
    out_weight_load = pltpu.make_async_copy(out_weight_ref, out_weight_copy, out_weight_sem)
    spans = []
    for size in CHUNKS:
        begin = spans[-1].stop if spans else 0
        spans.append(slice(begin, begin + size))
    weight_loads = [
        pltpu.make_async_copy(
            weight_ref.at[:, pl.ds(start, FCOLS)], weight_copy.at[:, pl.ds(start, FCOLS)], weight_sems.at[start // FCOLS]
        )
        for start in range(0, width, FCOLS)
    ]

    def chunk(ref, rows):
        return ref.at[pl.ds(rows.start, rows.stop - rows.start)]

    latent_loads = [
        pltpu.make_async_copy(chunk(latent_ref, rows), chunk(latent_copy, rows), latent_sems.at[index])
        for index, rows in enumerate(spans)
    ]
    weight_loads[0].start()
    latent_loads[0].start()
    for load in weight_loads[1:] + latent_loads[1:]:
        load.start()
    out_weight_load.start()
    out_weight_load.wait()
    turned_weight = jnp.concatenate(
        [out_weight_copy[...], jnp.zeros((WIDE - variables, width), bf16)], axis=0
    )
    padded_ref[...] = turned_weight.T
    stores = []
    for index, rows in enumerate(spans):
        latent_loads[index].wait()
        for start in range(0, width, FCOLS):
            columns = slice(start, start + FCOLS)
            if index == 0:
                weight_loads[start // FCOLS].wait()
            pre = jnp.dot(latent_copy[rows, :], weight_copy[:, columns], preferred_element_type=f32)
            sig = 0.5 * jnp.tanh(0.5 * pre) + 0.5
            hidden = pre * sig
            hidden_ref[rows, columns] = hidden.astype(bf16)
            slope_ref[rows, columns] = (sig + hidden * (1.0 - sig)).astype(bf16)
        for made, out, sems in ((hidden_ref, hidden_out, hidden_sems), (slope_ref, slope_out, slope_sems)):
            store = pltpu.make_async_copy(chunk(made, rows), chunk(out, rows), sems.at[index])
            store.start()
            stores.append(store)
        for share in range(rows.start // SHARE, rows.stop // SHARE):
            forecast_ref[share] = lax.dot_general(
                turned_weight[:TALL],
                hidden_ref[share * SHARE : (share + 1) * SHARE, :],
                NT,
                preferred_element_type=f32,
            )
    for store in stores:
        store.wait()


def pinned(value):
    return pltpu.with_memory_space_constraint(value, pltpu.HBM)


def forward(latent, weight, out_weight):
    nodes, width = latent.shape
    return pl.pallas_call(
        forward_kernel,
        in_specs=[anywhere] * 3,
        out_specs=[vmem, anywhere, anywhere, vmem],
        out_shape=[
            jax.ShapeDtypeStruct((nodes // SHARE, TALL, SHARE), f32),
            pltpu.HBM((nodes, width), bf16),
            pltpu.HBM((nodes, width), bf16),
            jax.ShapeDtypeStruct((width, WIDE), bf16),
        ],
        scratch_shapes=[
            pltpu.VMEM((nodes, width), bf16),
            pltpu.VMEM((nodes, width), bf16),
            pltpu.VMEM((nodes, width), bf16),
            pltpu.VMEM((width, width), bf16),
            pltpu.VMEM(out_weight.shape, bf16),
            pltpu.SemaphoreType.DMA((len(CHUNKS),)),
            pltpu.SemaphoreType.DMA((width // FCOLS,)),
            pltpu.SemaphoreType.DMA,
            pltpu.SemaphoreType.DMA((len(CHUNKS),)),
            pltpu.SemaphoreType.DMA((len(CHUNKS),)),
        ],
        compiler_params=params(32),
        cost_estimate=cost(2 * nodes * width * (width + WIDE), 20 << 20),
        name="forward",
    )(pinned(latent), pinned(weight), pinned(out_weight))


def slope_function(diff):
    return diff * lax.rsqrt(diff * diff + smooth_sq)


def pair_kernel(place_ref, blocks_ref, observed_ref, area_ref, low_ref, here_ref, weight_ref, sems):
    members = blocks_ref.shape[0]
    variables = observed_ref.shape[0]
    at = pl.multiple_of(place_ref[0] * SHARE, SHARE)
    loads = [
        pltpu.make_async_copy(observed_ref.at[:, pl.ds(at, SHARE)], here_ref, sems.at[0]),
        pltpu.make_async_copy(area_ref.at[:, pl.ds(at, SHARE)], weight_ref, sems.at[1]),
    ]
    for load in loads:
        load.start()
    for start in range(0, TALL, 16):
        rows = slice(start, start + 16)
        values = [blocks_ref[a, rows, :] for a in range(members)]
        totals = [0.0] * members
        for a in range(members):
            for b in range(a + 1, members):
                slope = slope_function(values[a] - values[b])
                totals[a] = totals[a] + slope
                totals[b] = totals[b] - slope
        if start == 0:
            for load in loads:
                load.wait()
        area = weight_ref[...]
        real = min(16, variables - start)
        observed = here_ref[start : start + real, :]
        if real < 16:
            observed = jnp.concatenate([observed, jnp.zeros((16 - real, SHARE), f32)], axis=0)
        for a in range(members):
            field = area * (slope_function(values[a] - observed) - totals[a] * (1.0 / (members - 1)))
            low_ref[a, rows, :] = field.astype(bf16)


def pairs(place, blocks, observed, area):
    members = blocks.shape[0]
    variables = observed.shape[0]
    return pl.pallas_call(
        pair_kernel,
        in_specs=[smem, vmem, anywhere, anywhere],
        out_specs=vmem,
        out_shape=jax.ShapeDtypeStruct((members, TALL, SHARE), bf16),
        scratch_shapes=[
            pltpu.VMEM((variables, SHARE), f32),
            pltpu.VMEM((1, SHARE), f32),
            pltpu.SemaphoreType.DMA((2,)),
        ],
        compiler_params=params(8),
        cost_estimate=cost(4 << 20, 2 << 20),
        name="pairs",
    )(place, blocks, observed, area)


def position(grid_ref):
    grid = grid_ref[0]
    return grid >> 3, (grid >> 1) & 3, grid & 1


STEPS = ((1, 3), (2, 0))


def owner(block, steps, x_lo, z):
    return ((block & 1) ^ x_lo) * 4 + ((z + steps[block >> 1]) & 3)


def turn_kernel(grid_ref, latent_ref, turned_ref):
    nodes, width = latent_ref.shape
    x_lo, z, core = position(grid_ref)
    for group in range(8):
        step = (group - z) & 3
        odd = step & 1
        place = odd * (step >> 1) + (1 - odd) * (3 - (step >> 1))
        at = (place >> 1) * 512 + (place & 1) * 128 + ((group >> 2) ^ x_lo) * 64
        first = pl.multiple_of(at + (1 - core) * 256, 64)
        second = pl.multiple_of(at + core * 256, 64)
        for row in range(0, nodes, ROWS):
            columns = slice(row, row + ROWS)
            block = latent_ref[columns, group * 128 : (group + 1) * 128].T
            turned_ref[pl.ds(first, 64), columns] = block[:64]
            turned_ref[pl.ds(second, 64), columns] = block[64:]


def turned(grid, latent):
    nodes, width = latent.shape
    return pl.pallas_call(
        turn_kernel,
        in_specs=[smem, vmem],
        out_specs=vmem,
        out_shape=jax.ShapeDtypeStruct((width, nodes), bf16),
        compiler_params=params(8),
        cost_estimate=cost(0, 8 << 20),
        name="turned",
    )(grid, latent)


def turned_load(turned_hbm, start, turned_ref, sem):
    return pltpu.make_async_copy(turned_hbm.at[pl.ds(start, 256)], turned_ref, sem)


def hidden_loads(part, grid_ref, hidden_hbm, hidden_ref, sems):
    x_lo, z, core = position(grid_ref)
    return [
        pltpu.make_async_copy(
            hidden_hbm.at[:, pl.ds(pl.multiple_of(owner(block, STEPS[part], x_lo, z) * 128, 128), 128)],
            hidden_ref.at[:, pl.ds(block * 128, 128)],
            sems.at[block],
        )
        for block in range(4)
    ]


def first_product(turned_ref, pre_ref, out_ref):
    width = pre_ref.shape[1]
    for column in range(0, width, 512):
        columns = slice(column, column + 512)
        part = jnp.dot(turned_ref[...], pre_ref[:, columns], preferred_element_type=f32)
        out_ref[:, columns] = part.astype(bf16)


def second_product(grid_ref, flat_ref, hidden_ref, send_ref, second_ref, scratch_ref):
    width = send_ref.shape[1] - WIDE
    core = position(grid_ref)[2]
    for start in (0, 256):
        rows = slice(start, start + 256)
        second = jnp.dot(flat_ref[...], hidden_ref[:, rows], preferred_element_type=f32)
        scratch_ref[rows, :] = second.T.astype(bf16)
    for block in range(4):
        rows = slice(block * 64, (block + 1) * 64)
        mine = pl.multiple_of(block * 128 + core * 64, 64)
        other = pl.multiple_of(block * 128 + (1 - core) * 64, 64)
        second_ref[rows, :] = scratch_ref[pl.ds(mine, 64), :]
        send_ref[rows, width:] = scratch_ref[pl.ds(other, 64), :]


def send_a_kernel(
    grid_ref,
    low_ref,
    turned_hbm,
    slope_hbm,
    hidden_hbm,
    padded_ref,
    pre_ref,
    send_ref,
    second_ref,
    flat_ref,
    next_turned_ref,
    turn_ref,
    turned_ref,
    hidden_ref,
    scratch_ref,
    slope_ref,
    turned_sems,
    hidden_sems,
    slope_sems,
):
    nodes, width = pre_ref.shape
    slope_loads = [
        pltpu.make_async_copy(
            slope_hbm.at[:, pl.ds(start, COLS)], slope_ref.at[:, pl.ds(start, COLS)], slope_sems.at[start // COLS]
        )
        for start in range(0, width, COLS)
    ]
    turned_now = turned_load(turned_hbm, 0, turned_ref, turned_sems.at[0])
    turned_next = turned_load(turned_hbm, 256, next_turned_ref, turned_sems.at[1])
    hidden_now = hidden_loads(0, grid_ref, hidden_hbm, hidden_ref, hidden_sems)
    for load in slope_loads + [turned_now] + hidden_now + [turned_next]:
        load.start()
    for share in range(low_ref.shape[0]):
        columns = slice(share * SHARE, (share + 1) * SHARE)
        low = jnp.concatenate([low_ref[share], jnp.zeros((WIDE - TALL, SHARE), bf16)], axis=0)
        flat_ref[:, columns] = low
        turn_ref[columns, :] = low.T
    for column in range(0, width, COLS):
        columns = slice(column, column + COLS)
        slope_loads[column // COLS].wait()
        for start in range(0, nodes, ROWS):
            rows = slice(start, start + ROWS)
            grad_hidden = lax.dot_general(turn_ref[rows, :], padded_ref[columns, :], NT, preferred_element_type=f32)
            pre_ref[rows, columns] = (grad_hidden * slope_ref[rows, columns].astype(f32)).astype(bf16)
    turned_now.wait()
    first_product(turned_ref, pre_ref, send_ref)
    for load in hidden_now:
        load.wait()
    second_product(grid_ref, flat_ref, hidden_ref, send_ref, second_ref, scratch_ref)
    turned_next.wait()


def keep_a_kernel(
    grid_ref,
    turned_hbm,
    hidden_hbm,
    pre_ref,
    turned_ref,
    second_ref,
    keep_ref,
    next_turned_ref,
    next_hidden_ref,
    turned_sem,
    hidden_sems,
):
    loads = [turned_load(turned_hbm, 512, next_turned_ref, turned_sem)]
    loads += hidden_loads(1, grid_ref, hidden_hbm, next_hidden_ref, hidden_sems)
    for load in loads:
        load.start()
    first_product(turned_ref, pre_ref, keep_ref)
    keep_ref[:, pre_ref.shape[1] :] = second_ref[...]
    for load in loads:
        load.wait()


def send_b_kernel(
    grid_ref,
    turned_hbm,
    pre_ref,
    flat_ref,
    turned_ref,
    hidden_ref,
    send_ref,
    second_ref,
    next_turned_ref,
    scratch_ref,
    turned_sem,
):
    load = turned_load(turned_hbm, 768, next_turned_ref, turned_sem)
    load.start()
    first_product(turned_ref, pre_ref, send_ref)
    second_product(grid_ref, flat_ref, hidden_ref, send_ref, second_ref, scratch_ref)
    load.wait()


def keep_b_kernel(weight_hbm, pre_ref, turned_ref, second_ref, keep_ref, weight_ref, weight_sem):
    load = pltpu.make_async_copy(weight_hbm, weight_ref, weight_sem)
    load.start()
    first_product(turned_ref, pre_ref, keep_ref)
    keep_ref[:, pre_ref.shape[1] :] = second_ref[...]
    load.wait()


def shape(*dims):
    return jax.ShapeDtypeStruct(dims, bf16)


def send_a(grid, low, turned_latent, slope, hidden, padded):
    nodes, width = slope.shape
    return pl.pallas_call(
        send_a_kernel,
        in_specs=[smem, vmem, anywhere, anywhere, anywhere, vmem],
        out_specs=[vmem] * 5,
        out_shape=[
            shape(nodes, width),
            shape(256, width + WIDE),
            shape(256, WIDE),
            shape(WIDE, nodes),
            shape(256, nodes),
        ],
        scratch_shapes=[
            pltpu.VMEM((nodes, WIDE), bf16),
            pltpu.VMEM((256, nodes), bf16),
            pltpu.VMEM((nodes, 512), bf16),
            pltpu.VMEM((512, WIDE), bf16),
            pltpu.VMEM((nodes, width), bf16),
            pltpu.SemaphoreType.DMA((2,)),
            pltpu.SemaphoreType.DMA((4,)),
            pltpu.SemaphoreType.DMA((width // COLS,)),
        ],
        compiler_params=params(20),
        cost_estimate=cost(nodes * width * (width // 2 + 3 * WIDE), 8 << 20),
        name="send_a",
    )(grid, low, pinned(turned_latent), pinned(slope), pinned(hidden), padded)


def keep_a(grid, turned_latent, hidden, grad_pre, turned_now, second):
    nodes, width = hidden.shape
    return pl.pallas_call(
        keep_a_kernel,
        in_specs=[smem, anywhere, anywhere] + [vmem] * 3,
        out_specs=[vmem] * 3,
        out_shape=[shape(256, width + WIDE), shape(256, nodes), shape(nodes, 512)],
        scratch_shapes=[pltpu.SemaphoreType.DMA, pltpu.SemaphoreType.DMA((4,))],
        compiler_params=params(12),
        cost_estimate=cost(nodes * width * width // 2, 4 << 20),
        name="keep_a",
    )(grid, pinned(turned_latent), pinned(hidden), grad_pre, turned_now, second)


def send_b(grid, turned_latent, grad_pre, flat, turned_now, hidden_now):
    nodes, width = grad_pre.shape
    return pl.pallas_call(
        send_b_kernel,
        in_specs=[smem, anywhere] + [vmem] * 4,
        out_specs=[vmem] * 3,
        out_shape=[shape(256, width + WIDE), shape(256, WIDE), shape(256, nodes)],
        scratch_shapes=[pltpu.VMEM((512, WIDE), bf16), pltpu.SemaphoreType.DMA],
        compiler_params=params(12),
        cost_estimate=cost(nodes * width * width // 2, 4 << 20),
        name="send_b",
    )(grid, pinned(turned_latent), grad_pre, flat, turned_now, hidden_now)


def keep_b(weight, grad_pre, turned_now, second):
    nodes, width = grad_pre.shape
    return pl.pallas_call(
        keep_b_kernel,
        in_specs=[anywhere] + [vmem] * 3,
        out_specs=[vmem] * 2,
        out_shape=[shape(256, width + WIDE), shape(width, width)],
        scratch_shapes=[pltpu.SemaphoreType.DMA],
        compiler_params=params(12),
        cost_estimate=cost(nodes * width * width // 2, 4 << 20),
        name="keep_b",
    )(pinned(weight), grad_pre, turned_now, second)


def latent_kernel(pre_ref, weight_ref, out_ref, result_ref, sems):
    nodes, width = pre_ref.shape
    stores = []
    for row in range(0, nodes, ROWS):
        rows = slice(row, row + ROWS)
        for start in range(0, width, COLS):
            columns = slice(start, start + COLS)
            result_ref[rows, columns] = lax.dot_general(
                pre_ref[rows, :], weight_ref[columns, :], NT, preferred_element_type=f32
            ).astype(bf16)
        store = pltpu.make_async_copy(
            result_ref.at[pl.ds(row, ROWS)], out_ref.at[pl.ds(row, ROWS)], sems.at[row // ROWS]
        )
        store.start()
        stores.append(store)
    for store in stores:
        store.wait()


def latent_gradient(grad_pre, weight):
    nodes, width = grad_pre.shape
    return pl.pallas_call(
        latent_kernel,
        in_specs=[vmem, vmem],
        out_specs=anywhere,
        out_shape=pltpu.HBM((nodes, width), bf16),
        scratch_shapes=[pltpu.VMEM((nodes, width), bf16), pltpu.SemaphoreType.DMA((nodes // ROWS,))],
        compiler_params=params(12),
        cost_estimate=cost(2 * nodes * width * width, 10 << 20),
        name="latent_gradient",
    )(grad_pre, weight)


def finish_kernel(own_ref, *refs, factor):
    *others, first_ref, second_ref = refs
    width, variables = first_ref.shape[1], second_ref.shape[1]
    total = own_ref[...].astype(f32)
    for other in others:
        total = total + other[...].astype(f32)
    total = total * factor
    first_ref[...] = total[:, :width]
    second_ref[...] = total[:, width : width + variables]


def finish(own, others, width, variables, factor):
    rows = own.shape[0]
    return pl.pallas_call(
        functools.partial(finish_kernel, factor=factor),
        in_specs=[vmem] * (1 + len(others)),
        out_specs=[vmem] * 2,
        out_shape=[jax.ShapeDtypeStruct((rows, width), f32), jax.ShapeDtypeStruct((rows, variables), f32)],
        compiler_params=params(8),
        cost_estimate=cost(0, 1 << 20),
        name="finish",
    )(own, *others)


def moved(value, move):
    moves = []
    for member in range(8):
        for grid in range(16):
            y, x_hi, x_lo, z, core = member // 2, member % 2, grid // 8, (grid // 2) % 4, grid % 2
            y, x, z, core = move(y, x_hi * 2 + x_lo, z, core)
            target = (y * 2 + x // 2) * 16 + ((x % 2) * 4 + z) * 2 + core
            moves.append((member * 16 + grid, target))
    return lax.ppermute(value, ("member", "grid"), moves)


def summed(own, others):
    total = own.astype(f32)
    for other in others:
        total = total + other.astype(f32)
    return total


def over_core(send, keep):
    got = moved(send, lambda y, x, z, c: (y, x, z, 1 - c))
    return summed(keep, [got]).astype(bf16)


def over_z(part, rows):
    blocks = rows.reshape(2, 2, 64, rows.shape[1])
    return [
        moved(block, lambda y, x, z, c, k=k: (y, x, (z + k) % 4, c)) if k else block
        for k, block in zip(STEPS[part], blocks)
    ]


def over_x(blocks):
    got = [
        moved(blocks[0] if k == 2 else blocks[1], lambda y, x, z, c, k=k: (y, x ^ k, z, c))
        for k in (1, 3, 2)
    ]
    return summed(blocks[0], got).astype(bf16)


def over_y(block):
    return [moved(block, lambda y, x, z, c, k=k: (y ^ k, x, z, c)) for k in (1, 3, 2)]


def body(latents, hidden_weight, output_weight, observed, node_area_weight):
    latent = latents[0]
    members = lax.axis_size("member")
    groups = lax.axis_size("grid")
    nodes, width = latent.shape
    variables = output_weight.shape[1]
    place = lax.axis_index("member").astype(jnp.int32).reshape(1)
    grid = lax.axis_index("grid").astype(jnp.int32).reshape(1)

    forecast, hidden, slope, padded = forward(latent, hidden_weight, output_weight.T)
    blocks, late_grid = lax.optimization_barrier(((0.25 * forecast).astype(f16), grid))
    blocks = lax.all_to_all(blocks, "member", 0, 0, tiled=True)
    turned_latent = turned(late_grid, latent)
    low = pairs(place, 4.0 * blocks.astype(f32), observed, node_area_weight.reshape(1, nodes))
    low = lax.all_to_all(low, "member", 0, 0, tiled=True)
    grad_pre, rows_a, second_a, flat, turned_now = send_a(grid, low, turned_latent, slope, hidden, padded)
    kept_a, turned_now, hidden_now = keep_a(grid, turned_latent, hidden, grad_pre, turned_now, second_a)
    rows_a, flat = lax.optimization_barrier((over_core(rows_a, kept_a), flat))
    rows_b, second_b, turned_now = send_b(grid, turned_latent, grad_pre, flat, turned_now, hidden_now)
    kept_b, weight_copy = keep_b(hidden_weight, grad_pre, turned_now, second_b)
    rows_b, grad_pre = lax.optimization_barrier((over_core(rows_b, kept_b), grad_pre))
    grad_latent = latent_gradient(grad_pre, weight_copy)
    plus, minus = over_z(0, rows_a)
    across, own = over_z(1, rows_b)
    blocks = summed(own, [plus, minus, across]).astype(bf16)
    blocks, grad_latent = lax.optimization_barrier((blocks, grad_latent))
    block = over_x(blocks)
    factor = 1.0 / math.sqrt(members * nodes * groups)
    first, second = finish(block, over_y(block), width, variables, factor)
    return grad_latent[None], first, second


def solution(mesh):
    in_specs = (P("member", "grid", None), P(), P(), P(None, "grid"), P("grid"))
    out_specs = (P("member", "grid", None), P("grid", None), P("grid", None))
    return jax.shard_map(body, mesh=mesh, in_specs=in_specs, out_specs=out_specs, check_vma=False)
```

```python
import functools
import math

import jax
import jax.numpy as jnp
from jax import lax
from jax.experimental import pallas as pl
from jax.experimental.pallas import tpu as pltpu
from jax.sharding import PartitionSpec as P

smooth_sq = 0.0025
bf16 = jnp.bfloat16
f16 = jnp.float16
f32 = jnp.float32

NT = (((1,), (1,)), ((), ()))
WIDE = 128
TALL = 112
SHARE = 256
ROWS = 512
COLS = 256

vmem = pl.BlockSpec(memory_space=pltpu.VMEM)
smem = pl.BlockSpec(memory_space=pltpu.SMEM)
anywhere = pl.BlockSpec(memory_space=pltpu.HBM)


def params(mib):
    return pltpu.CompilerParams(vmem_limit_bytes=mib * 1024 * 1024)


def cost(flops, nbytes, trans=0):
    return pl.CostEstimate(flops=flops, bytes_accessed=nbytes, transcendentals=trans)


CHUNKS = (512, 512, 512, 256, 256)
FCOLS = 512


def forward_kernel(
    latent_ref,
    weight_ref,
    out_weight_ref,
    forecast_ref,
    hidden_out,
    slope_out,
    padded_ref,
    hidden_ref,
    slope_ref,
    latent_copy,
    weight_copy,
    out_weight_copy,
    latent_sems,
    weight_sems,
    out_weight_sem,
    hidden_sems,
    slope_sems,
):
    nodes, width = latent_ref.shape
    variables = out_weight_ref.shape[0]
    out_weight_load = pltpu.make_async_copy(out_weight_ref, out_weight_copy, out_weight_sem)
    spans = []
    for size in CHUNKS:
        begin = spans[-1].stop if spans else 0
        spans.append(slice(begin, begin + size))
    weight_loads = [
        pltpu.make_async_copy(
            weight_ref.at[:, pl.ds(start, FCOLS)], weight_copy.at[:, pl.ds(start, FCOLS)], weight_sems.at[start // FCOLS]
        )
        for start in range(0, width, FCOLS)
    ]

    def chunk(ref, rows):
        return ref.at[pl.ds(rows.start, rows.stop - rows.start)]

    latent_loads = [
        pltpu.make_async_copy(chunk(latent_ref, rows), chunk(latent_copy, rows), latent_sems.at[index])
        for index, rows in enumerate(spans)
    ]
    weight_loads[0].start()
    latent_loads[0].start()
    for load in weight_loads[1:] + latent_loads[1:]:
        load.start()
    out_weight_load.start()
    out_weight_load.wait()
    turned_weight = jnp.concatenate(
        [out_weight_copy[...], jnp.zeros((WIDE - variables, width), bf16)], axis=0
    )
    padded_ref[...] = turned_weight.T
    stores = []
    for index, rows in enumerate(spans):
        latent_loads[index].wait()
        for start in range(0, width, FCOLS):
            columns = slice(start, start + FCOLS)
            if index == 0:
                weight_loads[start // FCOLS].wait()
            pre = jnp.dot(latent_copy[rows, :], weight_copy[:, columns], preferred_element_type=f32)
            sig = 0.5 * jnp.tanh(0.5 * pre) + 0.5
            hidden = pre * sig
            hidden_ref[rows, columns] = hidden.astype(bf16)
            slope_ref[rows, columns] = (sig + hidden * (1.0 - sig)).astype(bf16)
        for made, out, sems in ((hidden_ref, hidden_out, hidden_sems), (slope_ref, slope_out, slope_sems)):
            store = pltpu.make_async_copy(chunk(made, rows), chunk(out, rows), sems.at[index])
            store.start()
            stores.append(store)
        for share in range(rows.start // SHARE, rows.stop // SHARE):
            forecast_ref[share] = lax.dot_general(
                turned_weight[:TALL],
                hidden_ref[share * SHARE : (share + 1) * SHARE, :],
                NT,
                preferred_element_type=f32,
            )
    for store in stores:
        store.wait()


def pinned(value):
    return pltpu.with_memory_space_constraint(value, pltpu.HBM)


def forward(latent, weight, out_weight):
    nodes, width = latent.shape
    return pl.pallas_call(
        forward_kernel,
        in_specs=[anywhere] * 3,
        out_specs=[vmem, anywhere, anywhere, vmem],
        out_shape=[
            jax.ShapeDtypeStruct((nodes // SHARE, TALL, SHARE), f32),
            pltpu.HBM((nodes, width), bf16),
            pltpu.HBM((nodes, width), bf16),
            jax.ShapeDtypeStruct((width, WIDE), bf16),
        ],
        scratch_shapes=[
            pltpu.VMEM((nodes, width), bf16),
            pltpu.VMEM((nodes, width), bf16),
            pltpu.VMEM((nodes, width), bf16),
            pltpu.VMEM((width, width), bf16),
            pltpu.VMEM(out_weight.shape, bf16),
            pltpu.SemaphoreType.DMA((len(CHUNKS),)),
            pltpu.SemaphoreType.DMA((width // FCOLS,)),
            pltpu.SemaphoreType.DMA,
            pltpu.SemaphoreType.DMA((len(CHUNKS),)),
            pltpu.SemaphoreType.DMA((len(CHUNKS),)),
        ],
        compiler_params=params(32),
        cost_estimate=cost(2 * nodes * width * (width + WIDE), 20 << 20),
        name="forward",
    )(pinned(latent), pinned(weight), pinned(out_weight))


def slope_function(diff):
    return diff * lax.rsqrt(diff * diff + smooth_sq)


def pair_kernel(place_ref, blocks_ref, observed_ref, area_ref, low_ref, here_ref, weight_ref, sems):
    members = blocks_ref.shape[0]
    variables = observed_ref.shape[0]
    at = pl.multiple_of(place_ref[0] * SHARE, SHARE)
    loads = [
        pltpu.make_async_copy(observed_ref.at[:, pl.ds(at, SHARE)], here_ref, sems.at[0]),
        pltpu.make_async_copy(area_ref.at[:, pl.ds(at, SHARE)], weight_ref, sems.at[1]),
    ]
    for load in loads:
        load.start()
    for start in range(0, TALL, 16):
        rows = slice(start, start + 16)
        values = [blocks_ref[a, rows, :] for a in range(members)]
        totals = [0.0] * members
        for a in range(members):
            for b in range(a + 1, members):
                slope = slope_function(values[a] - values[b])
                totals[a] = totals[a] + slope
                totals[b] = totals[b] - slope
        if start == 0:
            for load in loads:
                load.wait()
        area = weight_ref[...]
        real = min(16, variables - start)
        observed = here_ref[start : start + real, :]
        if real < 16:
            observed = jnp.concatenate([observed, jnp.zeros((16 - real, SHARE), f32)], axis=0)
        for a in range(members):
            field = area * (slope_function(values[a] - observed) - totals[a] * (1.0 / (members - 1)))
            low_ref[a, rows, :] = field.astype(bf16)


def pairs(place, blocks, observed, area):
    members = blocks.shape[0]
    variables = observed.shape[0]
    return pl.pallas_call(
        pair_kernel,
        in_specs=[smem, vmem, anywhere, anywhere],
        out_specs=vmem,
        out_shape=jax.ShapeDtypeStruct((members, TALL, SHARE), bf16),
        scratch_shapes=[
            pltpu.VMEM((variables, SHARE), f32),
            pltpu.VMEM((1, SHARE), f32),
            pltpu.SemaphoreType.DMA((2,)),
        ],
        compiler_params=params(8),
        cost_estimate=cost(4 << 20, 2 << 20),
        name="pairs",
    )(place, blocks, observed, area)


def position(grid_ref):
    grid = grid_ref[0]
    return grid >> 3, (grid >> 1) & 3, grid & 1


STEPS = ((2, 0), (1, 3))


def owner(block, steps, x_lo, z):
    return ((block & 1) ^ x_lo) * 4 + ((z + steps[block >> 1]) & 3)


def turn_kernel(grid_ref, latent_ref, turned_ref):
    nodes, width = latent_ref.shape
    x_lo, z, core = position(grid_ref)
    for group in range(8):
        step = (group - z) & 3
        odd = step & 1
        place = odd * (2 + (step >> 1)) + (1 - odd) * (1 - (step >> 1))
        at = (place >> 1) * 512 + (place & 1) * 128 + ((group >> 2) ^ x_lo) * 64
        first = pl.multiple_of(at + (1 - core) * 256, 64)
        second = pl.multiple_of(at + core * 256, 64)
        for row in range(0, nodes, ROWS):
            columns = slice(row, row + ROWS)
            block = latent_ref[columns, group * 128 : (group + 1) * 128].T
            turned_ref[pl.ds(first, 64), columns] = block[:64]
            turned_ref[pl.ds(second, 64), columns] = block[64:]


def turned(grid, latent):
    nodes, width = latent.shape
    return pl.pallas_call(
        turn_kernel,
        in_specs=[smem, vmem],
        out_specs=vmem,
        out_shape=jax.ShapeDtypeStruct((width, nodes), bf16),
        compiler_params=params(8),
        cost_estimate=cost(0, 8 << 20),
        name="turned",
    )(grid, latent)


def turned_load(turned_hbm, start, turned_ref, sem):
    return pltpu.make_async_copy(turned_hbm.at[pl.ds(start, 256)], turned_ref, sem)


def hidden_loads(part, grid_ref, hidden_hbm, hidden_ref, sems):
    x_lo, z, core = position(grid_ref)
    return [
        pltpu.make_async_copy(
            hidden_hbm.at[:, pl.ds(pl.multiple_of(owner(block, STEPS[part], x_lo, z) * 128, 128), 128)],
            hidden_ref.at[:, pl.ds(block * 128, 128)],
            sems.at[block],
        )
        for block in range(4)
    ]


def first_product(turned_ref, pre_ref, out_ref):
    width = pre_ref.shape[1]
    for column in range(0, width, 512):
        columns = slice(column, column + 512)
        part = jnp.dot(turned_ref[...], pre_ref[:, columns], preferred_element_type=f32)
        out_ref[:, columns] = part.astype(bf16)


def second_product(grid_ref, flat_ref, hidden_ref, send_ref, second_ref, scratch_ref):
    width = send_ref.shape[1] - WIDE
    core = position(grid_ref)[2]
    for start in (0, 256):
        rows = slice(start, start + 256)
        second = jnp.dot(flat_ref[...], hidden_ref[:, rows], preferred_element_type=f32)
        scratch_ref[rows, :] = second.T.astype(bf16)
    for block in range(4):
        rows = slice(block * 64, (block + 1) * 64)
        mine = pl.multiple_of(block * 128 + core * 64, 64)
        other = pl.multiple_of(block * 128 + (1 - core) * 64, 64)
        second_ref[rows, :] = scratch_ref[pl.ds(mine, 64), :]
        send_ref[rows, width:] = scratch_ref[pl.ds(other, 64), :]


def send_a_kernel(
    grid_ref,
    low_ref,
    turned_hbm,
    slope_hbm,
    hidden_hbm,
    padded_ref,
    pre_ref,
    send_ref,
    second_ref,
    flat_ref,
    next_turned_ref,
    turn_ref,
    turned_ref,
    hidden_ref,
    scratch_ref,
    slope_ref,
    turned_sems,
    hidden_sems,
    slope_sems,
):
    nodes, width = pre_ref.shape
    slope_loads = [
        pltpu.make_async_copy(
            slope_hbm.at[:, pl.ds(start, COLS)], slope_ref.at[:, pl.ds(start, COLS)], slope_sems.at[start // COLS]
        )
        for start in range(0, width, COLS)
    ]
    turned_now = turned_load(turned_hbm, 0, turned_ref, turned_sems.at[0])
    turned_next = turned_load(turned_hbm, 256, next_turned_ref, turned_sems.at[1])
    hidden_now = hidden_loads(0, grid_ref, hidden_hbm, hidden_ref, hidden_sems)
    for load in slope_loads + [turned_now] + hidden_now + [turned_next]:
        load.start()
    for share in range(low_ref.shape[0]):
        columns = slice(share * SHARE, (share + 1) * SHARE)
        low = jnp.concatenate([low_ref[share], jnp.zeros((WIDE - TALL, SHARE), bf16)], axis=0)
        flat_ref[:, columns] = low
        turn_ref[columns, :] = low.T
    for column in range(0, width, COLS):
        columns = slice(column, column + COLS)
        slope_loads[column // COLS].wait()
        for start in range(0, nodes, ROWS):
            rows = slice(start, start + ROWS)
            grad_hidden = lax.dot_general(turn_ref[rows, :], padded_ref[columns, :], NT, preferred_element_type=f32)
            pre_ref[rows, columns] = (grad_hidden * slope_ref[rows, columns].astype(f32)).astype(bf16)
    turned_now.wait()
    first_product(turned_ref, pre_ref, send_ref)
    for load in hidden_now:
        load.wait()
    second_product(grid_ref, flat_ref, hidden_ref, send_ref, second_ref, scratch_ref)
    turned_next.wait()


def keep_a_kernel(
    grid_ref,
    turned_hbm,
    hidden_hbm,
    pre_ref,
    turned_ref,
    second_ref,
    keep_ref,
    next_turned_ref,
    next_hidden_ref,
    turned_sem,
    hidden_sems,
):
    loads = [turned_load(turned_hbm, 512, next_turned_ref, turned_sem)]
    loads += hidden_loads(1, grid_ref, hidden_hbm, next_hidden_ref, hidden_sems)
    for load in loads:
        load.start()
    first_product(turned_ref, pre_ref, keep_ref)
    keep_ref[:, pre_ref.shape[1] :] = second_ref[...]
    for load in loads:
        load.wait()


def send_b_kernel(
    grid_ref,
    turned_hbm,
    pre_ref,
    flat_ref,
    turned_ref,
    hidden_ref,
    send_ref,
    second_ref,
    next_turned_ref,
    scratch_ref,
    turned_sem,
):
    load = turned_load(turned_hbm, 768, next_turned_ref, turned_sem)
    load.start()
    first_product(turned_ref, pre_ref, send_ref)
    second_product(grid_ref, flat_ref, hidden_ref, send_ref, second_ref, scratch_ref)
    load.wait()


def keep_b_kernel(weight_hbm, pre_ref, turned_ref, second_ref, keep_ref, weight_ref, weight_sem):
    load = pltpu.make_async_copy(weight_hbm, weight_ref, weight_sem)
    load.start()
    first_product(turned_ref, pre_ref, keep_ref)
    keep_ref[:, pre_ref.shape[1] :] = second_ref[...]
    load.wait()


def shape(*dims):
    return jax.ShapeDtypeStruct(dims, bf16)


def send_a(grid, low, turned_latent, slope, hidden, padded):
    nodes, width = slope.shape
    return pl.pallas_call(
        send_a_kernel,
        in_specs=[smem, vmem, anywhere, anywhere, anywhere, vmem],
        out_specs=[vmem] * 5,
        out_shape=[
            shape(nodes, width),
            shape(256, width + WIDE),
            shape(256, WIDE),
            shape(WIDE, nodes),
            shape(256, nodes),
        ],
        scratch_shapes=[
            pltpu.VMEM((nodes, WIDE), bf16),
            pltpu.VMEM((256, nodes), bf16),
            pltpu.VMEM((nodes, 512), bf16),
            pltpu.VMEM((512, WIDE), bf16),
            pltpu.VMEM((nodes, width), bf16),
            pltpu.SemaphoreType.DMA((2,)),
            pltpu.SemaphoreType.DMA((4,)),
            pltpu.SemaphoreType.DMA((width // COLS,)),
        ],
        compiler_params=params(20),
        cost_estimate=cost(nodes * width * (width // 2 + 3 * WIDE), 8 << 20),
        name="send_a",
    )(grid, low, pinned(turned_latent), pinned(slope), pinned(hidden), padded)


def keep_a(grid, turned_latent, hidden, grad_pre, turned_now, second):
    nodes, width = hidden.shape
    return pl.pallas_call(
        keep_a_kernel,
        in_specs=[smem, anywhere, anywhere] + [vmem] * 3,
        out_specs=[vmem] * 3,
        out_shape=[shape(256, width + WIDE), shape(256, nodes), shape(nodes, 512)],
        scratch_shapes=[pltpu.SemaphoreType.DMA, pltpu.SemaphoreType.DMA((4,))],
        compiler_params=params(12),
        cost_estimate=cost(nodes * width * width // 2, 4 << 20),
        name="keep_a",
    )(grid, pinned(turned_latent), pinned(hidden), grad_pre, turned_now, second)


def send_b(grid, turned_latent, grad_pre, flat, turned_now, hidden_now):
    nodes, width = grad_pre.shape
    return pl.pallas_call(
        send_b_kernel,
        in_specs=[smem, anywhere] + [vmem] * 4,
        out_specs=[vmem] * 3,
        out_shape=[shape(256, width + WIDE), shape(256, WIDE), shape(256, nodes)],
        scratch_shapes=[pltpu.VMEM((512, WIDE), bf16), pltpu.SemaphoreType.DMA],
        compiler_params=params(12),
        cost_estimate=cost(nodes * width * width // 2, 4 << 20),
        name="send_b",
    )(grid, pinned(turned_latent), grad_pre, flat, turned_now, hidden_now)


def keep_b(weight, grad_pre, turned_now, second):
    nodes, width = grad_pre.shape
    return pl.pallas_call(
        keep_b_kernel,
        in_specs=[anywhere] + [vmem] * 3,
        out_specs=[vmem] * 2,
        out_shape=[shape(256, width + WIDE), shape(width, width)],
        scratch_shapes=[pltpu.SemaphoreType.DMA],
        compiler_params=params(12),
        cost_estimate=cost(nodes * width * width // 2, 4 << 20),
        name="keep_b",
    )(pinned(weight), grad_pre, turned_now, second)


def latent_kernel(pre_ref, weight_ref, out_ref, result_ref, sems):
    nodes, width = pre_ref.shape
    stores = []
    for row in range(0, nodes, ROWS):
        rows = slice(row, row + ROWS)
        for start in range(0, width, COLS):
            columns = slice(start, start + COLS)
            result_ref[rows, columns] = lax.dot_general(
                pre_ref[rows, :], weight_ref[columns, :], NT, preferred_element_type=f32
            ).astype(bf16)
        store = pltpu.make_async_copy(
            result_ref.at[pl.ds(row, ROWS)], out_ref.at[pl.ds(row, ROWS)], sems.at[row // ROWS]
        )
        store.start()
        stores.append(store)
    for store in stores:
        store.wait()


def latent_gradient(grad_pre, weight):
    nodes, width = grad_pre.shape
    return pl.pallas_call(
        latent_kernel,
        in_specs=[vmem, vmem],
        out_specs=anywhere,
        out_shape=pltpu.HBM((nodes, width), bf16),
        scratch_shapes=[pltpu.VMEM((nodes, width), bf16), pltpu.SemaphoreType.DMA((nodes // ROWS,))],
        compiler_params=params(12),
        cost_estimate=cost(2 * nodes * width * width, 10 << 20),
        name="latent_gradient",
    )(grad_pre, weight)


def finish_kernel(own_ref, *refs, factor):
    *others, first_ref, second_ref = refs
    width, variables = first_ref.shape[1], second_ref.shape[1]
    total = own_ref[...].astype(f32)
    for other in others:
        total = total + other[...].astype(f32)
    total = total * factor
    first_ref[...] = total[:, :width]
    second_ref[...] = total[:, width : width + variables]


def finish(own, others, width, variables, factor):
    rows = own.shape[0]
    return pl.pallas_call(
        functools.partial(finish_kernel, factor=factor),
        in_specs=[vmem] * (1 + len(others)),
        out_specs=[vmem] * 2,
        out_shape=[jax.ShapeDtypeStruct((rows, width), f32), jax.ShapeDtypeStruct((rows, variables), f32)],
        compiler_params=params(8),
        cost_estimate=cost(0, 1 << 20),
        name="finish",
    )(own, *others)


def moved(value, move):
    moves = []
    for member in range(8):
        for grid in range(16):
            y, x_hi, x_lo, z, core = member // 2, member % 2, grid // 8, (grid // 2) % 4, grid % 2
            y, x, z, core = move(y, x_hi * 2 + x_lo, z, core)
            target = (y * 2 + x // 2) * 16 + ((x % 2) * 4 + z) * 2 + core
            moves.append((member * 16 + grid, target))
    return lax.ppermute(value, ("member", "grid"), moves)


def summed(own, others):
    total = own.astype(f32)
    for other in others:
        total = total + other.astype(f32)
    return total


def over_core(send, keep):
    got = moved(send, lambda y, x, z, c: (y, x, z, 1 - c))
    return summed(keep, [got]).reshape(2, 2, 64, send.shape[1])


def up(value):
    return moved(value, lambda y, x, z, c: (y, x, (z + 1) % 4, c))


def down(value):
    return moved(value, lambda y, x, z, c: (y, x, (z + 3) % 4, c))


def over_x(blocks):
    got = [
        moved(blocks[0] if k == 2 else blocks[1], lambda y, x, z, c, k=k: (y, x ^ k, z, c))
        for k in (1, 3, 2)
    ]
    return summed(blocks[0], got).astype(bf16)


def over_y(block):
    return [moved(block, lambda y, x, z, c, k=k: (y ^ k, x, z, c)) for k in (1, 3, 2)]


def body(latents, hidden_weight, output_weight, observed, node_area_weight):
    latent = latents[0]
    members = lax.axis_size("member")
    groups = lax.axis_size("grid")
    nodes, width = latent.shape
    variables = output_weight.shape[1]
    place = lax.axis_index("member").astype(jnp.int32).reshape(1)
    grid = lax.axis_index("grid").astype(jnp.int32).reshape(1)

    forecast, hidden, slope, padded = forward(latent, hidden_weight, output_weight.T)
    blocks, late_grid = lax.optimization_barrier(((0.25 * forecast).astype(f16), grid))
    blocks = lax.all_to_all(blocks, "member", 0, 0, tiled=True)
    turned_latent = turned(late_grid, latent)
    low = pairs(place, 4.0 * blocks.astype(f32), observed, node_area_weight.reshape(1, nodes))
    low = lax.all_to_all(low, "member", 0, 0, tiled=True)
    grad_pre, rows_a, second_a, flat, turned_now = send_a(grid, low, turned_latent, slope, hidden, padded)
    kept_a, turned_now, hidden_now = keep_a(grid, turned_latent, hidden, grad_pre, turned_now, second_a)
    far, own = over_core(rows_a, kept_a).astype(bf16)
    far, own, flat = lax.optimization_barrier((far, own, flat))
    upward, downward = up(far[0]), down(far[1])
    rows_b, second_b, turned_now = send_b(grid, turned_latent, grad_pre, flat, turned_now, hidden_now)
    kept_b, weight_copy = keep_b(hidden_weight, grad_pre, turned_now, second_b)
    above, below = over_core(rows_b, kept_b)
    above = jnp.stack([above[0] + upward.astype(f32), above[1]]).astype(bf16)
    below = jnp.stack([below[0], below[1] + downward.astype(f32)]).astype(bf16)
    above, below, grad_pre = lax.optimization_barrier((above, below, grad_pre))
    grad_latent = latent_gradient(grad_pre, weight_copy)
    blocks = summed(own, [up(above), down(below)]).astype(bf16)
    blocks, grad_latent = lax.optimization_barrier((blocks, grad_latent))
    block = over_x(blocks)
    factor = 1.0 / math.sqrt(members * nodes * groups)
    first, second = finish(block, over_y(block), width, variables, factor)
    return grad_latent[None], first, second


def solution(mesh):
    in_specs = (P("member", "grid", None), P(), P(), P(None, "grid"), P("grid"))
    out_specs = (P("member", "grid", None), P("grid", None), P("grid", None))
    return jax.shard_map(body, mesh=mesh, in_specs=in_specs, out_specs=out_specs, check_vma=False)
```

```python
import functools
import math

import jax
import jax.numpy as jnp
from jax import lax
from jax.experimental import pallas as pl
from jax.experimental.pallas import tpu as pltpu
from jax.sharding import PartitionSpec as P

smooth_sq = 0.0025
bf16 = jnp.bfloat16
f16 = jnp.float16
f32 = jnp.float32

NT = (((1,), (1,)), ((), ()))
WIDE = 128
TALL = 112
SHARE = 256
ROWS = 512
COLS = 256

vmem = pl.BlockSpec(memory_space=pltpu.VMEM)
smem = pl.BlockSpec(memory_space=pltpu.SMEM)
anywhere = pl.BlockSpec(memory_space=pltpu.HBM)


def params(mib):
    return pltpu.CompilerParams(vmem_limit_bytes=mib * 1024 * 1024)


def cost(flops, nbytes, trans=0):
    return pl.CostEstimate(flops=flops, bytes_accessed=nbytes, transcendentals=trans)


def chunk(ref, start):
    return ref.at[pl.ds(start, ROWS)]


def forward_kernel(
    latent_ref,
    weight_ref,
    out_weight_ref,
    forecast_ref,
    pre_out,
    padded_ref,
    pre_ref,
    hidden_ref,
    latent_copy,
    weight_copy,
    out_weight_copy,
    latent_sems,
    weight_sem,
    out_weight_sem,
    pre_sems,
):
    nodes, width = latent_ref.shape
    variables = out_weight_ref.shape[0]
    weight_load = pltpu.make_async_copy(weight_ref, weight_copy, weight_sem)
    out_weight_load = pltpu.make_async_copy(out_weight_ref, out_weight_copy, out_weight_sem)
    latent_loads = [
        pltpu.make_async_copy(chunk(latent_ref, start), chunk(latent_copy, start), latent_sems.at[start // ROWS])
        for start in range(0, nodes, ROWS)
    ]
    out_weight_load.start()
    weight_load.start()
    for load in latent_loads:
        load.start()
    out_weight_load.wait()
    turned_weight = jnp.concatenate(
        [out_weight_copy[...], jnp.zeros((WIDE - variables, width), bf16)], axis=0
    )
    padded_ref[...] = turned_weight.T
    weight_load.wait()
    stores = []
    for start in range(0, nodes, ROWS):
        rows = slice(start, start + ROWS)
        latent_loads[start // ROWS].wait()
        pre = jnp.dot(latent_copy[rows, :], weight_copy[...], preferred_element_type=f32)
        pre_ref[rows, :] = pre.astype(bf16)
        hidden_ref[rows, :] = (pre * (0.5 * jnp.tanh(0.5 * pre) + 0.5)).astype(bf16)
        store = pltpu.make_async_copy(chunk(pre_ref, start), chunk(pre_out, start), pre_sems.at[start // ROWS])
        store.start()
        stores.append(store)
        for share in range(start // SHARE, (start + ROWS) // SHARE):
            forecast_ref[share] = lax.dot_general(
                turned_weight[:TALL],
                hidden_ref[share * SHARE : (share + 1) * SHARE, :],
                NT,
                preferred_element_type=f32,
            )
    for store in stores:
        store.wait()


def pinned(value):
    return pltpu.with_memory_space_constraint(value, pltpu.HBM)


def forward(latent, weight, out_weight):
    nodes, width = latent.shape
    return pl.pallas_call(
        forward_kernel,
        in_specs=[anywhere] * 3,
        out_specs=[vmem, anywhere, vmem],
        out_shape=[
            jax.ShapeDtypeStruct((nodes // SHARE, TALL, SHARE), f32),
            pltpu.HBM((nodes, width), bf16),
            jax.ShapeDtypeStruct((width, WIDE), bf16),
        ],
        scratch_shapes=[
            pltpu.VMEM((nodes, width), bf16),
            pltpu.VMEM((nodes, width), bf16),
            pltpu.VMEM((nodes, width), bf16),
            pltpu.VMEM((width, width), bf16),
            pltpu.VMEM(out_weight.shape, bf16),
            pltpu.SemaphoreType.DMA((nodes // ROWS,)),
            pltpu.SemaphoreType.DMA,
            pltpu.SemaphoreType.DMA,
            pltpu.SemaphoreType.DMA((nodes // ROWS,)),
        ],
        compiler_params=params(32),
        cost_estimate=cost(2 * nodes * width * (width + WIDE), 20 << 20),
        name="forward",
    )(pinned(latent), pinned(weight), pinned(out_weight))


def gate_kernel(pre_hbm, hidden_out, slope_out, pre_ref, hidden_ref, slope_ref, pre_sems, hidden_sems, slope_sems):
    nodes, width = pre_hbm.shape
    loads = [
        pltpu.make_async_copy(chunk(pre_hbm, start), chunk(pre_ref, start), pre_sems.at[start // ROWS])
        for start in range(0, nodes, ROWS)
    ]
    for load in loads:
        load.start()
    stores = []
    for start in range(0, nodes, ROWS):
        rows = slice(start, start + ROWS)
        loads[start // ROWS].wait()
        for group in range(width // 128):
            columns = slice(group * 128, (group + 1) * 128)
            pre = pre_ref[rows, columns].astype(f32)
            sig = 0.5 * jnp.tanh(0.5 * pre) + 0.5
            hidden = pre * sig
            hidden_ref[group, rows, :] = hidden.astype(bf16)
            slope_ref[rows, columns] = (sig + hidden * (1.0 - sig)).astype(bf16)
        for store in (
            pltpu.make_async_copy(
                hidden_ref.at[:, pl.ds(start, ROWS)], hidden_out.at[:, pl.ds(start, ROWS)], hidden_sems.at[start // ROWS]
            ),
            pltpu.make_async_copy(chunk(slope_ref, start), chunk(slope_out, start), slope_sems.at[start // ROWS]),
        ):
            store.start()
            stores.append(store)
    for store in stores:
        store.wait()


def gates(pre):
    nodes, width = pre.shape
    sems = pltpu.SemaphoreType.DMA((nodes // ROWS,))
    return pl.pallas_call(
        gate_kernel,
        in_specs=[anywhere],
        out_specs=[anywhere] * 2,
        out_shape=[pltpu.HBM((width // 128, nodes, 128), bf16), pltpu.HBM((nodes, width), bf16)],
        scratch_shapes=[
            pltpu.VMEM((nodes, width), bf16),
            pltpu.VMEM((width // 128, nodes, 128), bf16),
            pltpu.VMEM((nodes, width), bf16),
            sems,
            sems,
            sems,
        ],
        compiler_params=params(20),
        cost_estimate=cost(0, 12 << 20),
        name="gates",
    )(pinned(pre))


def slope_function(diff):
    return diff * lax.rsqrt(diff * diff + smooth_sq)


def pair_kernel(place_ref, blocks_ref, observed_ref, area_ref, low_ref, here_ref, weight_ref, totals_ref, sems):
    members = blocks_ref.shape[0]
    variables = observed_ref.shape[0]
    at = pl.multiple_of(place_ref[0] * SHARE, SHARE)
    loads = [
        pltpu.make_async_copy(observed_ref.at[:, pl.ds(at, SHARE)], here_ref, sems.at[0]),
        pltpu.make_async_copy(area_ref.at[:, pl.ds(at, SHARE)], weight_ref, sems.at[1]),
    ]
    for load in loads:
        load.start()
    for start in range(0, TALL, 16):
        rows = slice(start, start + 16)
        values = [blocks_ref[a, rows, :] for a in range(members)]
        totals = [0.0] * members
        for a in range(members):
            for b in range(a + 1, members):
                slope = slope_function(values[a] - values[b])
                totals[a] = totals[a] + slope
                totals[b] = totals[b] - slope
        for a in range(members):
            totals_ref[a, rows, :] = totals[a]
    for load in loads:
        load.wait()
    area = weight_ref[...]
    for start in range(0, TALL, 16):
        rows = slice(start, start + 16)
        real = min(16, variables - start)
        observed = here_ref[start : start + real, :]
        if real < 16:
            observed = jnp.concatenate([observed, jnp.zeros((16 - real, SHARE), f32)], axis=0)
        for a in range(members):
            own = slope_function(blocks_ref[a, rows, :] - observed)
            low_ref[a, rows, :] = (area * (own - totals_ref[a, rows, :] * (1.0 / (members - 1)))).astype(bf16)


def pairs(place, blocks, observed, area):
    members = blocks.shape[0]
    variables = observed.shape[0]
    return pl.pallas_call(
        pair_kernel,
        in_specs=[smem, vmem, anywhere, anywhere],
        out_specs=vmem,
        out_shape=jax.ShapeDtypeStruct((members, TALL, SHARE), bf16),
        scratch_shapes=[
            pltpu.VMEM((variables, SHARE), f32),
            pltpu.VMEM((1, SHARE), f32),
            pltpu.VMEM((members, TALL, SHARE), f32),
            pltpu.SemaphoreType.DMA((2,)),
        ],
        compiler_params=params(8),
        cost_estimate=cost(4 << 20, 2 << 20),
        name="pairs",
    )(place, blocks, observed, area)


def position(grid_ref):
    grid = grid_ref[0]
    return grid >> 3, (grid >> 1) & 3, grid & 1


STEPS = ((2, 0), (1, 3))


def owner(block, steps, x_lo, z):
    return ((block & 1) ^ x_lo) * 4 + ((z + steps[block >> 1]) & 3)


def turn_kernel(grid_ref, latent_ref, turned_ref):
    nodes, width = latent_ref.shape
    x_lo, z, core = position(grid_ref)
    for group in range(8):
        step = (group - z) & 3
        odd = step & 1
        place = odd * (2 + (step >> 1)) + (1 - odd) * (1 - (step >> 1))
        at = (place >> 1) * 512 + (place & 1) * 128 + ((group >> 2) ^ x_lo) * 64
        first = pl.multiple_of(at + (1 - core) * 256, 64)
        second = pl.multiple_of(at + core * 256, 64)
        for row in range(0, nodes, ROWS):
            columns = slice(row, row + ROWS)
            block = latent_ref[columns, group * 128 : (group + 1) * 128].T
            turned_ref[pl.ds(first, 64), columns] = block[:64]
            turned_ref[pl.ds(second, 64), columns] = block[64:]


def turned(grid, latent):
    nodes, width = latent.shape
    return pl.pallas_call(
        turn_kernel,
        in_specs=[smem, vmem],
        out_specs=vmem,
        out_shape=jax.ShapeDtypeStruct((width, nodes), bf16),
        compiler_params=params(8),
        cost_estimate=cost(0, 8 << 20),
        name="turned",
    )(grid, latent)


def turned_load(turned_hbm, start, turned_ref, sem):
    return pltpu.make_async_copy(turned_hbm.at[pl.ds(start, 256)], turned_ref, sem)


def hidden_loads(part, grid_ref, hidden_hbm, hidden_ref, sems):
    x_lo, z, core = position(grid_ref)
    return [
        pltpu.make_async_copy(
            hidden_hbm.at[owner(block, STEPS[part], x_lo, z)],
            hidden_ref.at[block],
            sems.at[block],
        )
        for block in range(4)
    ]


def first_product(turned_ref, pre_ref, out_ref):
    width = pre_ref.shape[1]
    for column in range(0, width, 512):
        columns = slice(column, column + 512)
        part = jnp.dot(turned_ref[...], pre_ref[:, columns], preferred_element_type=f32)
        out_ref[:, columns] = part.astype(bf16)


def second_product(grid_ref, flat_ref, hidden_ref, send_ref, second_ref, scratch_ref):
    width = send_ref.shape[1] - WIDE
    core = position(grid_ref)[2]
    for block in (0, 2):
        columns = jnp.concatenate([hidden_ref[block], hidden_ref[block + 1]], axis=1)
        second = jnp.dot(flat_ref[...], columns, preferred_element_type=f32)
        scratch_ref[block * 128 : (block + 2) * 128, :] = second.T.astype(bf16)
    for block in range(4):
        rows = slice(block * 64, (block + 1) * 64)
        mine = pl.multiple_of(block * 128 + core * 64, 64)
        other = pl.multiple_of(block * 128 + (1 - core) * 64, 64)
        second_ref[rows, :] = scratch_ref[pl.ds(mine, 64), :]
        send_ref[rows, width:] = scratch_ref[pl.ds(other, 64), :]


def send_a_kernel(
    grid_ref,
    low_ref,
    turned_hbm,
    slope_hbm,
    hidden_hbm,
    padded_ref,
    pre_ref,
    send_ref,
    second_ref,
    flat_ref,
    next_turned_ref,
    turn_ref,
    turned_ref,
    hidden_ref,
    scratch_ref,
    slope_ref,
    turned_sems,
    hidden_sems,
    slope_sems,
):
    nodes, width = pre_ref.shape
    slope_loads = [
        pltpu.make_async_copy(
            slope_hbm.at[pl.ds(start, ROWS)], slope_ref.at[pl.ds(start, ROWS)], slope_sems.at[start // ROWS]
        )
        for start in range(0, nodes, ROWS)
    ]
    turned_now = turned_load(turned_hbm, 0, turned_ref, turned_sems.at[0])
    turned_next = turned_load(turned_hbm, 256, next_turned_ref, turned_sems.at[1])
    hidden_now = hidden_loads(0, grid_ref, hidden_hbm, hidden_ref, hidden_sems)
    for load in slope_loads + [turned_now] + hidden_now + [turned_next]:
        load.start()
    for share in range(low_ref.shape[0]):
        columns = slice(share * SHARE, (share + 1) * SHARE)
        low = jnp.concatenate([low_ref[share], jnp.zeros((WIDE - TALL, SHARE), bf16)], axis=0)
        flat_ref[:, columns] = low
        turn_ref[columns, :] = low.T
    for start in range(0, nodes, ROWS):
        rows = slice(start, start + ROWS)
        slope_loads[start // ROWS].wait()
        for column in range(0, width, COLS):
            columns = slice(column, column + COLS)
            grad_hidden = lax.dot_general(turn_ref[rows, :], padded_ref[columns, :], NT, preferred_element_type=f32)
            pre_ref[rows, columns] = (grad_hidden * slope_ref[rows, columns].astype(f32)).astype(bf16)
    turned_now.wait()
    first_product(turned_ref, pre_ref, send_ref)
    for load in hidden_now:
        load.wait()
    second_product(grid_ref, flat_ref, hidden_ref, send_ref, second_ref, scratch_ref)
    turned_next.wait()


def keep_a_kernel(
    grid_ref,
    turned_hbm,
    hidden_hbm,
    pre_ref,
    turned_ref,
    second_ref,
    keep_ref,
    next_turned_ref,
    next_hidden_ref,
    turned_sem,
    hidden_sems,
):
    loads = [turned_load(turned_hbm, 512, next_turned_ref, turned_sem)]
    loads += hidden_loads(1, grid_ref, hidden_hbm, next_hidden_ref, hidden_sems)
    for load in loads:
        load.start()
    first_product(turned_ref, pre_ref, keep_ref)
    keep_ref[:, pre_ref.shape[1] :] = second_ref[...]
    for load in loads:
        load.wait()


def send_b_kernel(
    grid_ref,
    turned_hbm,
    pre_ref,
    flat_ref,
    turned_ref,
    hidden_ref,
    send_ref,
    second_ref,
    next_turned_ref,
    scratch_ref,
    turned_sem,
):
    load = turned_load(turned_hbm, 768, next_turned_ref, turned_sem)
    load.start()
    first_product(turned_ref, pre_ref, send_ref)
    second_product(grid_ref, flat_ref, hidden_ref, send_ref, second_ref, scratch_ref)
    load.wait()


def keep_b_kernel(weight_hbm, pre_ref, turned_ref, second_ref, keep_ref, weight_ref, weight_sem):
    load = pltpu.make_async_copy(weight_hbm, weight_ref, weight_sem)
    load.start()
    first_product(turned_ref, pre_ref, keep_ref)
    keep_ref[:, pre_ref.shape[1] :] = second_ref[...]
    load.wait()


def shape(*dims):
    return jax.ShapeDtypeStruct(dims, bf16)


def send_a(grid, low, turned_latent, slope, hidden, padded):
    nodes, width = slope.shape
    return pl.pallas_call(
        send_a_kernel,
        in_specs=[smem, vmem, anywhere, anywhere, anywhere, vmem],
        out_specs=[vmem] * 5,
        out_shape=[
            shape(nodes, width),
            shape(256, width + WIDE),
            shape(256, WIDE),
            shape(WIDE, nodes),
            shape(256, nodes),
        ],
        scratch_shapes=[
            pltpu.VMEM((nodes, WIDE), bf16),
            pltpu.VMEM((256, nodes), bf16),
            pltpu.VMEM((4, nodes, 128), bf16),
            pltpu.VMEM((512, WIDE), bf16),
            pltpu.VMEM((nodes, width), bf16),
            pltpu.SemaphoreType.DMA((2,)),
            pltpu.SemaphoreType.DMA((4,)),
            pltpu.SemaphoreType.DMA((nodes // ROWS,)),
        ],
        compiler_params=params(20),
        cost_estimate=cost(nodes * width * (width // 2 + 3 * WIDE), 8 << 20),
        name="send_a",
    )(grid, low, pinned(turned_latent), pinned(slope), pinned(hidden), padded)


def keep_a(grid, turned_latent, hidden, grad_pre, turned_now, second):
    nodes, width = grad_pre.shape
    return pl.pallas_call(
        keep_a_kernel,
        in_specs=[smem, anywhere, anywhere] + [vmem] * 3,
        out_specs=[vmem] * 3,
        out_shape=[shape(256, width + WIDE), shape(256, nodes), shape(4, nodes, 128)],
        scratch_shapes=[pltpu.SemaphoreType.DMA, pltpu.SemaphoreType.DMA((4,))],
        compiler_params=params(12),
        cost_estimate=cost(nodes * width * width // 2, 4 << 20),
        name="keep_a",
    )(grid, pinned(turned_latent), pinned(hidden), grad_pre, turned_now, second)


def send_b(grid, turned_latent, grad_pre, flat, turned_now, hidden_now):
    nodes, width = grad_pre.shape
    return pl.pallas_call(
        send_b_kernel,
        in_specs=[smem, anywhere] + [vmem] * 4,
        out_specs=[vmem] * 3,
        out_shape=[shape(256, width + WIDE), shape(256, WIDE), shape(256, nodes)],
        scratch_shapes=[pltpu.VMEM((512, WIDE), bf16), pltpu.SemaphoreType.DMA],
        compiler_params=params(12),
        cost_estimate=cost(nodes * width * width // 2, 4 << 20),
        name="send_b",
    )(grid, pinned(turned_latent), grad_pre, flat, turned_now, hidden_now)


def keep_b(weight, grad_pre, turned_now, second):
    nodes, width = grad_pre.shape
    return pl.pallas_call(
        keep_b_kernel,
        in_specs=[anywhere] + [vmem] * 3,
        out_specs=[vmem] * 2,
        out_shape=[shape(256, width + WIDE), shape(width, width)],
        scratch_shapes=[pltpu.SemaphoreType.DMA],
        compiler_params=params(12),
        cost_estimate=cost(nodes * width * width // 2, 4 << 20),
        name="keep_b",
    )(pinned(weight), grad_pre, turned_now, second)


def latent_kernel(pre_ref, weight_ref, out_ref, result_ref, sems):
    nodes, width = pre_ref.shape
    stores = []
    for row in range(0, nodes, ROWS):
        rows = slice(row, row + ROWS)
        for start in range(0, width, COLS):
            columns = slice(start, start + COLS)
            result_ref[rows, columns] = lax.dot_general(
                pre_ref[rows, :], weight_ref[columns, :], NT, preferred_element_type=f32
            ).astype(bf16)
        store = pltpu.make_async_copy(
            result_ref.at[pl.ds(row, ROWS)], out_ref.at[pl.ds(row, ROWS)], sems.at[row // ROWS]
        )
        store.start()
        stores.append(store)
    for store in stores:
        store.wait()


def latent_gradient(grad_pre, weight):
    nodes, width = grad_pre.shape
    return pl.pallas_call(
        latent_kernel,
        in_specs=[vmem, vmem],
        out_specs=anywhere,
        out_shape=pltpu.HBM((nodes, width), bf16),
        scratch_shapes=[pltpu.VMEM((nodes, width), bf16), pltpu.SemaphoreType.DMA((nodes // ROWS,))],
        compiler_params=params(12),
        cost_estimate=cost(2 * nodes * width * width, 10 << 20),
        name="latent_gradient",
    )(grad_pre, weight)


def finish_kernel(own_ref, *refs, factor):
    *others, first_ref, second_ref = refs
    width, variables = first_ref.shape[1], second_ref.shape[1]
    total = own_ref[...].astype(f32)
    for other in others:
        total = total + other[...].astype(f32)
    total = total * factor
    first_ref[...] = total[:, :width]
    second_ref[...] = total[:, width : width + variables]


def finish(own, others, width, variables, factor):
    rows = own.shape[0]
    return pl.pallas_call(
        functools.partial(finish_kernel, factor=factor),
        in_specs=[vmem] * (1 + len(others)),
        out_specs=[vmem] * 2,
        out_shape=[jax.ShapeDtypeStruct((rows, width), f32), jax.ShapeDtypeStruct((rows, variables), f32)],
        compiler_params=params(8),
        cost_estimate=cost(0, 1 << 20),
        name="finish",
    )(own, *others)


def moved(value, move):
    moves = []
    for member in range(8):
        for grid in range(16):
            y, x_hi, x_lo, z, core = member // 2, member % 2, grid // 8, (grid // 2) % 4, grid % 2
            y, x, z, core = move(y, x_hi * 2 + x_lo, z, core)
            target = (y * 2 + x // 2) * 16 + ((x % 2) * 4 + z) * 2 + core
            moves.append((member * 16 + grid, target))
    return lax.ppermute(value, ("member", "grid"), moves)


def summed(own, others):
    total = own.astype(f32)
    for other in others:
        total = total + other.astype(f32)
    return total


def over_core(send, keep):
    got = moved(send, lambda y, x, z, c: (y, x, z, 1 - c))
    return summed(keep, [got]).reshape(2, 2, 64, send.shape[1])


def up(value):
    return moved(value, lambda y, x, z, c: (y, x, (z + 1) % 4, c))


def down(value):
    return moved(value, lambda y, x, z, c: (y, x, (z + 3) % 4, c))


def over_x(blocks):
    got = [
        moved(blocks[0] if k == 2 else blocks[1], lambda y, x, z, c, k=k: (y, x ^ k, z, c))
        for k in (1, 3, 2)
    ]
    return summed(blocks[0], got).astype(bf16)


def over_y(block):
    return [moved(block, lambda y, x, z, c, k=k: (y ^ k, x, z, c)) for k in (1, 3, 2)]


def body(latents, hidden_weight, output_weight, observed, node_area_weight):
    latent = latents[0]
    members = lax.axis_size("member")
    groups = lax.axis_size("grid")
    nodes, width = latent.shape
    variables = output_weight.shape[1]
    place = lax.axis_index("member").astype(jnp.int32).reshape(1)
    grid = lax.axis_index("grid").astype(jnp.int32).reshape(1)

    forecast, pre, padded = forward(latent, hidden_weight, output_weight.T)
    blocks, pre = lax.optimization_barrier(((0.25 * forecast).astype(f16), pre))
    blocks = lax.all_to_all(blocks, "member", 0, 0, tiled=True)
    hidden, slope = gates(pre)
    blocks, hidden, slope = lax.optimization_barrier((blocks, hidden, slope))
    low = pairs(place, 4.0 * blocks.astype(f32), observed, node_area_weight.reshape(1, nodes))
    low, late_grid = lax.optimization_barrier((low, grid))
    low = lax.all_to_all(low, "member", 0, 0, tiled=True)
    turned_latent = turned(late_grid, latent)
    grad_pre, rows_a, second_a, flat, turned_now = send_a(grid, low, turned_latent, slope, hidden, padded)
    kept_a, turned_now, hidden_now = keep_a(grid, turned_latent, hidden, grad_pre, turned_now, second_a)
    far, own = over_core(rows_a, kept_a).astype(bf16)
    far, own, flat = lax.optimization_barrier((far, own, flat))
    upward, downward = up(far[0]), down(far[1])
    rows_b, second_b, turned_now = send_b(grid, turned_latent, grad_pre, flat, turned_now, hidden_now)
    kept_b, weight_copy = keep_b(hidden_weight, grad_pre, turned_now, second_b)
    above, below = over_core(rows_b, kept_b)
    above = jnp.stack([above[0] + upward.astype(f32), above[1]]).astype(bf16)
    below = jnp.stack([below[0], below[1] + downward.astype(f32)]).astype(bf16)
    above, below, grad_pre = lax.optimization_barrier((above, below, grad_pre))
    grad_latent = latent_gradient(grad_pre, weight_copy)
    blocks = summed(own, [up(above), down(below)]).astype(bf16)
    blocks, grad_latent = lax.optimization_barrier((blocks, grad_latent))
    block = over_x(blocks)
    factor = 1.0 / math.sqrt(members * nodes * groups)
    first, second = finish(block, over_y(block), width, variables, factor)
    return grad_latent[None], first, second


def solution(mesh):
    in_specs = (P("member", "grid", None), P(), P(), P(None, "grid"), P("grid"))
    out_specs = (P("member", "grid", None), P("grid", None), P("grid", None))
    return jax.shard_map(body, mesh=mesh, in_specs=in_specs, out_specs=out_specs, check_vma=False)
```

```python
import functools
import math

import jax
import jax.numpy as jnp
from jax import lax
from jax.experimental import pallas as pl
from jax.experimental.pallas import tpu as pltpu
from jax.sharding import PartitionSpec as P

smooth_sq = 0.0025
bf16 = jnp.bfloat16
f16 = jnp.float16
f32 = jnp.float32

NT = (((1,), (1,)), ((), ()))
WIDE = 128
TALL = 112
SHARE = 256
ROWS = 512
COLS = 256

vmem = pl.BlockSpec(memory_space=pltpu.VMEM)
smem = pl.BlockSpec(memory_space=pltpu.SMEM)
anywhere = pl.BlockSpec(memory_space=pltpu.HBM)


def params(mib):
    return pltpu.CompilerParams(vmem_limit_bytes=mib * 1024 * 1024)


def cost(flops, nbytes, trans=0):
    return pl.CostEstimate(flops=flops, bytes_accessed=nbytes, transcendentals=trans)


def chunk(ref, start):
    return ref.at[pl.ds(start, ROWS)]


def forward_kernel(
    latent_ref,
    weight_ref,
    out_weight_ref,
    forecast_ref,
    pre_out,
    padded_ref,
    pre_ref,
    hidden_ref,
    latent_copy,
    weight_copy,
    out_weight_copy,
    latent_sems,
    weight_sem,
    out_weight_sem,
    pre_sems,
):
    nodes, width = latent_ref.shape
    variables = out_weight_ref.shape[0]
    weight_load = pltpu.make_async_copy(weight_ref, weight_copy, weight_sem)
    out_weight_load = pltpu.make_async_copy(out_weight_ref, out_weight_copy, out_weight_sem)
    latent_loads = [
        pltpu.make_async_copy(chunk(latent_ref, start), chunk(latent_copy, start), latent_sems.at[start // ROWS])
        for start in range(0, nodes, ROWS)
    ]
    out_weight_load.start()
    weight_load.start()
    for load in latent_loads:
        load.start()
    out_weight_load.wait()
    turned_weight = jnp.concatenate(
        [out_weight_copy[...], jnp.zeros((WIDE - variables, width), bf16)], axis=0
    )
    padded_ref[...] = turned_weight.T
    weight_load.wait()
    stores = []
    for start in range(0, nodes, ROWS):
        rows = slice(start, start + ROWS)
        latent_loads[start // ROWS].wait()
        pre = jnp.dot(latent_copy[rows, :], weight_copy[...], preferred_element_type=f32)
        pre_ref[rows, :] = pre.astype(bf16)
        hidden_ref[rows, :] = (pre * (0.5 * jnp.tanh(0.5 * pre) + 0.5)).astype(bf16)
        store = pltpu.make_async_copy(chunk(pre_ref, start), chunk(pre_out, start), pre_sems.at[start // ROWS])
        store.start()
        stores.append(store)
        for share in range(start // SHARE, (start + ROWS) // SHARE):
            forecast_ref[share] = lax.dot_general(
                turned_weight[:TALL],
                hidden_ref[share * SHARE : (share + 1) * SHARE, :],
                NT,
                preferred_element_type=f32,
            )
    for store in stores:
        store.wait()


def pinned(value):
    return pltpu.with_memory_space_constraint(value, pltpu.HBM)


def forward(latent, weight, out_weight):
    nodes, width = latent.shape
    return pl.pallas_call(
        forward_kernel,
        in_specs=[anywhere] * 3,
        out_specs=[vmem, anywhere, vmem],
        out_shape=[
            jax.ShapeDtypeStruct((nodes // SHARE, TALL, SHARE), f32),
            pltpu.HBM((nodes, width), bf16),
            jax.ShapeDtypeStruct((width, WIDE), bf16),
        ],
        scratch_shapes=[
            pltpu.VMEM((nodes, width), bf16),
            pltpu.VMEM((nodes, width), bf16),
            pltpu.VMEM((nodes, width), bf16),
            pltpu.VMEM((width, width), bf16),
            pltpu.VMEM(out_weight.shape, bf16),
            pltpu.SemaphoreType.DMA((nodes // ROWS,)),
            pltpu.SemaphoreType.DMA,
            pltpu.SemaphoreType.DMA,
            pltpu.SemaphoreType.DMA((nodes // ROWS,)),
        ],
        compiler_params=params(32),
        cost_estimate=cost(2 * nodes * width * (width + WIDE), 20 << 20),
        name="forward",
    )(pinned(latent), pinned(weight), pinned(out_weight))


def gate_kernel(pre_hbm, hidden_out, slope_out, pre_ref, hidden_ref, slope_ref, pre_sems, hidden_sems, slope_sems):
    nodes, width = pre_hbm.shape
    loads = [
        pltpu.make_async_copy(chunk(pre_hbm, start), chunk(pre_ref, start), pre_sems.at[start // ROWS])
        for start in range(0, nodes, ROWS)
    ]
    for load in loads:
        load.start()
    stores = []
    for start in range(0, nodes, ROWS):
        rows = slice(start, start + ROWS)
        loads[start // ROWS].wait()
        for group in range(width // 128):
            columns = slice(group * 128, (group + 1) * 128)
            pre = pre_ref[rows, columns].astype(f32)
            sig = 0.5 * jnp.tanh(0.5 * pre) + 0.5
            hidden = pre * sig
            hidden_ref[group, rows, :] = hidden.astype(bf16)
            slope_ref[rows, columns] = (sig + hidden * (1.0 - sig)).astype(bf16)
        for store in (
            pltpu.make_async_copy(
                hidden_ref.at[:, pl.ds(start, ROWS)], hidden_out.at[:, pl.ds(start, ROWS)], hidden_sems.at[start // ROWS]
            ),
            pltpu.make_async_copy(chunk(slope_ref, start), chunk(slope_out, start), slope_sems.at[start // ROWS]),
        ):
            store.start()
            stores.append(store)
    for store in stores:
        store.wait()


def gates(pre):
    nodes, width = pre.shape
    sems = pltpu.SemaphoreType.DMA((nodes // ROWS,))
    return pl.pallas_call(
        gate_kernel,
        in_specs=[anywhere],
        out_specs=[anywhere] * 2,
        out_shape=[pltpu.HBM((width // 128, nodes, 128), bf16), pltpu.HBM((nodes, width), bf16)],
        scratch_shapes=[
            pltpu.VMEM((nodes, width), bf16),
            pltpu.VMEM((width // 128, nodes, 128), bf16),
            pltpu.VMEM((nodes, width), bf16),
            sems,
            sems,
            sems,
        ],
        compiler_params=params(20),
        cost_estimate=cost(0, 12 << 20),
        name="gates",
    )(pinned(pre))


def slope_function(diff):
    return diff * lax.rsqrt(diff * diff + smooth_sq)


def pair_kernel(place_ref, blocks_ref, observed_ref, area_ref, low_ref, here_ref, weight_ref, totals_ref, sems):
    members = blocks_ref.shape[0]
    variables = observed_ref.shape[0]
    at = pl.multiple_of(place_ref[0] * SHARE, SHARE)
    loads = [
        pltpu.make_async_copy(observed_ref.at[:, pl.ds(at, SHARE)], here_ref, sems.at[0]),
        pltpu.make_async_copy(area_ref.at[:, pl.ds(at, SHARE)], weight_ref, sems.at[1]),
    ]
    for load in loads:
        load.start()
    for start in range(0, TALL, 16):
        rows = slice(start, start + 16)
        values = [blocks_ref[a, rows, :] for a in range(members)]
        totals = [0.0] * members
        for a in range(members):
            for b in range(a + 1, members):
                slope = slope_function(values[a] - values[b])
                totals[a] = totals[a] + slope
                totals[b] = totals[b] - slope
        for a in range(members):
            totals_ref[a, rows, :] = totals[a]
    for load in loads:
        load.wait()
    area = weight_ref[...]
    for start in range(0, TALL, 16):
        rows = slice(start, start + 16)
        real = min(16, variables - start)
        observed = here_ref[start : start + real, :]
        if real < 16:
            observed = jnp.concatenate([observed, jnp.zeros((16 - real, SHARE), f32)], axis=0)
        for a in range(members):
            own = slope_function(blocks_ref[a, rows, :] - observed)
            low_ref[a, rows, :] = (area * (own - totals_ref[a, rows, :] * (1.0 / (members - 1)))).astype(bf16)


def pairs(place, blocks, observed, area):
    members = blocks.shape[0]
    variables = observed.shape[0]
    return pl.pallas_call(
        pair_kernel,
        in_specs=[smem, vmem, anywhere, anywhere],
        out_specs=vmem,
        out_shape=jax.ShapeDtypeStruct((members, TALL, SHARE), bf16),
        scratch_shapes=[
            pltpu.VMEM((variables, SHARE), f32),
            pltpu.VMEM((1, SHARE), f32),
            pltpu.VMEM((members, TALL, SHARE), f32),
            pltpu.SemaphoreType.DMA((2,)),
        ],
        compiler_params=params(8),
        cost_estimate=cost(4 << 20, 2 << 20),
        name="pairs",
    )(place, blocks, observed, area)


def position(grid_ref):
    grid = grid_ref[0]
    return grid >> 3, (grid >> 1) & 3, grid & 1


STEPS = ((2, 0), (1, 3))


def owner(block, steps, x_lo, z):
    return ((block & 1) ^ x_lo) * 4 + ((z + steps[block >> 1]) & 3)


def turn_kernel(grid_ref, latent_ref, turned_ref):
    nodes, width = latent_ref.shape
    x_lo, z, core = position(grid_ref)
    for group in range(8):
        step = (group - z) & 3
        odd = step & 1
        place = odd * (2 + (step >> 1)) + (1 - odd) * (1 - (step >> 1))
        at = (place >> 1) * 512 + (place & 1) * 128 + ((group >> 2) ^ x_lo) * 64
        first = pl.multiple_of(at + (1 - core) * 256, 64)
        second = pl.multiple_of(at + core * 256, 64)
        for row in range(0, nodes, ROWS):
            columns = slice(row, row + ROWS)
            block = latent_ref[columns, group * 128 : (group + 1) * 128].T
            turned_ref[pl.ds(first, 64), columns] = block[:64]
            turned_ref[pl.ds(second, 64), columns] = block[64:]


def turned(grid, latent):
    nodes, width = latent.shape
    return pl.pallas_call(
        turn_kernel,
        in_specs=[smem, vmem],
        out_specs=vmem,
        out_shape=jax.ShapeDtypeStruct((width, nodes), bf16),
        compiler_params=params(8),
        cost_estimate=cost(0, 8 << 20),
        name="turned",
    )(grid, latent)


def turned_load(turned_hbm, start, turned_ref, sem):
    return pltpu.make_async_copy(turned_hbm.at[pl.ds(start, 256)], turned_ref, sem)


def hidden_loads(part, grid_ref, hidden_hbm, hidden_ref, sems):
    x_lo, z, core = position(grid_ref)
    return [
        pltpu.make_async_copy(
            hidden_hbm.at[owner(block, STEPS[part], x_lo, z)],
            hidden_ref.at[block],
            sems.at[block],
        )
        for block in range(4)
    ]


def first_product(turned_ref, pre_ref, out_ref):
    width = pre_ref.shape[1]
    for column in range(0, width, 512):
        columns = slice(column, column + 512)
        part = jnp.dot(turned_ref[...], pre_ref[:, columns], preferred_element_type=f32)
        out_ref[:, columns] = part.astype(bf16)


def second_product(grid_ref, flat_ref, hidden_ref, send_ref, second_ref, scratch_ref):
    width = send_ref.shape[1] - WIDE
    core = position(grid_ref)[2]
    for block in (0, 2):
        columns = jnp.concatenate([hidden_ref[block], hidden_ref[block + 1]], axis=1)
        second = jnp.dot(flat_ref[...], columns, preferred_element_type=f32)
        scratch_ref[block * 128 : (block + 2) * 128, :] = second.T.astype(bf16)
    for block in range(4):
        rows = slice(block * 64, (block + 1) * 64)
        mine = pl.multiple_of(block * 128 + core * 64, 64)
        other = pl.multiple_of(block * 128 + (1 - core) * 64, 64)
        second_ref[rows, :] = scratch_ref[pl.ds(mine, 64), :]
        send_ref[rows, width:] = scratch_ref[pl.ds(other, 64), :]


def send_a_kernel(
    grid_ref,
    low_ref,
    turned_hbm,
    slope_hbm,
    hidden_hbm,
    padded_ref,
    pre_ref,
    send_ref,
    second_ref,
    flat_ref,
    next_turned_ref,
    turn_ref,
    turned_ref,
    hidden_ref,
    scratch_ref,
    slope_ref,
    turned_sems,
    hidden_sems,
    slope_sems,
):
    nodes, width = pre_ref.shape
    slope_loads = [
        pltpu.make_async_copy(
            slope_hbm.at[pl.ds(start, ROWS)], slope_ref.at[pl.ds(start, ROWS)], slope_sems.at[start // ROWS]
        )
        for start in range(0, nodes, ROWS)
    ]
    turned_now = turned_load(turned_hbm, 0, turned_ref, turned_sems.at[0])
    turned_next = turned_load(turned_hbm, 256, next_turned_ref, turned_sems.at[1])
    hidden_now = hidden_loads(0, grid_ref, hidden_hbm, hidden_ref, hidden_sems)
    for load in slope_loads + [turned_now] + hidden_now + [turned_next]:
        load.start()
    for share in range(low_ref.shape[0]):
        columns = slice(share * SHARE, (share + 1) * SHARE)
        low = jnp.concatenate([low_ref[share], jnp.zeros((WIDE - TALL, SHARE), bf16)], axis=0)
        flat_ref[:, columns] = low
        turn_ref[columns, :] = low.T
    for start in range(0, nodes, ROWS):
        rows = slice(start, start + ROWS)
        slope_loads[start // ROWS].wait()
        for column in range(0, width, COLS):
            columns = slice(column, column + COLS)
            grad_hidden = lax.dot_general(turn_ref[rows, :], padded_ref[columns, :], NT, preferred_element_type=f32)
            pre_ref[rows, columns] = (grad_hidden * slope_ref[rows, columns].astype(f32)).astype(bf16)
    turned_now.wait()
    first_product(turned_ref, pre_ref, send_ref)
    for load in hidden_now:
        load.wait()
    second_product(grid_ref, flat_ref, hidden_ref, send_ref, second_ref, scratch_ref)
    turned_next.wait()


def keep_a_kernel(
    grid_ref,
    turned_hbm,
    hidden_hbm,
    pre_ref,
    turned_ref,
    second_ref,
    keep_ref,
    next_turned_ref,
    next_hidden_ref,
    turned_sem,
    hidden_sems,
):
    loads = [turned_load(turned_hbm, 512, next_turned_ref, turned_sem)]
    loads += hidden_loads(1, grid_ref, hidden_hbm, next_hidden_ref, hidden_sems)
    for load in loads:
        load.start()
    first_product(turned_ref, pre_ref, keep_ref)
    keep_ref[:, pre_ref.shape[1] :] = second_ref[...]
    for load in loads:
        load.wait()


def send_b_kernel(
    grid_ref,
    turned_hbm,
    pre_ref,
    flat_ref,
    turned_ref,
    hidden_ref,
    send_ref,
    second_ref,
    next_turned_ref,
    scratch_ref,
    turned_sem,
):
    load = turned_load(turned_hbm, 768, next_turned_ref, turned_sem)
    load.start()
    first_product(turned_ref, pre_ref, send_ref)
    second_product(grid_ref, flat_ref, hidden_ref, send_ref, second_ref, scratch_ref)
    load.wait()


def keep_b_kernel(weight_hbm, pre_ref, turned_ref, second_ref, keep_ref, weight_ref, weight_sem):
    load = pltpu.make_async_copy(weight_hbm, weight_ref, weight_sem)
    load.start()
    first_product(turned_ref, pre_ref, keep_ref)
    keep_ref[:, pre_ref.shape[1] :] = second_ref[...]
    load.wait()


def shape(*dims):
    return jax.ShapeDtypeStruct(dims, bf16)


def send_a(grid, low, turned_latent, slope, hidden, padded):
    nodes, width = slope.shape
    return pl.pallas_call(
        send_a_kernel,
        in_specs=[smem, vmem, anywhere, anywhere, anywhere, vmem],
        out_specs=[vmem] * 5,
        out_shape=[
            shape(nodes, width),
            shape(256, width + WIDE),
            shape(256, WIDE),
            shape(WIDE, nodes),
            shape(256, nodes),
        ],
        scratch_shapes=[
            pltpu.VMEM((nodes, WIDE), bf16),
            pltpu.VMEM((256, nodes), bf16),
            pltpu.VMEM((4, nodes, 128), bf16),
            pltpu.VMEM((512, WIDE), bf16),
            pltpu.VMEM((nodes, width), bf16),
            pltpu.SemaphoreType.DMA((2,)),
            pltpu.SemaphoreType.DMA((4,)),
            pltpu.SemaphoreType.DMA((nodes // ROWS,)),
        ],
        compiler_params=params(20),
        cost_estimate=cost(nodes * width * (width // 2 + 3 * WIDE), 8 << 20),
        name="send_a",
    )(grid, low, pinned(turned_latent), pinned(slope), pinned(hidden), padded)


def keep_a(grid, turned_latent, hidden, grad_pre, turned_now, second):
    nodes, width = grad_pre.shape
    return pl.pallas_call(
        keep_a_kernel,
        in_specs=[smem, anywhere, anywhere] + [vmem] * 3,
        out_specs=[vmem] * 3,
        out_shape=[shape(256, width + WIDE), shape(256, nodes), shape(4, nodes, 128)],
        scratch_shapes=[pltpu.SemaphoreType.DMA, pltpu.SemaphoreType.DMA((4,))],
        compiler_params=params(12),
        cost_estimate=cost(nodes * width * width // 2, 4 << 20),
        name="keep_a",
    )(grid, pinned(turned_latent), pinned(hidden), grad_pre, turned_now, second)


def send_b(grid, turned_latent, grad_pre, flat, turned_now, hidden_now):
    nodes, width = grad_pre.shape
    return pl.pallas_call(
        send_b_kernel,
        in_specs=[smem, anywhere] + [vmem] * 4,
        out_specs=[vmem] * 3,
        out_shape=[shape(256, width + WIDE), shape(256, WIDE), shape(256, nodes)],
        scratch_shapes=[pltpu.VMEM((512, WIDE), bf16), pltpu.SemaphoreType.DMA],
        compiler_params=params(12),
        cost_estimate=cost(nodes * width * width // 2, 4 << 20),
        name="send_b",
    )(grid, pinned(turned_latent), grad_pre, flat, turned_now, hidden_now)


def keep_b(weight, grad_pre, turned_now, second):
    nodes, width = grad_pre.shape
    return pl.pallas_call(
        keep_b_kernel,
        in_specs=[anywhere] + [vmem] * 3,
        out_specs=[vmem] * 2,
        out_shape=[shape(256, width + WIDE), shape(width, width)],
        scratch_shapes=[pltpu.SemaphoreType.DMA],
        compiler_params=params(12),
        cost_estimate=cost(nodes * width * width // 2, 4 << 20),
        name="keep_b",
    )(pinned(weight), grad_pre, turned_now, second)


def latent_kernel(pre_ref, weight_ref, *refs, begin):
    out_ref, result_ref, sems = refs[-3:]
    width = pre_ref.shape[1]
    stores = []
    for row in range(0, result_ref.shape[0], ROWS):
        rows = slice(begin + row, begin + row + ROWS)
        for start in range(0, width, COLS):
            columns = slice(start, start + COLS)
            result_ref[row : row + ROWS, columns] = lax.dot_general(
                pre_ref[rows, :], weight_ref[columns, :], NT, preferred_element_type=f32
            ).astype(bf16)
        store = pltpu.make_async_copy(
            result_ref.at[pl.ds(row, ROWS)], out_ref.at[pl.ds(begin + row, ROWS)], sems.at[row // ROWS]
        )
        store.start()
        stores.append(store)
    for store in stores:
        store.wait()


def latent_gradient(grad_pre, weight, begin, so_far=None):
    nodes, width = grad_pre.shape
    half = nodes // 2
    more = [] if so_far is None else [so_far]
    return pl.pallas_call(
        functools.partial(latent_kernel, begin=begin),
        in_specs=[vmem, vmem] + [anywhere] * len(more),
        out_specs=anywhere,
        out_shape=pltpu.HBM((nodes, width), bf16),
        input_output_aliases={2: 0} if more else {},
        scratch_shapes=[pltpu.VMEM((half, width), bf16), pltpu.SemaphoreType.DMA((half // ROWS,))],
        compiler_params=params(12),
        cost_estimate=cost(nodes * width * width, 5 << 20),
        name="latent_gradient",
    )(grad_pre, weight, *more)


def finish_kernel(own_ref, *refs, factor):
    *others, first_ref, second_ref = refs
    width, variables = first_ref.shape[1], second_ref.shape[1]
    total = own_ref[...].astype(f32)
    for other in others:
        total = total + other[...].astype(f32)
    total = total * factor
    first_ref[...] = total[:, :width]
    second_ref[...] = total[:, width : width + variables]


def finish(own, others, width, variables, factor):
    rows = own.shape[0]
    return pl.pallas_call(
        functools.partial(finish_kernel, factor=factor),
        in_specs=[vmem] * (1 + len(others)),
        out_specs=[vmem] * 2,
        out_shape=[jax.ShapeDtypeStruct((rows, width), f32), jax.ShapeDtypeStruct((rows, variables), f32)],
        compiler_params=params(8),
        cost_estimate=cost(0, 1 << 20),
        name="finish",
    )(own, *others)


def moved(value, move):
    moves = []
    for member in range(8):
        for grid in range(16):
            y, x_hi, x_lo, z, core = member // 2, member % 2, grid // 8, (grid // 2) % 4, grid % 2
            y, x, z, core = move(y, x_hi * 2 + x_lo, z, core)
            target = (y * 2 + x // 2) * 16 + ((x % 2) * 4 + z) * 2 + core
            moves.append((member * 16 + grid, target))
    return lax.ppermute(value, ("member", "grid"), moves)


def summed(own, others):
    total = own.astype(f32)
    for other in others:
        total = total + other.astype(f32)
    return total


def over_core(send, keep):
    got = moved(send, lambda y, x, z, c: (y, x, z, 1 - c))
    return summed(keep, [got]).reshape(2, 2, 64, send.shape[1])


def up(value):
    return moved(value, lambda y, x, z, c: (y, x, (z + 1) % 4, c))


def down(value):
    return moved(value, lambda y, x, z, c: (y, x, (z + 3) % 4, c))


def over_x(blocks):
    got = [
        moved(blocks[0] if k == 2 else blocks[1], lambda y, x, z, c, k=k: (y, x ^ k, z, c))
        for k in (1, 3, 2)
    ]
    return summed(blocks[0], got).astype(bf16)


def over_y(block):
    return [moved(block, lambda y, x, z, c, k=k: (y ^ k, x, z, c)) for k in (1, 3, 2)]


def body(latents, hidden_weight, output_weight, observed, node_area_weight):
    latent = latents[0]
    members = lax.axis_size("member")
    groups = lax.axis_size("grid")
    nodes, width = latent.shape
    variables = output_weight.shape[1]
    place = lax.axis_index("member").astype(jnp.int32).reshape(1)
    grid = lax.axis_index("grid").astype(jnp.int32).reshape(1)

    forecast, pre, padded = forward(latent, hidden_weight, output_weight.T)
    blocks, pre = lax.optimization_barrier(((0.25 * forecast).astype(f16), pre))
    blocks = lax.all_to_all(blocks, "member", 0, 0, tiled=True)
    hidden, slope = gates(pre)
    blocks, hidden, slope = lax.optimization_barrier((blocks, hidden, slope))
    low = pairs(place, 4.0 * blocks.astype(f32), observed, node_area_weight.reshape(1, nodes))
    low, late_grid = lax.optimization_barrier((low, grid))
    low = lax.all_to_all(low, "member", 0, 0, tiled=True)
    turned_latent = turned(late_grid, latent)
    grad_pre, rows_a, second_a, flat, turned_now = send_a(grid, low, turned_latent, slope, hidden, padded)
    kept_a, turned_now, hidden_now = keep_a(grid, turned_latent, hidden, grad_pre, turned_now, second_a)
    far, own = over_core(rows_a, kept_a).astype(bf16)
    far, own, flat = lax.optimization_barrier((far, own, flat))
    upward, downward = up(far[0]), down(far[1])
    rows_b, second_b, turned_now = send_b(grid, turned_latent, grad_pre, flat, turned_now, hidden_now)
    kept_b, weight_copy = keep_b(hidden_weight, grad_pre, turned_now, second_b)
    above, below = over_core(rows_b, kept_b)
    grad_latent = latent_gradient(grad_pre, weight_copy, 0)
    upward, downward, grad_latent = lax.optimization_barrier((upward, downward, grad_latent))
    above = jnp.stack([above[0] + upward.astype(f32), above[1]]).astype(bf16)
    below = jnp.stack([below[0], below[1] + downward.astype(f32)]).astype(bf16)
    above, below, grad_pre = lax.optimization_barrier((above, below, grad_pre))
    grad_latent = latent_gradient(grad_pre, weight_copy, nodes // 2, grad_latent)
    blocks = summed(own, [up(above), down(below)]).astype(bf16)
    blocks, grad_latent = lax.optimization_barrier((blocks, grad_latent))
    block = over_x(blocks)
    factor = 1.0 / math.sqrt(members * nodes * groups)
    first, second = finish(block, over_y(block), width, variables, factor)
    return grad_latent[None], first, second


def solution(mesh):
    in_specs = (P("member", "grid", None), P(), P(), P(None, "grid"), P("grid"))
    out_specs = (P("member", "grid", None), P("grid", None), P("grid", None))
    return jax.shard_map(body, mesh=mesh, in_specs=in_specs, out_specs=out_specs, check_vma=False)
```

```python
import functools
import math

import jax
import jax.numpy as jnp
from jax import lax
from jax.experimental import pallas as pl
from jax.experimental.pallas import tpu as pltpu
from jax.sharding import PartitionSpec as P

smooth_sq = 0.0025
bf16 = jnp.bfloat16
f16 = jnp.float16
f32 = jnp.float32

NT = (((1,), (1,)), ((), ()))
WIDE = 128
TALL = 112
SHARE = 256
ROWS = 512
COLS = 256

vmem = pl.BlockSpec(memory_space=pltpu.VMEM)
smem = pl.BlockSpec(memory_space=pltpu.SMEM)
anywhere = pl.BlockSpec(memory_space=pltpu.HBM)


def params(mib):
    return pltpu.CompilerParams(vmem_limit_bytes=mib * 1024 * 1024)


def cost(flops, nbytes, trans=0):
    return pl.CostEstimate(flops=flops, bytes_accessed=nbytes, transcendentals=trans)


def chunk(ref, start):
    return ref.at[pl.ds(start, ROWS)]


def forward_kernel(
    latent_ref,
    weight_ref,
    out_weight_ref,
    forecast_ref,
    pre_out,
    padded_ref,
    pre_ref,
    hidden_ref,
    latent_copy,
    weight_copy,
    out_weight_copy,
    latent_sems,
    weight_sem,
    out_weight_sem,
    pre_sems,
):
    nodes, width = latent_ref.shape
    variables = out_weight_ref.shape[0]
    weight_load = pltpu.make_async_copy(weight_ref, weight_copy, weight_sem)
    out_weight_load = pltpu.make_async_copy(out_weight_ref, out_weight_copy, out_weight_sem)
    latent_loads = [
        pltpu.make_async_copy(chunk(latent_ref, start), chunk(latent_copy, start), latent_sems.at[start // ROWS])
        for start in range(0, nodes, ROWS)
    ]
    out_weight_load.start()
    weight_load.start()
    for load in latent_loads:
        load.start()
    out_weight_load.wait()
    turned_weight = jnp.concatenate(
        [out_weight_copy[...], jnp.zeros((WIDE - variables, width), bf16)], axis=0
    )
    padded_ref[...] = turned_weight.T
    weight_load.wait()
    stores = []
    for start in range(0, nodes, ROWS):
        rows = slice(start, start + ROWS)
        latent_loads[start // ROWS].wait()
        pre = jnp.dot(latent_copy[rows, :], weight_copy[...], preferred_element_type=f32)
        pre_ref[rows, :] = pre.astype(bf16)
        hidden_ref[rows, :] = (pre * (0.5 * jnp.tanh(0.5 * pre) + 0.5)).astype(bf16)
        store = pltpu.make_async_copy(chunk(pre_ref, start), chunk(pre_out, start), pre_sems.at[start // ROWS])
        store.start()
        stores.append(store)
        for share in range(start // SHARE, (start + ROWS) // SHARE):
            forecast_ref[share] = lax.dot_general(
                turned_weight[:TALL],
                hidden_ref[share * SHARE : (share + 1) * SHARE, :],
                NT,
                preferred_element_type=f32,
            )
    for store in stores:
        store.wait()


def pinned(value):
    return pltpu.with_memory_space_constraint(value, pltpu.HBM)


def forward(latent, weight, out_weight):
    nodes, width = latent.shape
    return pl.pallas_call(
        forward_kernel,
        in_specs=[anywhere] * 3,
        out_specs=[vmem, anywhere, vmem],
        out_shape=[
            jax.ShapeDtypeStruct((nodes // SHARE, TALL, SHARE), f32),
            pltpu.HBM((nodes, width), bf16),
            jax.ShapeDtypeStruct((width, WIDE), bf16),
        ],
        scratch_shapes=[
            pltpu.VMEM((nodes, width), bf16),
            pltpu.VMEM((nodes, width), bf16),
            pltpu.VMEM((nodes, width), bf16),
            pltpu.VMEM((width, width), bf16),
            pltpu.VMEM(out_weight.shape, bf16),
            pltpu.SemaphoreType.DMA((nodes // ROWS,)),
            pltpu.SemaphoreType.DMA,
            pltpu.SemaphoreType.DMA,
            pltpu.SemaphoreType.DMA((nodes // ROWS,)),
        ],
        compiler_params=params(32),
        cost_estimate=cost(2 * nodes * width * (width + WIDE), 20 << 20),
        name="forward",
    )(pinned(latent), pinned(weight), pinned(out_weight))


def gate_kernel(pre_hbm, hidden_out, slope_out, pre_ref, hidden_ref, slope_ref, pre_sems, hidden_sems, slope_sems):
    nodes, width = pre_hbm.shape
    loads = [
        pltpu.make_async_copy(chunk(pre_hbm, start), chunk(pre_ref, start), pre_sems.at[start // ROWS])
        for start in range(0, nodes, ROWS)
    ]
    for load in loads:
        load.start()
    stores = []
    for start in range(0, nodes, ROWS):
        rows = slice(start, start + ROWS)
        loads[start // ROWS].wait()
        for group in range(width // 128):
            columns = slice(group * 128, (group + 1) * 128)
            pre = pre_ref[rows, columns].astype(f32)
            sig = 0.5 * jnp.tanh(0.5 * pre) + 0.5
            hidden = pre * sig
            hidden_ref[group, rows, :] = hidden.astype(bf16)
            slope_ref[rows, columns] = (sig + hidden * (1.0 - sig)).astype(bf16)
        for store in (
            pltpu.make_async_copy(
                hidden_ref.at[:, pl.ds(start, ROWS)], hidden_out.at[:, pl.ds(start, ROWS)], hidden_sems.at[start // ROWS]
            ),
            pltpu.make_async_copy(chunk(slope_ref, start), chunk(slope_out, start), slope_sems.at[start // ROWS]),
        ):
            store.start()
            stores.append(store)
    for store in stores:
        store.wait()


def gates(pre):
    nodes, width = pre.shape
    sems = pltpu.SemaphoreType.DMA((nodes // ROWS,))
    return pl.pallas_call(
        gate_kernel,
        in_specs=[anywhere],
        out_specs=[anywhere] * 2,
        out_shape=[pltpu.HBM((width // 128, nodes, 128), bf16), pltpu.HBM((nodes, width), bf16)],
        scratch_shapes=[
            pltpu.VMEM((nodes, width), bf16),
            pltpu.VMEM((width // 128, nodes, 128), bf16),
            pltpu.VMEM((nodes, width), bf16),
            sems,
            sems,
            sems,
        ],
        compiler_params=params(20),
        cost_estimate=cost(0, 12 << 20),
        name="gates",
    )(pinned(pre))


def slope_function(diff):
    return diff * lax.rsqrt(diff * diff + smooth_sq)


def pair_kernel(place_ref, blocks_ref, observed_ref, area_ref, low_ref, here_ref, weight_ref, totals_ref, sems):
    members = blocks_ref.shape[0]
    variables = observed_ref.shape[0]
    at = pl.multiple_of(place_ref[0] * SHARE, SHARE)
    loads = [
        pltpu.make_async_copy(observed_ref.at[:, pl.ds(at, SHARE)], here_ref, sems.at[0]),
        pltpu.make_async_copy(area_ref.at[:, pl.ds(at, SHARE)], weight_ref, sems.at[1]),
    ]
    for load in loads:
        load.start()
    for start in range(0, TALL, 16):
        rows = slice(start, start + 16)
        values = [blocks_ref[a, rows, :] for a in range(members)]
        totals = [0.0] * members
        for a in range(members):
            for b in range(a + 1, members):
                slope = slope_function(values[a] - values[b])
                totals[a] = totals[a] + slope
                totals[b] = totals[b] - slope
        for a in range(members):
            totals_ref[a, rows, :] = totals[a]
    for load in loads:
        load.wait()
    area = weight_ref[...]
    for start in range(0, TALL, 16):
        rows = slice(start, start + 16)
        real = min(16, variables - start)
        observed = here_ref[start : start + real, :]
        if real < 16:
            observed = jnp.concatenate([observed, jnp.zeros((16 - real, SHARE), f32)], axis=0)
        for a in range(members):
            own = slope_function(blocks_ref[a, rows, :] - observed)
            low_ref[a, rows, :] = (area * (own - totals_ref[a, rows, :] * (1.0 / (members - 1)))).astype(bf16)


def pairs(place, blocks, observed, area):
    members = blocks.shape[0]
    variables = observed.shape[0]
    return pl.pallas_call(
        pair_kernel,
        in_specs=[smem, vmem, anywhere, anywhere],
        out_specs=vmem,
        out_shape=jax.ShapeDtypeStruct((members, TALL, SHARE), bf16),
        scratch_shapes=[
            pltpu.VMEM((variables, SHARE), f32),
            pltpu.VMEM((1, SHARE), f32),
            pltpu.VMEM((members, TALL, SHARE), f32),
            pltpu.SemaphoreType.DMA((2,)),
        ],
        compiler_params=params(8),
        cost_estimate=cost(4 << 20, 2 << 20),
        name="pairs",
    )(place, blocks, observed, area)


def position(grid_ref):
    grid = grid_ref[0]
    return grid >> 3, (grid >> 1) & 3, grid & 1


FAR = 256
NEAR = 384
NEAR_STEPS = (1, 3, 0)


def owner(step, other_x, x_lo, z):
    return (other_x ^ x_lo) * 4 + ((z + step) & 3)


def turn_kernel(grid_ref, latent_ref, turned_ref):
    nodes, width = latent_ref.shape
    x_lo, z, core = position(grid_ref)
    for group in range(8):
        step = (group - z) & 3
        other_x = (group >> 2) ^ x_lo
        odd = step & 1
        far = (step >> 1) * (1 - odd)
        near = FAR + (odd * (step >> 1) + (1 - odd) * 2) * 128 + other_x * 64
        first = far * (other_x * 128 + (1 - core) * 64) + (1 - far) * (near + (1 - core) * NEAR)
        second = far * (other_x * 128 + core * 64) + (1 - far) * (near + core * NEAR)
        first = pl.multiple_of(first, 64)
        second = pl.multiple_of(second, 64)
        for row in range(0, nodes, ROWS):
            columns = slice(row, row + ROWS)
            block = latent_ref[columns, group * 128 : (group + 1) * 128].T
            turned_ref[pl.ds(first, 64), columns] = block[:64]
            turned_ref[pl.ds(second, 64), columns] = block[64:]


def turned(grid, latent):
    nodes, width = latent.shape
    return pl.pallas_call(
        turn_kernel,
        in_specs=[smem, vmem],
        out_specs=vmem,
        out_shape=jax.ShapeDtypeStruct((width, nodes), bf16),
        compiler_params=params(8),
        cost_estimate=cost(0, 8 << 20),
        name="turned",
    )(grid, latent)


def first_product(turned_ref, pre_ref, out_ref):
    width = pre_ref.shape[1]
    for column in range(0, width, 512):
        columns = slice(column, column + 512)
        part = jnp.dot(turned_ref[...], pre_ref[:, columns], preferred_element_type=f32)
        out_ref[:, columns] = part.astype(bf16)


def second_product(flat_ref, hidden_ref, scratch_ref):
    for block in range(0, hidden_ref.shape[0], 2):
        columns = jnp.concatenate([hidden_ref[block], hidden_ref[block + 1]], axis=1)
        second = jnp.dot(flat_ref[...], columns, preferred_element_type=f32)
        scratch_ref[block * 128 : (block + 2) * 128, :] = second.T.astype(bf16)


def far_kernel(
    grid_ref,
    low_ref,
    turned_hbm,
    slope_hbm,
    hidden_hbm,
    padded_ref,
    pre_ref,
    up_ref,
    down_ref,
    flat_ref,
    turn_ref,
    turned_ref,
    hidden_ref,
    scratch_ref,
    slope_ref,
    turned_sem,
    hidden_sems,
    slope_sems,
):
    nodes, width = pre_ref.shape
    x_lo, z, core = position(grid_ref)
    slope_loads = [
        pltpu.make_async_copy(chunk(slope_hbm, start), chunk(slope_ref, start), slope_sems.at[start // ROWS])
        for start in range(0, nodes, ROWS)
    ]
    turned_load = pltpu.make_async_copy(turned_hbm.at[pl.ds(0, FAR)], turned_ref, turned_sem)
    hidden_loads = [
        pltpu.make_async_copy(hidden_hbm.at[owner(2, other_x, x_lo, z)], hidden_ref.at[other_x], hidden_sems.at[other_x])
        for other_x in (0, 1)
    ]
    for load in slope_loads + [turned_load] + hidden_loads:
        load.start()
    for share in range(low_ref.shape[0]):
        columns = slice(share * SHARE, (share + 1) * SHARE)
        low = jnp.concatenate([low_ref[share], jnp.zeros((WIDE - TALL, SHARE), bf16)], axis=0)
        flat_ref[:, columns] = low
        turn_ref[columns, :] = low.T
    for start in range(0, nodes, ROWS):
        rows = slice(start, start + ROWS)
        slope_loads[start // ROWS].wait()
        for column in range(0, width, COLS):
            columns = slice(column, column + COLS)
            grad_hidden = lax.dot_general(turn_ref[rows, :], padded_ref[columns, :], NT, preferred_element_type=f32)
            pre_ref[rows, columns] = (grad_hidden * slope_ref[rows, columns].astype(f32)).astype(bf16)
    turned_load.wait()
    for column in range(0, width, 512):
        columns = slice(column, column + 512)
        part = jnp.dot(turned_ref[...], pre_ref[:, columns], preferred_element_type=f32).astype(bf16)
        up_ref[:, columns] = part[:128]
        down_ref[:, columns] = part[128:]
    for load in hidden_loads:
        load.wait()
    second_product(flat_ref, hidden_ref, scratch_ref)
    for block, out_ref in enumerate((up_ref, down_ref)):
        mine = pl.multiple_of(block * 128 + core * 64, 64)
        other = pl.multiple_of(block * 128 + (1 - core) * 64, 64)
        out_ref[:64, width:] = scratch_ref[pl.ds(other, 64), :]
        out_ref[64:, width:] = scratch_ref[pl.ds(mine, 64), :]


def near_kernel(
    grid_ref,
    turned_hbm,
    hidden_hbm,
    weight_hbm,
    pre_ref,
    flat_ref,
    send_ref,
    keep_ref,
    weight_ref,
    turned_ref,
    hidden_ref,
    scratch_ref,
    turned_sems,
    hidden_sems,
    weight_sem,
):
    width = pre_ref.shape[1]
    x_lo, z, core = position(grid_ref)
    turned_loads = [
        pltpu.make_async_copy(turned_hbm.at[pl.ds(FAR + part * NEAR, NEAR)], turned_ref.at[part], turned_sems.at[part])
        for part in (0, 1)
    ]
    hidden_loads = [
        pltpu.make_async_copy(
            hidden_hbm.at[owner(NEAR_STEPS[block // 2], block % 2, x_lo, z)], hidden_ref.at[block], hidden_sems.at[block]
        )
        for block in range(6)
    ]
    weight_load = pltpu.make_async_copy(weight_hbm, weight_ref, weight_sem)
    for load in turned_loads + hidden_loads + [weight_load]:
        load.start()
    for part, out_ref in enumerate((send_ref, keep_ref)):
        turned_loads[part].wait()
        first_product(turned_ref.at[part], pre_ref, out_ref)
    for load in hidden_loads:
        load.wait()
    second_product(flat_ref, hidden_ref, scratch_ref)
    for block in range(6):
        rows = slice(block * 64, (block + 1) * 64)
        mine = pl.multiple_of(block * 128 + core * 64, 64)
        other = pl.multiple_of(block * 128 + (1 - core) * 64, 64)
        keep_ref[rows, width:] = scratch_ref[pl.ds(mine, 64), :]
        send_ref[rows, width:] = scratch_ref[pl.ds(other, 64), :]
    weight_load.wait()


def shape(*dims):
    return jax.ShapeDtypeStruct(dims, bf16)


def backward_far(grid, low, turned_latent, slope, hidden, padded):
    nodes, width = slope.shape
    return pl.pallas_call(
        far_kernel,
        in_specs=[smem, vmem, anywhere, anywhere, anywhere, vmem],
        out_specs=[vmem] * 4,
        out_shape=[
            shape(nodes, width),
            shape(128, width + WIDE),
            shape(128, width + WIDE),
            shape(WIDE, nodes),
        ],
        scratch_shapes=[
            pltpu.VMEM((nodes, WIDE), bf16),
            pltpu.VMEM((FAR, nodes), bf16),
            pltpu.VMEM((2, nodes, 128), bf16),
            pltpu.VMEM((256, WIDE), bf16),
            pltpu.VMEM((nodes, width), bf16),
            pltpu.SemaphoreType.DMA,
            pltpu.SemaphoreType.DMA((2,)),
            pltpu.SemaphoreType.DMA((nodes // ROWS,)),
        ],
        compiler_params=params(20),
        cost_estimate=cost(nodes * width * (width // 2 + 3 * WIDE), 8 << 20),
        name="backward_far",
    )(grid, low, pinned(turned_latent), pinned(slope), pinned(hidden), padded)


def backward_near(grid, turned_latent, hidden, weight, grad_pre, flat):
    nodes, width = grad_pre.shape
    return pl.pallas_call(
        near_kernel,
        in_specs=[smem, anywhere, anywhere, anywhere, vmem, vmem],
        out_specs=[vmem] * 3,
        out_shape=[shape(NEAR, width + WIDE), shape(NEAR, width + WIDE), shape(width, width)],
        scratch_shapes=[
            pltpu.VMEM((2, NEAR, nodes), bf16),
            pltpu.VMEM((6, nodes, 128), bf16),
            pltpu.VMEM((768, WIDE), bf16),
            pltpu.SemaphoreType.DMA((2,)),
            pltpu.SemaphoreType.DMA((6,)),
            pltpu.SemaphoreType.DMA,
        ],
        compiler_params=params(20),
        cost_estimate=cost(nodes * width * (3 * width // 2 + 2 * WIDE), 8 << 20),
        name="backward_near",
    )(grid, pinned(turned_latent), pinned(hidden), pinned(weight), grad_pre, flat)


def latent_kernel(pre_ref, weight_ref, out_ref, result_ref, sems):
    nodes, width = pre_ref.shape
    stores = []
    for row in range(0, nodes, ROWS):
        rows = slice(row, row + ROWS)
        for start in range(0, width, COLS):
            columns = slice(start, start + COLS)
            result_ref[rows, columns] = lax.dot_general(
                pre_ref[rows, :], weight_ref[columns, :], NT, preferred_element_type=f32
            ).astype(bf16)
        store = pltpu.make_async_copy(
            result_ref.at[pl.ds(row, ROWS)], out_ref.at[pl.ds(row, ROWS)], sems.at[row // ROWS]
        )
        store.start()
        stores.append(store)
    for store in stores:
        store.wait()


def latent_gradient(grad_pre, weight):
    nodes, width = grad_pre.shape
    return pl.pallas_call(
        latent_kernel,
        in_specs=[vmem, vmem],
        out_specs=anywhere,
        out_shape=pltpu.HBM((nodes, width), bf16),
        scratch_shapes=[pltpu.VMEM((nodes, width), bf16), pltpu.SemaphoreType.DMA((nodes // ROWS,))],
        compiler_params=params(12),
        cost_estimate=cost(2 * nodes * width * width, 10 << 20),
        name="latent_gradient",
    )(grad_pre, weight)


def finish_kernel(own_ref, *refs, factor):
    *others, first_ref, second_ref = refs
    width, variables = first_ref.shape[1], second_ref.shape[1]
    total = own_ref[...].astype(f32)
    for other in others:
        total = total + other[...].astype(f32)
    total = total * factor
    first_ref[...] = total[:, :width]
    second_ref[...] = total[:, width : width + variables]


def finish(own, others, width, variables, factor):
    rows = own.shape[0]
    return pl.pallas_call(
        functools.partial(finish_kernel, factor=factor),
        in_specs=[vmem] * (1 + len(others)),
        out_specs=[vmem] * 2,
        out_shape=[jax.ShapeDtypeStruct((rows, width), f32), jax.ShapeDtypeStruct((rows, variables), f32)],
        compiler_params=params(8),
        cost_estimate=cost(0, 1 << 20),
        name="finish",
    )(own, *others)


def moved(value, move):
    moves = []
    for member in range(8):
        for grid in range(16):
            y, x_hi, x_lo, z, core = member // 2, member % 2, grid // 8, (grid // 2) % 4, grid % 2
            y, x, z, core = move(y, x_hi * 2 + x_lo, z, core)
            target = (y * 2 + x // 2) * 16 + ((x % 2) * 4 + z) * 2 + core
            moves.append((member * 16 + grid, target))
    return lax.ppermute(value, ("member", "grid"), moves)


def summed(own, others):
    total = own.astype(f32)
    for other in others:
        total = total + other.astype(f32)
    return total


def up(value):
    return moved(value, lambda y, x, z, c: (y, x, (z + 1) % 4, c))


def down(value):
    return moved(value, lambda y, x, z, c: (y, x, (z + 3) % 4, c))


def over_x(blocks):
    got = [
        moved(blocks[0] if k == 2 else blocks[1], lambda y, x, z, c, k=k: (y, x ^ k, z, c))
        for k in (1, 3, 2)
    ]
    return summed(blocks[0], got).astype(bf16)


def over_y(block):
    return [moved(block, lambda y, x, z, c, k=k: (y ^ k, x, z, c)) for k in (1, 3, 2)]


def body(latents, hidden_weight, output_weight, observed, node_area_weight):
    latent = latents[0]
    members = lax.axis_size("member")
    groups = lax.axis_size("grid")
    nodes, width = latent.shape
    variables = output_weight.shape[1]
    place = lax.axis_index("member").astype(jnp.int32).reshape(1)
    grid = lax.axis_index("grid").astype(jnp.int32).reshape(1)

    forecast, pre, padded = forward(latent, hidden_weight, output_weight.T)
    blocks, pre = lax.optimization_barrier(((0.25 * forecast).astype(f16), pre))
    blocks = lax.all_to_all(blocks, "member", 0, 0, tiled=True)
    hidden, slope = gates(pre)
    blocks, hidden, slope = lax.optimization_barrier((blocks, hidden, slope))
    low = pairs(place, 4.0 * blocks.astype(f32), observed, node_area_weight.reshape(1, nodes))
    low, late_grid = lax.optimization_barrier((low, grid))
    low = lax.all_to_all(low, "member", 0, 0, tiled=True)
    turned_latent = turned(late_grid, latent)
    grad_pre, upward, downward, flat = backward_far(grid, low, turned_latent, slope, hidden, padded)
    upward, downward = up(upward).astype(f32), down(downward).astype(f32)
    send, keep, weight_copy = backward_near(grid, turned_latent, hidden, hidden_weight, grad_pre, flat)

    def joined(rows, at):
        rows = rows.astype(f32).reshape(3, 2, 64, rows.shape[1])
        above = jnp.stack([rows[0, 0] + upward[at : at + 64], rows[0, 1]])
        below = jnp.stack([rows[1, 0], rows[1, 1] + downward[at : at + 64]])
        return jnp.stack([above, below, rows[2]])

    got = moved(joined(send, 0).astype(bf16), lambda y, x, z, c: (y, x, z, 1 - c))
    above, below, own = (joined(keep, 64) + got.astype(f32)).astype(bf16)
    above, below, grad_pre = lax.optimization_barrier((above, below, grad_pre))
    grad_latent = latent_gradient(grad_pre, weight_copy)
    blocks = summed(own, [up(above), down(below)]).astype(bf16)
    blocks, grad_latent = lax.optimization_barrier((blocks, grad_latent))
    block = over_x(blocks)
    factor = 1.0 / math.sqrt(members * nodes * groups)
    first, second = finish(block, over_y(block), width, variables, factor)
    return grad_latent[None], first, second


def solution(mesh):
    in_specs = (P("member", "grid", None), P(), P(), P(None, "grid"), P("grid"))
    out_specs = (P("member", "grid", None), P("grid", None), P("grid", None))
    return jax.shard_map(body, mesh=mesh, in_specs=in_specs, out_specs=out_specs, check_vma=False)
```

```python
import functools
import math

import jax
import jax.numpy as jnp
from jax import lax
from jax.experimental import pallas as pl
from jax.experimental.pallas import tpu as pltpu
from jax.sharding import PartitionSpec as P

smooth_sq = 0.0025
bf16 = jnp.bfloat16
f16 = jnp.float16
f32 = jnp.float32

NT = (((1,), (1,)), ((), ()))
WIDE = 128
TALL = 112
SHARE = 256
ROWS = 512
COLS = 256

vmem = pl.BlockSpec(memory_space=pltpu.VMEM)
smem = pl.BlockSpec(memory_space=pltpu.SMEM)
anywhere = pl.BlockSpec(memory_space=pltpu.HBM)


def params(mib):
    return pltpu.CompilerParams(vmem_limit_bytes=mib * 1024 * 1024)


def cost(flops, nbytes, trans=0):
    return pl.CostEstimate(flops=flops, bytes_accessed=nbytes, transcendentals=trans)


def chunk(ref, start):
    return ref.at[pl.ds(start, ROWS)]


def forward_kernel(
    latent_ref,
    weight_ref,
    out_weight_ref,
    forecast_ref,
    pre_out,
    padded_ref,
    pre_ref,
    hidden_ref,
    latent_copy,
    weight_copy,
    out_weight_copy,
    latent_sems,
    weight_sem,
    out_weight_sem,
    pre_sems,
):
    nodes, width = latent_ref.shape
    variables = out_weight_ref.shape[0]
    weight_load = pltpu.make_async_copy(weight_ref, weight_copy, weight_sem)
    out_weight_load = pltpu.make_async_copy(out_weight_ref, out_weight_copy, out_weight_sem)
    latent_loads = [
        pltpu.make_async_copy(chunk(latent_ref, start), chunk(latent_copy, start), latent_sems.at[start // ROWS])
        for start in range(0, nodes, ROWS)
    ]
    out_weight_load.start()
    weight_load.start()
    for load in latent_loads:
        load.start()
    out_weight_load.wait()
    turned_weight = jnp.concatenate(
        [out_weight_copy[...], jnp.zeros((WIDE - variables, width), bf16)], axis=0
    )
    padded_ref[...] = turned_weight.T
    weight_load.wait()
    stores = []
    for start in range(0, nodes, ROWS):
        rows = slice(start, start + ROWS)
        latent_loads[start // ROWS].wait()
        pre = jnp.dot(latent_copy[rows, :], weight_copy[...], preferred_element_type=f32)
        pre_ref[rows, :] = pre.astype(bf16)
        hidden_ref[rows, :] = (pre * (0.5 * jnp.tanh(0.5 * pre) + 0.5)).astype(bf16)
        store = pltpu.make_async_copy(chunk(pre_ref, start), chunk(pre_out, start), pre_sems.at[start // ROWS])
        store.start()
        stores.append(store)
        for share in range(start // SHARE, (start + ROWS) // SHARE):
            forecast_ref[share] = lax.dot_general(
                turned_weight[:TALL],
                hidden_ref[share * SHARE : (share + 1) * SHARE, :],
                NT,
                preferred_element_type=f32,
            )
    for store in stores:
        store.wait()


def pinned(value):
    return pltpu.with_memory_space_constraint(value, pltpu.HBM)


def forward(latent, weight, out_weight):
    nodes, width = latent.shape
    return pl.pallas_call(
        forward_kernel,
        in_specs=[anywhere] * 3,
        out_specs=[vmem, anywhere, vmem],
        out_shape=[
            jax.ShapeDtypeStruct((nodes // SHARE, TALL, SHARE), f32),
            pltpu.HBM((nodes, width), bf16),
            jax.ShapeDtypeStruct((width, WIDE), bf16),
        ],
        scratch_shapes=[
            pltpu.VMEM((nodes, width), bf16),
            pltpu.VMEM((nodes, width), bf16),
            pltpu.VMEM((nodes, width), bf16),
            pltpu.VMEM((width, width), bf16),
            pltpu.VMEM(out_weight.shape, bf16),
            pltpu.SemaphoreType.DMA((nodes // ROWS,)),
            pltpu.SemaphoreType.DMA,
            pltpu.SemaphoreType.DMA,
            pltpu.SemaphoreType.DMA((nodes // ROWS,)),
        ],
        compiler_params=params(32),
        cost_estimate=cost(2 * nodes * width * (width + WIDE), 20 << 20),
        name="forward",
    )(pinned(latent), pinned(weight), pinned(out_weight))


def gate_kernel(pre_hbm, hidden_out, slope_out, pre_ref, hidden_ref, slope_ref, pre_sems, hidden_sems, slope_sems):
    nodes, width = pre_hbm.shape
    loads = [
        pltpu.make_async_copy(chunk(pre_hbm, start), chunk(pre_ref, start), pre_sems.at[start // ROWS])
        for start in range(0, nodes, ROWS)
    ]
    for load in loads:
        load.start()
    stores = []
    for start in range(0, nodes, ROWS):
        rows = slice(start, start + ROWS)
        loads[start // ROWS].wait()
        for group in range(width // 128):
            columns = slice(group * 128, (group + 1) * 128)
            pre = pre_ref[rows, columns].astype(f32)
            sig = 0.5 * jnp.tanh(0.5 * pre) + 0.5
            hidden = pre * sig
            hidden_ref[group, rows, :] = hidden.astype(bf16)
            slope_ref[rows, columns] = (sig + hidden * (1.0 - sig)).astype(bf16)
        for store in (
            pltpu.make_async_copy(
                hidden_ref.at[:, pl.ds(start, ROWS)], hidden_out.at[:, pl.ds(start, ROWS)], hidden_sems.at[start // ROWS]
            ),
            pltpu.make_async_copy(chunk(slope_ref, start), chunk(slope_out, start), slope_sems.at[start // ROWS]),
        ):
            store.start()
            stores.append(store)
    for store in stores:
        store.wait()


def gates(pre):
    nodes, width = pre.shape
    sems = pltpu.SemaphoreType.DMA((nodes // ROWS,))
    return pl.pallas_call(
        gate_kernel,
        in_specs=[anywhere],
        out_specs=[anywhere] * 2,
        out_shape=[pltpu.HBM((width // 128, nodes, 128), bf16), pltpu.HBM((nodes, width), bf16)],
        scratch_shapes=[
            pltpu.VMEM((nodes, width), bf16),
            pltpu.VMEM((width // 128, nodes, 128), bf16),
            pltpu.VMEM((nodes, width), bf16),
            sems,
            sems,
            sems,
        ],
        compiler_params=params(20),
        cost_estimate=cost(0, 12 << 20),
        name="gates",
    )(pinned(pre))


def slope_function(diff):
    return diff * lax.rsqrt(diff * diff + smooth_sq)


def pair_kernel(place_ref, blocks_ref, observed_ref, area_ref, low_ref, here_ref, weight_ref, totals_ref, sems):
    members = blocks_ref.shape[0]
    variables = observed_ref.shape[0]
    at = pl.multiple_of(place_ref[0] * SHARE, SHARE)
    loads = [
        pltpu.make_async_copy(observed_ref.at[:, pl.ds(at, SHARE)], here_ref, sems.at[0]),
        pltpu.make_async_copy(area_ref.at[:, pl.ds(at, SHARE)], weight_ref, sems.at[1]),
    ]
    for load in loads:
        load.start()
    for start in range(0, TALL, 16):
        rows = slice(start, start + 16)
        values = [blocks_ref[a, rows, :] for a in range(members)]
        totals = [0.0] * members
        for a in range(members):
            for b in range(a + 1, members):
                slope = slope_function(values[a] - values[b])
                totals[a] = totals[a] + slope
                totals[b] = totals[b] - slope
        for a in range(members):
            totals_ref[a, rows, :] = totals[a]
    for load in loads:
        load.wait()
    area = weight_ref[...]
    for start in range(0, TALL, 16):
        rows = slice(start, start + 16)
        real = min(16, variables - start)
        observed = here_ref[start : start + real, :]
        if real < 16:
            observed = jnp.concatenate([observed, jnp.zeros((16 - real, SHARE), f32)], axis=0)
        for a in range(members):
            own = slope_function(blocks_ref[a, rows, :] - observed)
            low_ref[a, rows, :] = (area * (own - totals_ref[a, rows, :] * (1.0 / (members - 1)))).astype(bf16)


def pairs(place, blocks, observed, area):
    members = blocks.shape[0]
    variables = observed.shape[0]
    return pl.pallas_call(
        pair_kernel,
        in_specs=[smem, vmem, anywhere, anywhere],
        out_specs=vmem,
        out_shape=jax.ShapeDtypeStruct((members, TALL, SHARE), bf16),
        scratch_shapes=[
            pltpu.VMEM((variables, SHARE), f32),
            pltpu.VMEM((1, SHARE), f32),
            pltpu.VMEM((members, TALL, SHARE), f32),
            pltpu.SemaphoreType.DMA((2,)),
        ],
        compiler_params=params(8),
        cost_estimate=cost(4 << 20, 2 << 20),
        name="pairs",
    )(place, blocks, observed, area)


def position(grid_ref):
    grid = grid_ref[0]
    return grid >> 3, (grid >> 1) & 3, grid & 1


PARTS = (((2, 0), (2, 1), (1, 1), (3, 0)), ((1, 0), (3, 1), (0, 0), (0, 1)))


def turn_kernel(grid_ref, latent_ref, turned_ref):
    nodes, width = latent_ref.shape
    x_lo, z, core = position(grid_ref)
    for group in range(8):
        step = (group - z) & 3
        other_x = (group >> 2) ^ x_lo
        odd, back = step & 1, step >> 1
        part = odd * (1 - (other_x ^ back)) + (1 - odd) * (1 - back)
        place = odd * (back + 2 * (1 - part)) + (1 - odd) * (other_x + 2 * part)
        at = part * 512 + place * 64
        first = pl.multiple_of(at + (1 - core) * 256, 64)
        second = pl.multiple_of(at + core * 256, 64)
        for row in range(0, nodes, ROWS):
            columns = slice(row, row + ROWS)
            block = latent_ref[columns, group * 128 : (group + 1) * 128].T
            turned_ref[pl.ds(first, 64), columns] = block[:64]
            turned_ref[pl.ds(second, 64), columns] = block[64:]


def turned(grid, latent):
    nodes, width = latent.shape
    return pl.pallas_call(
        turn_kernel,
        in_specs=[smem, vmem],
        out_specs=vmem,
        out_shape=jax.ShapeDtypeStruct((width, nodes), bf16),
        compiler_params=params(8),
        cost_estimate=cost(0, 8 << 20),
        name="turned",
    )(grid, latent)


def turned_load(turned_hbm, start, turned_ref, sem):
    return pltpu.make_async_copy(turned_hbm.at[pl.ds(start, 256)], turned_ref, sem)


def hidden_loads(part, grid_ref, hidden_hbm, hidden_ref, sems):
    x_lo, z, core = position(grid_ref)
    return [
        pltpu.make_async_copy(
            hidden_hbm.at[(other_x ^ x_lo) * 4 + ((z + step) & 3)], hidden_ref.at[block], sems.at[block]
        )
        for block, (step, other_x) in enumerate(PARTS[part])
    ]


def first_product(turned_ref, pre_ref, out_ref):
    width = pre_ref.shape[1]
    for column in range(0, width, 512):
        columns = slice(column, column + 512)
        part = jnp.dot(turned_ref[...], pre_ref[:, columns], preferred_element_type=f32)
        out_ref[:, columns] = part.astype(bf16)


def second_product(grid_ref, flat_ref, hidden_ref, send_ref, second_ref, scratch_ref):
    width = send_ref.shape[1] - WIDE
    core = position(grid_ref)[2]
    for block in (0, 2):
        columns = jnp.concatenate([hidden_ref[block], hidden_ref[block + 1]], axis=1)
        second = jnp.dot(flat_ref[...], columns, preferred_element_type=f32)
        scratch_ref[block * 128 : (block + 2) * 128, :] = second.T.astype(bf16)
    for block in range(4):
        rows = slice(block * 64, (block + 1) * 64)
        mine = pl.multiple_of(block * 128 + core * 64, 64)
        other = pl.multiple_of(block * 128 + (1 - core) * 64, 64)
        second_ref[rows, :] = scratch_ref[pl.ds(mine, 64), :]
        send_ref[rows, width:] = scratch_ref[pl.ds(other, 64), :]


def send_a_kernel(
    grid_ref,
    low_ref,
    turned_hbm,
    slope_hbm,
    hidden_hbm,
    padded_ref,
    pre_ref,
    send_ref,
    second_ref,
    flat_ref,
    next_turned_ref,
    turn_ref,
    turned_ref,
    hidden_ref,
    scratch_ref,
    slope_ref,
    turned_sems,
    hidden_sems,
    slope_sems,
):
    nodes, width = pre_ref.shape
    slope_loads = [
        pltpu.make_async_copy(
            slope_hbm.at[pl.ds(start, ROWS)], slope_ref.at[pl.ds(start, ROWS)], slope_sems.at[start // ROWS]
        )
        for start in range(0, nodes, ROWS)
    ]
    turned_now = turned_load(turned_hbm, 0, turned_ref, turned_sems.at[0])
    turned_next = turned_load(turned_hbm, 256, next_turned_ref, turned_sems.at[1])
    hidden_now = hidden_loads(0, grid_ref, hidden_hbm, hidden_ref, hidden_sems)
    for load in slope_loads + [turned_now] + hidden_now + [turned_next]:
        load.start()
    for share in range(low_ref.shape[0]):
        columns = slice(share * SHARE, (share + 1) * SHARE)
        low = jnp.concatenate([low_ref[share], jnp.zeros((WIDE - TALL, SHARE), bf16)], axis=0)
        flat_ref[:, columns] = low
        turn_ref[columns, :] = low.T
    for start in range(0, nodes, ROWS):
        rows = slice(start, start + ROWS)
        slope_loads[start // ROWS].wait()
        for column in range(0, width, COLS):
            columns = slice(column, column + COLS)
            grad_hidden = lax.dot_general(turn_ref[rows, :], padded_ref[columns, :], NT, preferred_element_type=f32)
            pre_ref[rows, columns] = (grad_hidden * slope_ref[rows, columns].astype(f32)).astype(bf16)
    turned_now.wait()
    first_product(turned_ref, pre_ref, send_ref)
    for load in hidden_now:
        load.wait()
    second_product(grid_ref, flat_ref, hidden_ref, send_ref, second_ref, scratch_ref)
    turned_next.wait()


def keep_a_kernel(
    grid_ref,
    turned_hbm,
    hidden_hbm,
    pre_ref,
    turned_ref,
    second_ref,
    keep_ref,
    next_turned_ref,
    next_hidden_ref,
    turned_sem,
    hidden_sems,
):
    loads = [turned_load(turned_hbm, 512, next_turned_ref, turned_sem)]
    loads += hidden_loads(1, grid_ref, hidden_hbm, next_hidden_ref, hidden_sems)
    for load in loads:
        load.start()
    first_product(turned_ref, pre_ref, keep_ref)
    keep_ref[:, pre_ref.shape[1] :] = second_ref[...]
    for load in loads:
        load.wait()


def send_b_kernel(
    grid_ref,
    turned_hbm,
    pre_ref,
    flat_ref,
    turned_ref,
    hidden_ref,
    send_ref,
    second_ref,
    next_turned_ref,
    scratch_ref,
    turned_sem,
):
    load = turned_load(turned_hbm, 768, next_turned_ref, turned_sem)
    load.start()
    first_product(turned_ref, pre_ref, send_ref)
    second_product(grid_ref, flat_ref, hidden_ref, send_ref, second_ref, scratch_ref)
    load.wait()


def keep_b_kernel(weight_hbm, pre_ref, turned_ref, second_ref, keep_ref, weight_ref, weight_sem):
    load = pltpu.make_async_copy(weight_hbm, weight_ref, weight_sem)
    load.start()
    first_product(turned_ref, pre_ref, keep_ref)
    keep_ref[:, pre_ref.shape[1] :] = second_ref[...]
    load.wait()


def shape(*dims):
    return jax.ShapeDtypeStruct(dims, bf16)


def send_a(grid, low, turned_latent, slope, hidden, padded):
    nodes, width = slope.shape
    return pl.pallas_call(
        send_a_kernel,
        in_specs=[smem, vmem, anywhere, anywhere, anywhere, vmem],
        out_specs=[vmem] * 5,
        out_shape=[
            shape(nodes, width),
            shape(256, width + WIDE),
            shape(256, WIDE),
            shape(WIDE, nodes),
            shape(256, nodes),
        ],
        scratch_shapes=[
            pltpu.VMEM((nodes, WIDE), bf16),
            pltpu.VMEM((256, nodes), bf16),
            pltpu.VMEM((4, nodes, 128), bf16),
            pltpu.VMEM((512, WIDE), bf16),
            pltpu.VMEM((nodes, width), bf16),
            pltpu.SemaphoreType.DMA((2,)),
            pltpu.SemaphoreType.DMA((4,)),
            pltpu.SemaphoreType.DMA((nodes // ROWS,)),
        ],
        compiler_params=params(20),
        cost_estimate=cost(nodes * width * (width // 2 + 3 * WIDE), 8 << 20),
        name="send_a",
    )(grid, low, pinned(turned_latent), pinned(slope), pinned(hidden), padded)


def keep_a(grid, turned_latent, hidden, grad_pre, turned_now, second):
    nodes, width = grad_pre.shape
    return pl.pallas_call(
        keep_a_kernel,
        in_specs=[smem, anywhere, anywhere] + [vmem] * 3,
        out_specs=[vmem] * 3,
        out_shape=[shape(256, width + WIDE), shape(256, nodes), shape(4, nodes, 128)],
        scratch_shapes=[pltpu.SemaphoreType.DMA, pltpu.SemaphoreType.DMA((4,))],
        compiler_params=params(12),
        cost_estimate=cost(nodes * width * width // 2, 4 << 20),
        name="keep_a",
    )(grid, pinned(turned_latent), pinned(hidden), grad_pre, turned_now, second)


def send_b(grid, turned_latent, grad_pre, flat, turned_now, hidden_now):
    nodes, width = grad_pre.shape
    return pl.pallas_call(
        send_b_kernel,
        in_specs=[smem, anywhere] + [vmem] * 4,
        out_specs=[vmem] * 3,
        out_shape=[shape(256, width + WIDE), shape(256, WIDE), shape(256, nodes)],
        scratch_shapes=[pltpu.VMEM((512, WIDE), bf16), pltpu.SemaphoreType.DMA],
        compiler_params=params(12),
        cost_estimate=cost(nodes * width * width // 2, 4 << 20),
        name="send_b",
    )(grid, pinned(turned_latent), grad_pre, flat, turned_now, hidden_now)


def keep_b(weight, grad_pre, turned_now, second):
    nodes, width = grad_pre.shape
    return pl.pallas_call(
        keep_b_kernel,
        in_specs=[anywhere] + [vmem] * 3,
        out_specs=[vmem] * 2,
        out_shape=[shape(256, width + WIDE), shape(width, width)],
        scratch_shapes=[pltpu.SemaphoreType.DMA],
        compiler_params=params(12),
        cost_estimate=cost(nodes * width * width // 2, 4 << 20),
        name="keep_b",
    )(pinned(weight), grad_pre, turned_now, second)


def latent_kernel(pre_ref, weight_ref, out_ref, result_ref, sems):
    nodes, width = pre_ref.shape
    stores = []
    for row in range(0, nodes, ROWS):
        rows = slice(row, row + ROWS)
        for start in range(0, width, COLS):
            columns = slice(start, start + COLS)
            result_ref[rows, columns] = lax.dot_general(
                pre_ref[rows, :], weight_ref[columns, :], NT, preferred_element_type=f32
            ).astype(bf16)
        store = pltpu.make_async_copy(
            result_ref.at[pl.ds(row, ROWS)], out_ref.at[pl.ds(row, ROWS)], sems.at[row // ROWS]
        )
        store.start()
        stores.append(store)
    for store in stores:
        store.wait()


def latent_gradient(grad_pre, weight):
    nodes, width = grad_pre.shape
    return pl.pallas_call(
        latent_kernel,
        in_specs=[vmem, vmem],
        out_specs=anywhere,
        out_shape=pltpu.HBM((nodes, width), bf16),
        scratch_shapes=[pltpu.VMEM((nodes, width), bf16), pltpu.SemaphoreType.DMA((nodes // ROWS,))],
        compiler_params=params(12),
        cost_estimate=cost(2 * nodes * width * width, 10 << 20),
        name="latent_gradient",
    )(grad_pre, weight)


def finish_kernel(own_ref, *refs, factor):
    *others, first_ref, second_ref = refs
    width, variables = first_ref.shape[1], second_ref.shape[1]
    total = own_ref[...].astype(f32)
    for other in others:
        total = total + other[...].astype(f32)
    total = total * factor
    first_ref[...] = total[:, :width]
    second_ref[...] = total[:, width : width + variables]


def finish(own, others, width, variables, factor):
    rows = own.shape[0]
    return pl.pallas_call(
        functools.partial(finish_kernel, factor=factor),
        in_specs=[vmem] * (1 + len(others)),
        out_specs=[vmem] * 2,
        out_shape=[jax.ShapeDtypeStruct((rows, width), f32), jax.ShapeDtypeStruct((rows, variables), f32)],
        compiler_params=params(8),
        cost_estimate=cost(0, 1 << 20),
        name="finish",
    )(own, *others)


def moved(value, move):
    moves = []
    for member in range(8):
        for grid in range(16):
            y, x_hi, x_lo, z, core = member // 2, member % 2, grid // 8, (grid // 2) % 4, grid % 2
            y, x, z, core = move(y, x_hi * 2 + x_lo, z, core)
            target = (y * 2 + x // 2) * 16 + ((x % 2) * 4 + z) * 2 + core
            moves.append((member * 16 + grid, target))
    return lax.ppermute(value, ("member", "grid"), moves)


def summed(own, others):
    total = own.astype(f32)
    for other in others:
        total = total + other.astype(f32)
    return total


def over_core(send, keep):
    got = moved(send, lambda y, x, z, c: (y, x, z, 1 - c))
    return summed(keep, [got]).reshape(4, 64, send.shape[1])


def up(value):
    return moved(value, lambda y, x, z, c: (y, x, (z + 1) % 4, c))


def down(value):
    return moved(value, lambda y, x, z, c: (y, x, (z + 3) % 4, c))


def over_x(blocks):
    got = [
        moved(blocks[0] if k == 2 else blocks[1], lambda y, x, z, c, k=k: (y, x ^ k, z, c))
        for k in (1, 3, 2)
    ]
    return summed(blocks[0], got).astype(bf16)


def over_y(block):
    return [moved(block, lambda y, x, z, c, k=k: (y ^ k, x, z, c)) for k in (1, 3, 2)]


def body(latents, hidden_weight, output_weight, observed, node_area_weight):
    latent = latents[0]
    members = lax.axis_size("member")
    groups = lax.axis_size("grid")
    nodes, width = latent.shape
    variables = output_weight.shape[1]
    place = lax.axis_index("member").astype(jnp.int32).reshape(1)
    grid = lax.axis_index("grid").astype(jnp.int32).reshape(1)

    forecast, pre, padded = forward(latent, hidden_weight, output_weight.T)
    blocks, pre = lax.optimization_barrier(((0.25 * forecast).astype(f16), pre))
    blocks = lax.all_to_all(blocks, "member", 0, 0, tiled=True)
    hidden, slope = gates(pre)
    blocks, hidden, slope = lax.optimization_barrier((blocks, hidden, slope))
    low = pairs(place, 4.0 * blocks.astype(f32), observed, node_area_weight.reshape(1, nodes))
    low, late_grid = lax.optimization_barrier((low, grid))
    low = lax.all_to_all(low, "member", 0, 0, tiled=True)
    turned_latent = turned(late_grid, latent)
    grad_pre, rows_a, second_a, flat, turned_now = send_a(grid, low, turned_latent, slope, hidden, padded)
    kept_a, turned_now, hidden_now = keep_a(grid, turned_latent, hidden, grad_pre, turned_now, second_a)
    far_up, far_down, near_up, near_down = over_core(rows_a, kept_a).astype(bf16)
    far_up, far_down, near_up, near_down, flat = lax.optimization_barrier((far_up, far_down, near_up, near_down, flat))
    upward, downward = up(far_up), down(far_down)
    from_below, from_above = up(near_up), down(near_down)
    rows_b, second_b, turned_now = send_b(grid, turned_latent, grad_pre, flat, turned_now, hidden_now)
    kept_b, weight_copy = keep_b(hidden_weight, grad_pre, turned_now, second_b)
    above, below, own, other = over_core(rows_b, kept_b)
    above = (above + upward.astype(f32)).astype(bf16)
    below = (below + downward.astype(f32)).astype(bf16)
    above, below, grad_pre = lax.optimization_barrier((above, below, grad_pre))
    grad_latent = latent_gradient(grad_pre, weight_copy)
    own = summed(own, [up(above), from_above])
    other = summed(other, [from_below, down(below)])
    blocks = jnp.stack([own, other]).astype(bf16)
    blocks, grad_latent = lax.optimization_barrier((blocks, grad_latent))
    block = over_x(blocks)
    factor = 1.0 / math.sqrt(members * nodes * groups)
    first, second = finish(block, over_y(block), width, variables, factor)
    return grad_latent[None], first, second


def solution(mesh):
    in_specs = (P("member", "grid", None), P(), P(), P(None, "grid"), P("grid"))
    out_specs = (P("member", "grid", None), P("grid", None), P("grid", None))
    return jax.shard_map(body, mesh=mesh, in_specs=in_specs, out_specs=out_specs, check_vma=False)
```

```python
import functools
import math

import jax
import jax.numpy as jnp
from jax import lax
from jax.experimental import pallas as pl
from jax.experimental.pallas import tpu as pltpu
from jax.sharding import PartitionSpec as P

smooth_sq = 0.0025
bf16 = jnp.bfloat16
f16 = jnp.float16
f32 = jnp.float32

NT = (((1,), (1,)), ((), ()))
WIDE = 128
TALL = 112
SHARE = 256
ROWS = 512
COLS = 256

vmem = pl.BlockSpec(memory_space=pltpu.VMEM)
smem = pl.BlockSpec(memory_space=pltpu.SMEM)
anywhere = pl.BlockSpec(memory_space=pltpu.HBM)


def params(mib):
    return pltpu.CompilerParams(vmem_limit_bytes=mib * 1024 * 1024)


def cost(flops, nbytes, trans=0):
    return pl.CostEstimate(flops=flops, bytes_accessed=nbytes, transcendentals=trans)


def chunk(ref, start):
    return ref.at[pl.ds(start, ROWS)]


def forward_kernel(
    latent_ref,
    weight_ref,
    out_weight_ref,
    forecast_ref,
    pre_out,
    padded_ref,
    pre_ref,
    hidden_ref,
    latent_copy,
    weight_copy,
    out_weight_copy,
    latent_sems,
    weight_sem,
    out_weight_sem,
    pre_sems,
):
    nodes, width = latent_ref.shape
    variables = out_weight_ref.shape[0]
    weight_load = pltpu.make_async_copy(weight_ref, weight_copy, weight_sem)
    out_weight_load = pltpu.make_async_copy(out_weight_ref, out_weight_copy, out_weight_sem)
    latent_loads = [
        pltpu.make_async_copy(chunk(latent_ref, start), chunk(latent_copy, start), latent_sems.at[start // ROWS])
        for start in range(0, nodes, ROWS)
    ]
    out_weight_load.start()
    weight_load.start()
    for load in latent_loads:
        load.start()
    out_weight_load.wait()
    turned_weight = jnp.concatenate(
        [out_weight_copy[...], jnp.zeros((WIDE - variables, width), bf16)], axis=0
    )
    padded_ref[...] = turned_weight.T
    weight_load.wait()
    stores = []
    for start in range(0, nodes, ROWS):
        rows = slice(start, start + ROWS)
        latent_loads[start // ROWS].wait()
        pre = jnp.dot(latent_copy[rows, :], weight_copy[...], preferred_element_type=f32)
        pre_ref[rows, :] = pre.astype(bf16)
        hidden_ref[rows, :] = (pre * (0.5 * jnp.tanh(0.5 * pre) + 0.5)).astype(bf16)
        store = pltpu.make_async_copy(chunk(pre_ref, start), chunk(pre_out, start), pre_sems.at[start // ROWS])
        store.start()
        stores.append(store)
        for share in range(start // SHARE, (start + ROWS) // SHARE):
            forecast_ref[share] = lax.dot_general(
                turned_weight[:TALL],
                hidden_ref[share * SHARE : (share + 1) * SHARE, :],
                NT,
                preferred_element_type=f32,
            )
    for store in stores:
        store.wait()


def pinned(value):
    return pltpu.with_memory_space_constraint(value, pltpu.HBM)


def forward(latent, weight, out_weight):
    nodes, width = latent.shape
    return pl.pallas_call(
        forward_kernel,
        in_specs=[anywhere] * 3,
        out_specs=[vmem, anywhere, vmem],
        out_shape=[
            jax.ShapeDtypeStruct((nodes // SHARE, TALL, SHARE), f32),
            pltpu.HBM((nodes, width), bf16),
            jax.ShapeDtypeStruct((width, WIDE), bf16),
        ],
        scratch_shapes=[
            pltpu.VMEM((nodes, width), bf16),
            pltpu.VMEM((nodes, width), bf16),
            pltpu.VMEM((nodes, width), bf16),
            pltpu.VMEM((width, width), bf16),
            pltpu.VMEM(out_weight.shape, bf16),
            pltpu.SemaphoreType.DMA((nodes // ROWS,)),
            pltpu.SemaphoreType.DMA,
            pltpu.SemaphoreType.DMA,
            pltpu.SemaphoreType.DMA((nodes // ROWS,)),
        ],
        compiler_params=params(32),
        cost_estimate=cost(2 * nodes * width * (width + WIDE), 20 << 20),
        name="forward",
    )(pinned(latent), pinned(weight), pinned(out_weight))


def gate_kernel(pre_hbm, hidden_out, slope_out, pre_ref, hidden_ref, slope_ref, pre_sems, hidden_sems, slope_sems):
    nodes, width = pre_hbm.shape
    loads = [
        pltpu.make_async_copy(chunk(pre_hbm, start), chunk(pre_ref, start), pre_sems.at[start // ROWS])
        for start in range(0, nodes, ROWS)
    ]
    for load in loads:
        load.start()
    stores = []
    for start in range(0, nodes, ROWS):
        rows = slice(start, start + ROWS)
        loads[start // ROWS].wait()
        for group in range(width // 128):
            columns = slice(group * 128, (group + 1) * 128)
            pre = pre_ref[rows, columns].astype(f32)
            sig = 0.5 * jnp.tanh(0.5 * pre) + 0.5
            hidden = pre * sig
            hidden_ref[group, rows, :] = hidden.astype(bf16)
            slope_ref[rows, columns] = (sig + hidden * (1.0 - sig)).astype(bf16)
        for store in (
            pltpu.make_async_copy(
                hidden_ref.at[:, pl.ds(start, ROWS)], hidden_out.at[:, pl.ds(start, ROWS)], hidden_sems.at[start // ROWS]
            ),
            pltpu.make_async_copy(chunk(slope_ref, start), chunk(slope_out, start), slope_sems.at[start // ROWS]),
        ):
            store.start()
            stores.append(store)
    for store in stores:
        store.wait()


def gates(pre):
    nodes, width = pre.shape
    sems = pltpu.SemaphoreType.DMA((nodes // ROWS,))
    return pl.pallas_call(
        gate_kernel,
        in_specs=[anywhere],
        out_specs=[anywhere] * 2,
        out_shape=[pltpu.HBM((width // 128, nodes, 128), bf16), pltpu.HBM((nodes, width), bf16)],
        scratch_shapes=[
            pltpu.VMEM((nodes, width), bf16),
            pltpu.VMEM((width // 128, nodes, 128), bf16),
            pltpu.VMEM((nodes, width), bf16),
            sems,
            sems,
            sems,
        ],
        compiler_params=params(20),
        cost_estimate=cost(0, 12 << 20),
        name="gates",
    )(pinned(pre))


def slope_function(diff):
    return diff * lax.rsqrt(diff * diff + smooth_sq)


def pair_kernel(place_ref, blocks_ref, observed_ref, area_ref, low_ref, here_ref, weight_ref, totals_ref, sems):
    members = blocks_ref.shape[0]
    variables = observed_ref.shape[0]
    at = pl.multiple_of(place_ref[0] * SHARE, SHARE)
    loads = [
        pltpu.make_async_copy(observed_ref.at[:, pl.ds(at, SHARE)], here_ref, sems.at[0]),
        pltpu.make_async_copy(area_ref.at[:, pl.ds(at, SHARE)], weight_ref, sems.at[1]),
    ]
    for load in loads:
        load.start()
    for start in range(0, TALL, 16):
        rows = slice(start, start + 16)
        values = [blocks_ref[a, rows, :] for a in range(members)]
        totals = [0.0] * members
        for a in range(members):
            for b in range(a + 1, members):
                slope = slope_function(values[a] - values[b])
                totals[a] = totals[a] + slope
                totals[b] = totals[b] - slope
        for a in range(members):
            totals_ref[a, rows, :] = totals[a]
    for load in loads:
        load.wait()
    area = weight_ref[...]
    for start in range(0, TALL, 16):
        rows = slice(start, start + 16)
        real = min(16, variables - start)
        observed = here_ref[start : start + real, :]
        if real < 16:
            observed = jnp.concatenate([observed, jnp.zeros((16 - real, SHARE), f32)], axis=0)
        for a in range(members):
            own = slope_function(blocks_ref[a, rows, :] - observed)
            low_ref[a, rows, :] = (area * (own - totals_ref[a, rows, :] * (1.0 / (members - 1)))).astype(bf16)


def pairs(place, blocks, observed, area):
    members = blocks.shape[0]
    variables = observed.shape[0]
    return pl.pallas_call(
        pair_kernel,
        in_specs=[smem, vmem, anywhere, anywhere],
        out_specs=vmem,
        out_shape=jax.ShapeDtypeStruct((members, TALL, SHARE), bf16),
        scratch_shapes=[
            pltpu.VMEM((variables, SHARE), f32),
            pltpu.VMEM((1, SHARE), f32),
            pltpu.VMEM((members, TALL, SHARE), f32),
            pltpu.SemaphoreType.DMA((2,)),
        ],
        compiler_params=params(8),
        cost_estimate=cost(4 << 20, 2 << 20),
        name="pairs",
    )(place, blocks, observed, area)


def position(grid_ref):
    grid = grid_ref[0]
    return grid >> 3, (grid >> 1) & 3, grid & 1


PARTS = (((2, 0), (2, 1), (1, 1), (3, 0)), ((1, 0), (3, 1), (0, 0), (0, 1)))


def turn_kernel(grid_ref, latent_ref, turned_ref):
    nodes, width = latent_ref.shape
    x_lo, z, core = position(grid_ref)
    for group in range(8):
        step = (group - z) & 3
        other_x = (group >> 2) ^ x_lo
        odd, back = step & 1, step >> 1
        part = odd * (1 - (other_x ^ back)) + (1 - odd) * (1 - back)
        place = odd * (back + 2 * (1 - part)) + (1 - odd) * (other_x + 2 * part)
        at = part * 512 + place * 64
        first = pl.multiple_of(at + (1 - core) * 256, 64)
        second = pl.multiple_of(at + core * 256, 64)
        for row in range(0, nodes, ROWS):
            columns = slice(row, row + ROWS)
            block = latent_ref[columns, group * 128 : (group + 1) * 128].T
            turned_ref[pl.ds(first, 64), columns] = block[:64]
            turned_ref[pl.ds(second, 64), columns] = block[64:]


def turned(grid, latent):
    nodes, width = latent.shape
    return pl.pallas_call(
        turn_kernel,
        in_specs=[smem, vmem],
        out_specs=vmem,
        out_shape=jax.ShapeDtypeStruct((width, nodes), bf16),
        compiler_params=params(8),
        cost_estimate=cost(0, 8 << 20),
        name="turned",
    )(grid, latent)


def turned_load(turned_hbm, start, turned_ref, sem):
    return pltpu.make_async_copy(turned_hbm.at[pl.ds(start, 256)], turned_ref, sem)


def hidden_loads(part, grid_ref, hidden_hbm, hidden_ref, sems):
    x_lo, z, core = position(grid_ref)
    return [
        pltpu.make_async_copy(
            hidden_hbm.at[(other_x ^ x_lo) * 4 + ((z + step) & 3)], hidden_ref.at[block], sems.at[block]
        )
        for block, (step, other_x) in enumerate(PARTS[part])
    ]


def first_product(turned_ref, pre_ref, out_ref):
    width = pre_ref.shape[1]
    for column in range(0, width, 512):
        columns = slice(column, column + 512)
        part = jnp.dot(turned_ref[...], pre_ref[:, columns], preferred_element_type=f32)
        out_ref[:, columns] = part.astype(bf16)


def second_product(grid_ref, flat_ref, hidden_ref, send_ref, second_ref, scratch_ref):
    width = send_ref.shape[1] - WIDE
    core = position(grid_ref)[2]
    for block in (0, 2):
        columns = jnp.concatenate([hidden_ref[block], hidden_ref[block + 1]], axis=1)
        second = jnp.dot(flat_ref[...], columns, preferred_element_type=f32)
        scratch_ref[block * 128 : (block + 2) * 128, :] = second.T.astype(bf16)
    for block in range(4):
        rows = slice(block * 64, (block + 1) * 64)
        mine = pl.multiple_of(block * 128 + core * 64, 64)
        other = pl.multiple_of(block * 128 + (1 - core) * 64, 64)
        second_ref[rows, :] = scratch_ref[pl.ds(mine, 64), :]
        send_ref[rows, width:] = scratch_ref[pl.ds(other, 64), :]


def send_a_kernel(
    grid_ref,
    low_ref,
    turned_hbm,
    slope_hbm,
    hidden_hbm,
    padded_ref,
    pre_ref,
    send_ref,
    second_ref,
    flat_ref,
    next_turned_ref,
    turn_ref,
    turned_ref,
    hidden_ref,
    scratch_ref,
    slope_ref,
    turned_sems,
    hidden_sems,
    slope_sems,
):
    nodes, width = pre_ref.shape
    slope_loads = [
        pltpu.make_async_copy(
            slope_hbm.at[pl.ds(start, ROWS)], slope_ref.at[pl.ds(start, ROWS)], slope_sems.at[start // ROWS]
        )
        for start in range(0, nodes, ROWS)
    ]
    turned_now = turned_load(turned_hbm, 0, turned_ref, turned_sems.at[0])
    turned_next = turned_load(turned_hbm, 256, next_turned_ref, turned_sems.at[1])
    hidden_now = hidden_loads(0, grid_ref, hidden_hbm, hidden_ref, hidden_sems)
    for load in slope_loads + [turned_now] + hidden_now + [turned_next]:
        load.start()
    for share in range(low_ref.shape[0]):
        columns = slice(share * SHARE, (share + 1) * SHARE)
        low = jnp.concatenate([low_ref[share], jnp.zeros((WIDE - TALL, SHARE), bf16)], axis=0)
        flat_ref[:, columns] = low
        turn_ref[columns, :] = low.T
    for start in range(0, nodes, ROWS):
        rows = slice(start, start + ROWS)
        slope_loads[start // ROWS].wait()
        for column in range(0, width, COLS):
            columns = slice(column, column + COLS)
            grad_hidden = lax.dot_general(turn_ref[rows, :], padded_ref[columns, :], NT, preferred_element_type=f32)
            pre_ref[rows, columns] = (grad_hidden * slope_ref[rows, columns].astype(f32)).astype(bf16)
    turned_now.wait()
    first_product(turned_ref, pre_ref, send_ref)
    for load in hidden_now:
        load.wait()
    second_product(grid_ref, flat_ref, hidden_ref, send_ref, second_ref, scratch_ref)
    turned_next.wait()


def keep_a_kernel(
    grid_ref,
    turned_hbm,
    hidden_hbm,
    pre_ref,
    turned_ref,
    second_ref,
    keep_ref,
    next_turned_ref,
    next_hidden_ref,
    turned_sem,
    hidden_sems,
):
    loads = [turned_load(turned_hbm, 512, next_turned_ref, turned_sem)]
    loads += hidden_loads(1, grid_ref, hidden_hbm, next_hidden_ref, hidden_sems)
    for load in loads:
        load.start()
    first_product(turned_ref, pre_ref, keep_ref)
    keep_ref[:, pre_ref.shape[1] :] = second_ref[...]
    for load in loads:
        load.wait()


def send_b_kernel(
    grid_ref,
    turned_hbm,
    pre_ref,
    flat_ref,
    turned_ref,
    hidden_ref,
    send_ref,
    second_ref,
    next_turned_ref,
    scratch_ref,
    turned_sem,
):
    load = turned_load(turned_hbm, 768, next_turned_ref, turned_sem)
    load.start()
    first_product(turned_ref, pre_ref, send_ref)
    second_product(grid_ref, flat_ref, hidden_ref, send_ref, second_ref, scratch_ref)
    load.wait()


def keep_b_kernel(weight_hbm, pre_ref, turned_ref, second_ref, keep_ref, weight_ref, weight_sem):
    load = pltpu.make_async_copy(weight_hbm, weight_ref, weight_sem)
    load.start()
    first_product(turned_ref, pre_ref, keep_ref)
    keep_ref[:, pre_ref.shape[1] :] = second_ref[...]
    load.wait()


def shape(*dims):
    return jax.ShapeDtypeStruct(dims, bf16)


def send_a(grid, low, turned_latent, slope, hidden, padded):
    nodes, width = slope.shape
    return pl.pallas_call(
        send_a_kernel,
        in_specs=[smem, vmem, anywhere, anywhere, anywhere, vmem],
        out_specs=[vmem] * 5,
        out_shape=[
            shape(nodes, width),
            shape(256, width + WIDE),
            shape(256, WIDE),
            shape(WIDE, nodes),
            shape(256, nodes),
        ],
        scratch_shapes=[
            pltpu.VMEM((nodes, WIDE), bf16),
            pltpu.VMEM((256, nodes), bf16),
            pltpu.VMEM((4, nodes, 128), bf16),
            pltpu.VMEM((512, WIDE), bf16),
            pltpu.VMEM((nodes, width), bf16),
            pltpu.SemaphoreType.DMA((2,)),
            pltpu.SemaphoreType.DMA((4,)),
            pltpu.SemaphoreType.DMA((nodes // ROWS,)),
        ],
        compiler_params=params(20),
        cost_estimate=cost(nodes * width * (width // 2 + 3 * WIDE), 8 << 20),
        name="send_a",
    )(grid, low, pinned(turned_latent), pinned(slope), pinned(hidden), padded)


def keep_a(grid, turned_latent, hidden, grad_pre, turned_now, second):
    nodes, width = grad_pre.shape
    return pl.pallas_call(
        keep_a_kernel,
        in_specs=[smem, anywhere, anywhere] + [vmem] * 3,
        out_specs=[vmem] * 3,
        out_shape=[shape(256, width + WIDE), shape(256, nodes), shape(4, nodes, 128)],
        scratch_shapes=[pltpu.SemaphoreType.DMA, pltpu.SemaphoreType.DMA((4,))],
        compiler_params=params(12),
        cost_estimate=cost(nodes * width * width // 2, 4 << 20),
        name="keep_a",
    )(grid, pinned(turned_latent), pinned(hidden), grad_pre, turned_now, second)


def send_b(grid, turned_latent, grad_pre, flat, turned_now, hidden_now):
    nodes, width = grad_pre.shape
    return pl.pallas_call(
        send_b_kernel,
        in_specs=[smem, anywhere] + [vmem] * 4,
        out_specs=[vmem] * 3,
        out_shape=[shape(256, width + WIDE), shape(256, WIDE), shape(256, nodes)],
        scratch_shapes=[pltpu.VMEM((512, WIDE), bf16), pltpu.SemaphoreType.DMA],
        compiler_params=params(12),
        cost_estimate=cost(nodes * width * width // 2, 4 << 20),
        name="send_b",
    )(grid, pinned(turned_latent), grad_pre, flat, turned_now, hidden_now)


def keep_b(weight, grad_pre, turned_now, second):
    nodes, width = grad_pre.shape
    return pl.pallas_call(
        keep_b_kernel,
        in_specs=[anywhere] + [vmem] * 3,
        out_specs=[vmem] * 2,
        out_shape=[shape(256, width + WIDE), shape(width, width)],
        scratch_shapes=[pltpu.SemaphoreType.DMA],
        compiler_params=params(12),
        cost_estimate=cost(nodes * width * width // 2, 4 << 20),
        name="keep_b",
    )(pinned(weight), grad_pre, turned_now, second)


def latent_kernel(pre_ref, weight_ref, *refs, begin):
    out_ref, result_ref, sems = refs[-3:]
    width = pre_ref.shape[1]
    stores = []
    for row in range(0, result_ref.shape[0], ROWS):
        rows = slice(begin + row, begin + row + ROWS)
        for start in range(0, width, COLS):
            columns = slice(start, start + COLS)
            result_ref[row : row + ROWS, columns] = lax.dot_general(
                pre_ref[rows, :], weight_ref[columns, :], NT, preferred_element_type=f32
            ).astype(bf16)
        store = pltpu.make_async_copy(
            result_ref.at[pl.ds(row, ROWS)], out_ref.at[pl.ds(begin + row, ROWS)], sems.at[row // ROWS]
        )
        store.start()
        stores.append(store)
    for store in stores:
        store.wait()


def latent_gradient(grad_pre, weight, begin, so_far=None):
    nodes, width = grad_pre.shape
    half = nodes // 2
    more = [] if so_far is None else [so_far]
    return pl.pallas_call(
        functools.partial(latent_kernel, begin=begin),
        in_specs=[vmem, vmem] + [anywhere] * len(more),
        out_specs=anywhere,
        out_shape=pltpu.HBM((nodes, width), bf16),
        input_output_aliases={2: 0} if more else {},
        scratch_shapes=[pltpu.VMEM((half, width), bf16), pltpu.SemaphoreType.DMA((half // ROWS,))],
        compiler_params=params(12),
        cost_estimate=cost(nodes * width * width, 5 << 20),
        name="latent_gradient",
    )(grad_pre, weight, *more)


def finish_kernel(own_ref, *refs, factor):
    *others, first_ref, second_ref = refs
    width, variables = first_ref.shape[1], second_ref.shape[1]
    total = own_ref[...].astype(f32)
    for other in others:
        total = total + other[...].astype(f32)
    total = total * factor
    first_ref[...] = total[:, :width]
    second_ref[...] = total[:, width : width + variables]


def finish(own, others, width, variables, factor):
    rows = own.shape[0]
    return pl.pallas_call(
        functools.partial(finish_kernel, factor=factor),
        in_specs=[vmem] * (1 + len(others)),
        out_specs=[vmem] * 2,
        out_shape=[jax.ShapeDtypeStruct((rows, width), f32), jax.ShapeDtypeStruct((rows, variables), f32)],
        compiler_params=params(8),
        cost_estimate=cost(0, 1 << 20),
        name="finish",
    )(own, *others)


def moved(value, move):
    moves = []
    for member in range(8):
        for grid in range(16):
            y, x_hi, x_lo, z, core = member // 2, member % 2, grid // 8, (grid // 2) % 4, grid % 2
            y, x, z, core = move(y, x_hi * 2 + x_lo, z, core)
            target = (y * 2 + x // 2) * 16 + ((x % 2) * 4 + z) * 2 + core
            moves.append((member * 16 + grid, target))
    return lax.ppermute(value, ("member", "grid"), moves)


def summed(own, others):
    total = own.astype(f32)
    for other in others:
        total = total + other.astype(f32)
    return total


def over_core(send, keep):
    got = moved(send, lambda y, x, z, c: (y, x, z, 1 - c))
    return summed(keep, [got]).reshape(4, 64, send.shape[1])


def up(value):
    return moved(value, lambda y, x, z, c: (y, x, (z + 1) % 4, c))


def down(value):
    return moved(value, lambda y, x, z, c: (y, x, (z + 3) % 4, c))


def over_x(blocks):
    got = [
        moved(blocks[0] if k == 2 else blocks[1], lambda y, x, z, c, k=k: (y, x ^ k, z, c))
        for k in (1, 3, 2)
    ]
    return summed(blocks[0], got).astype(bf16)


def over_y(block):
    return [moved(block, lambda y, x, z, c, k=k: (y ^ k, x, z, c)) for k in (1, 3, 2)]


def body(latents, hidden_weight, output_weight, observed, node_area_weight):
    latent = latents[0]
    members = lax.axis_size("member")
    groups = lax.axis_size("grid")
    nodes, width = latent.shape
    variables = output_weight.shape[1]
    place = lax.axis_index("member").astype(jnp.int32).reshape(1)
    grid = lax.axis_index("grid").astype(jnp.int32).reshape(1)

    forecast, pre, padded = forward(latent, hidden_weight, output_weight.T)
    blocks, pre = lax.optimization_barrier(((0.25 * forecast).astype(f16), pre))
    blocks = lax.all_to_all(blocks, "member", 0, 0, tiled=True)
    hidden, slope = gates(pre)
    blocks, hidden, slope = lax.optimization_barrier((blocks, hidden, slope))
    low = pairs(place, 4.0 * blocks.astype(f32), observed, node_area_weight.reshape(1, nodes))
    low, late_grid = lax.optimization_barrier((low, grid))
    low = lax.all_to_all(low, "member", 0, 0, tiled=True)
    turned_latent = turned(late_grid, latent)
    grad_pre, rows_a, second_a, flat, turned_now = send_a(grid, low, turned_latent, slope, hidden, padded)
    kept_a, turned_now, hidden_now = keep_a(grid, turned_latent, hidden, grad_pre, turned_now, second_a)
    far_up, far_down, near_up, near_down = over_core(rows_a, kept_a).astype(bf16)
    far_up, far_down, near_up, near_down, flat = lax.optimization_barrier((far_up, far_down, near_up, near_down, flat))
    upward, downward = up(far_up), down(far_down)
    from_below, from_above = up(near_up), down(near_down)
    rows_b, second_b, turned_now = send_b(grid, turned_latent, grad_pre, flat, turned_now, hidden_now)
    kept_b, weight_copy = keep_b(hidden_weight, grad_pre, turned_now, second_b)
    above, below, own, other = over_core(rows_b, kept_b)
    above = (above + upward.astype(f32)).astype(bf16)
    below = (below + downward.astype(f32)).astype(bf16)
    above, below, grad_pre = lax.optimization_barrier((above, below, grad_pre))
    grad_latent = latent_gradient(grad_pre, weight_copy, 0)
    own = summed(own, [up(above), from_above])
    other = summed(other, [from_below, down(below)])
    blocks = jnp.stack([own, other]).astype(bf16)
    blocks, grad_latent = lax.optimization_barrier((blocks, grad_latent))
    grad_latent = latent_gradient(grad_pre, weight_copy, nodes // 2, grad_latent)
    block, grad_latent = lax.optimization_barrier((over_x(blocks), grad_latent))
    factor = 1.0 / math.sqrt(members * nodes * groups)
    first, second = finish(block, over_y(block), width, variables, factor)
    return grad_latent[None], first, second


def solution(mesh):
    in_specs = (P("member", "grid", None), P(), P(), P(None, "grid"), P("grid"))
    out_specs = (P("member", "grid", None), P("grid", None), P("grid", None))
    return jax.shard_map(body, mesh=mesh, in_specs=in_specs, out_specs=out_specs, check_vma=False)
```

```python
import functools
import math

import jax
import jax.numpy as jnp
from jax import lax
from jax.experimental import pallas as pl
from jax.experimental.pallas import tpu as pltpu
from jax.sharding import PartitionSpec as P

smooth_sq = 0.0025
bf16 = jnp.bfloat16
f16 = jnp.float16
f32 = jnp.float32

NT = (((1,), (1,)), ((), ()))
WIDE = 128
TALL = 112
SHARE = 256
ROWS = 512
COLS = 256

vmem = pl.BlockSpec(memory_space=pltpu.VMEM)
smem = pl.BlockSpec(memory_space=pltpu.SMEM)
anywhere = pl.BlockSpec(memory_space=pltpu.HBM)


def params(mib):
    return pltpu.CompilerParams(vmem_limit_bytes=mib * 1024 * 1024)


def cost(flops, nbytes, trans=0):
    return pl.CostEstimate(flops=flops, bytes_accessed=nbytes, transcendentals=trans)


def chunk(ref, start):
    return ref.at[pl.ds(start, ROWS)]


def forward_kernel(
    latent_ref,
    weight_ref,
    out_weight_ref,
    forecast_ref,
    pre_out,
    padded_ref,
    pre_ref,
    hidden_ref,
    latent_copy,
    weight_copy,
    out_weight_copy,
    latent_sems,
    weight_sem,
    out_weight_sem,
    pre_sems,
):
    nodes, width = latent_ref.shape
    variables = out_weight_ref.shape[0]
    weight_load = pltpu.make_async_copy(weight_ref, weight_copy, weight_sem)
    out_weight_load = pltpu.make_async_copy(out_weight_ref, out_weight_copy, out_weight_sem)
    latent_loads = [
        pltpu.make_async_copy(chunk(latent_ref, start), chunk(latent_copy, start), latent_sems.at[start // ROWS])
        for start in range(0, nodes, ROWS)
    ]
    out_weight_load.start()
    weight_load.start()
    for load in latent_loads:
        load.start()
    out_weight_load.wait()
    turned_weight = jnp.concatenate(
        [out_weight_copy[...], jnp.zeros((WIDE - variables, width), bf16)], axis=0
    )
    padded_ref[...] = turned_weight.T
    weight_load.wait()
    stores = []
    for start in range(0, nodes, ROWS):
        rows = slice(start, start + ROWS)
        latent_loads[start // ROWS].wait()
        pre = jnp.dot(latent_copy[rows, :], weight_copy[...], preferred_element_type=f32)
        pre_ref[rows, :] = pre.astype(bf16)
        hidden_ref[rows, :] = (pre * (0.5 * jnp.tanh(0.5 * pre) + 0.5)).astype(bf16)
        store = pltpu.make_async_copy(chunk(pre_ref, start), chunk(pre_out, start), pre_sems.at[start // ROWS])
        store.start()
        stores.append(store)
        for share in range(start // SHARE, (start + ROWS) // SHARE):
            forecast_ref[share] = lax.dot_general(
                turned_weight[:TALL],
                hidden_ref[share * SHARE : (share + 1) * SHARE, :],
                NT,
                preferred_element_type=f32,
            )
    for store in stores:
        store.wait()


def pinned(value):
    return pltpu.with_memory_space_constraint(value, pltpu.HBM)


def forward(latent, weight, out_weight):
    nodes, width = latent.shape
    return pl.pallas_call(
        forward_kernel,
        in_specs=[anywhere] * 3,
        out_specs=[vmem, anywhere, vmem],
        out_shape=[
            jax.ShapeDtypeStruct((nodes // SHARE, TALL, SHARE), f32),
            pltpu.HBM((nodes, width), bf16),
            jax.ShapeDtypeStruct((width, WIDE), bf16),
        ],
        scratch_shapes=[
            pltpu.VMEM((nodes, width), bf16),
            pltpu.VMEM((nodes, width), bf16),
            pltpu.VMEM((nodes, width), bf16),
            pltpu.VMEM((width, width), bf16),
            pltpu.VMEM(out_weight.shape, bf16),
            pltpu.SemaphoreType.DMA((nodes // ROWS,)),
            pltpu.SemaphoreType.DMA,
            pltpu.SemaphoreType.DMA,
            pltpu.SemaphoreType.DMA((nodes // ROWS,)),
        ],
        compiler_params=params(32),
        cost_estimate=cost(2 * nodes * width * (width + WIDE), 20 << 20),
        name="forward",
    )(pinned(latent), pinned(weight), pinned(out_weight))


def gate_kernel(pre_hbm, hidden_out, slope_out, pre_ref, hidden_ref, slope_ref, pre_sems, hidden_sems, slope_sems):
    nodes, width = pre_hbm.shape
    loads = [
        pltpu.make_async_copy(chunk(pre_hbm, start), chunk(pre_ref, start), pre_sems.at[start // ROWS])
        for start in range(0, nodes, ROWS)
    ]
    for load in loads:
        load.start()
    stores = []
    for start in range(0, nodes, ROWS):
        rows = slice(start, start + ROWS)
        loads[start // ROWS].wait()
        for group in range(width // 128):
            columns = slice(group * 128, (group + 1) * 128)
            pre = pre_ref[rows, columns].astype(f32)
            sig = 0.5 * jnp.tanh(0.5 * pre) + 0.5
            hidden = pre * sig
            hidden_ref[group, rows, :] = hidden.astype(bf16)
            slope_ref[rows, columns] = (sig + hidden * (1.0 - sig)).astype(bf16)
        for store in (
            pltpu.make_async_copy(
                hidden_ref.at[:, pl.ds(start, ROWS)], hidden_out.at[:, pl.ds(start, ROWS)], hidden_sems.at[start // ROWS]
            ),
            pltpu.make_async_copy(chunk(slope_ref, start), chunk(slope_out, start), slope_sems.at[start // ROWS]),
        ):
            store.start()
            stores.append(store)
    for store in stores:
        store.wait()


def gates(pre):
    nodes, width = pre.shape
    sems = pltpu.SemaphoreType.DMA((nodes // ROWS,))
    return pl.pallas_call(
        gate_kernel,
        in_specs=[anywhere],
        out_specs=[anywhere] * 2,
        out_shape=[pltpu.HBM((width // 128, nodes, 128), bf16), pltpu.HBM((nodes, width), bf16)],
        scratch_shapes=[
            pltpu.VMEM((nodes, width), bf16),
            pltpu.VMEM((width // 128, nodes, 128), bf16),
            pltpu.VMEM((nodes, width), bf16),
            sems,
            sems,
            sems,
        ],
        compiler_params=params(20),
        cost_estimate=cost(0, 12 << 20),
        name="gates",
    )(pinned(pre))


def slope_function(diff):
    return diff * lax.rsqrt(diff * diff + smooth_sq)


def pair_kernel(place_ref, blocks_ref, observed_ref, area_ref, low_ref, here_ref, weight_ref, totals_ref, sems):
    members = blocks_ref.shape[0]
    variables = observed_ref.shape[0]
    at = pl.multiple_of(place_ref[0] * SHARE, SHARE)
    loads = [
        pltpu.make_async_copy(observed_ref.at[:, pl.ds(at, SHARE)], here_ref, sems.at[0]),
        pltpu.make_async_copy(area_ref.at[:, pl.ds(at, SHARE)], weight_ref, sems.at[1]),
    ]
    for load in loads:
        load.start()
    for start in range(0, TALL, 16):
        rows = slice(start, start + 16)
        values = [blocks_ref[a, rows, :] for a in range(members)]
        totals = [0.0] * members
        for a in range(members):
            for b in range(a + 1, members):
                slope = slope_function(values[a] - values[b])
                totals[a] = totals[a] + slope
                totals[b] = totals[b] - slope
        for a in range(members):
            totals_ref[a, rows, :] = totals[a]
    for load in loads:
        load.wait()
    area = weight_ref[...]
    for start in range(0, TALL, 16):
        rows = slice(start, start + 16)
        real = min(16, variables - start)
        observed = here_ref[start : start + real, :]
        if real < 16:
            observed = jnp.concatenate([observed, jnp.zeros((16 - real, SHARE), f32)], axis=0)
        for a in range(members):
            own = slope_function(blocks_ref[a, rows, :] - observed)
            low_ref[a, rows, :] = (area * (own - totals_ref[a, rows, :] * (1.0 / (members - 1)))).astype(bf16)


def pairs(place, blocks, observed, area):
    members = blocks.shape[0]
    variables = observed.shape[0]
    return pl.pallas_call(
        pair_kernel,
        in_specs=[smem, vmem, anywhere, anywhere],
        out_specs=vmem,
        out_shape=jax.ShapeDtypeStruct((members, TALL, SHARE), bf16),
        scratch_shapes=[
            pltpu.VMEM((variables, SHARE), f32),
            pltpu.VMEM((1, SHARE), f32),
            pltpu.VMEM((members, TALL, SHARE), f32),
            pltpu.SemaphoreType.DMA((2,)),
        ],
        compiler_params=params(8),
        cost_estimate=cost(4 << 20, 2 << 20),
        name="pairs",
    )(place, blocks, observed, area)


def position(grid_ref):
    grid = grid_ref[0]
    return grid >> 3, (grid >> 1) & 3, grid & 1


PARTS = (((2, 0), (2, 1), (1, 1), (3, 0)), ((1, 0), (3, 1), (0, 0), (0, 1)))


def turn_kernel(grid_ref, latent_ref, turned_ref):
    nodes, width = latent_ref.shape
    x_lo, z, core = position(grid_ref)
    for group in range(8):
        step = (group - z) & 3
        other_x = (group >> 2) ^ x_lo
        odd, back = step & 1, step >> 1
        part = odd * (1 - (other_x ^ back)) + (1 - odd) * (1 - back)
        place = odd * (back + 2 * (1 - part)) + (1 - odd) * (other_x + 2 * part)
        at = part * 512 + place * 64
        first = pl.multiple_of(at + (1 - core) * 256, 64)
        second = pl.multiple_of(at + core * 256, 64)
        for row in range(0, nodes, ROWS):
            columns = slice(row, row + ROWS)
            block = latent_ref[columns, group * 128 : (group + 1) * 128].T
            turned_ref[pl.ds(first, 64), columns] = block[:64]
            turned_ref[pl.ds(second, 64), columns] = block[64:]


def turned(grid, latent):
    nodes, width = latent.shape
    return pl.pallas_call(
        turn_kernel,
        in_specs=[smem, vmem],
        out_specs=vmem,
        out_shape=jax.ShapeDtypeStruct((width, nodes), bf16),
        compiler_params=params(8),
        cost_estimate=cost(0, 8 << 20),
        name="turned",
    )(grid, latent)


def turned_load(turned_hbm, start, turned_ref, sem):
    return pltpu.make_async_copy(turned_hbm.at[pl.ds(start, 256)], turned_ref, sem)


def hidden_loads(part, grid_ref, hidden_hbm, hidden_ref, sems):
    x_lo, z, core = position(grid_ref)
    return [
        pltpu.make_async_copy(
            hidden_hbm.at[(other_x ^ x_lo) * 4 + ((z + step) & 3)], hidden_ref.at[block], sems.at[block]
        )
        for block, (step, other_x) in enumerate(PARTS[part])
    ]


def first_product(turned_ref, pre_ref, out_ref):
    width = pre_ref.shape[1]
    for column in range(0, width, 512):
        columns = slice(column, column + 512)
        part = jnp.dot(turned_ref[...], pre_ref[:, columns], preferred_element_type=f32)
        out_ref[:, columns] = part.astype(bf16)


def second_product(grid_ref, flat_ref, hidden_ref, send_ref, second_ref, scratch_ref):
    width = send_ref.shape[1] - WIDE
    core = position(grid_ref)[2]
    for block in (0, 2):
        columns = jnp.concatenate([hidden_ref[block], hidden_ref[block + 1]], axis=1)
        second = jnp.dot(flat_ref[...], columns, preferred_element_type=f32)
        scratch_ref[block * 128 : (block + 2) * 128, :] = second.T.astype(bf16)
    for block in range(4):
        rows = slice(block * 64, (block + 1) * 64)
        mine = pl.multiple_of(block * 128 + core * 64, 64)
        other = pl.multiple_of(block * 128 + (1 - core) * 64, 64)
        second_ref[rows, :] = scratch_ref[pl.ds(mine, 64), :]
        send_ref[rows, width:] = scratch_ref[pl.ds(other, 64), :]


def send_a_kernel(
    grid_ref,
    low_ref,
    turned_hbm,
    slope_hbm,
    hidden_hbm,
    padded_ref,
    pre_ref,
    send_ref,
    second_ref,
    flat_ref,
    next_turned_ref,
    turn_ref,
    turned_ref,
    hidden_ref,
    scratch_ref,
    slope_ref,
    turned_sems,
    hidden_sems,
    slope_sems,
):
    nodes, width = pre_ref.shape
    slope_loads = [
        pltpu.make_async_copy(
            slope_hbm.at[pl.ds(start, ROWS)], slope_ref.at[pl.ds(start, ROWS)], slope_sems.at[start // ROWS]
        )
        for start in range(0, nodes, ROWS)
    ]
    turned_now = turned_load(turned_hbm, 0, turned_ref, turned_sems.at[0])
    turned_next = turned_load(turned_hbm, 256, next_turned_ref, turned_sems.at[1])
    hidden_now = hidden_loads(0, grid_ref, hidden_hbm, hidden_ref, hidden_sems)
    for load in slope_loads + [turned_now] + hidden_now + [turned_next]:
        load.start()
    for share in range(low_ref.shape[0]):
        columns = slice(share * SHARE, (share + 1) * SHARE)
        low = jnp.concatenate([low_ref[share], jnp.zeros((WIDE - TALL, SHARE), bf16)], axis=0)
        flat_ref[:, columns] = low
        turn_ref[columns, :] = low.T
    for start in range(0, nodes, ROWS):
        rows = slice(start, start + ROWS)
        slope_loads[start // ROWS].wait()
        for column in range(0, width, COLS):
            columns = slice(column, column + COLS)
            grad_hidden = lax.dot_general(turn_ref[rows, :], padded_ref[columns, :], NT, preferred_element_type=f32)
            pre_ref[rows, columns] = (grad_hidden * slope_ref[rows, columns].astype(f32)).astype(bf16)
    turned_now.wait()
    first_product(turned_ref, pre_ref, send_ref)
    for load in hidden_now:
        load.wait()
    second_product(grid_ref, flat_ref, hidden_ref, send_ref, second_ref, scratch_ref)
    turned_next.wait()


def keep_a_kernel(
    grid_ref,
    turned_hbm,
    hidden_hbm,
    pre_ref,
    turned_ref,
    second_ref,
    keep_ref,
    next_turned_ref,
    next_hidden_ref,
    turned_sem,
    hidden_sems,
):
    loads = [turned_load(turned_hbm, 512, next_turned_ref, turned_sem)]
    loads += hidden_loads(1, grid_ref, hidden_hbm, next_hidden_ref, hidden_sems)
    for load in loads:
        load.start()
    first_product(turned_ref, pre_ref, keep_ref)
    keep_ref[:, pre_ref.shape[1] :] = second_ref[...]
    for load in loads:
        load.wait()


def send_b_kernel(
    grid_ref,
    turned_hbm,
    pre_ref,
    flat_ref,
    turned_ref,
    hidden_ref,
    send_ref,
    second_ref,
    next_turned_ref,
    scratch_ref,
    turned_sem,
):
    load = turned_load(turned_hbm, 768, next_turned_ref, turned_sem)
    load.start()
    first_product(turned_ref, pre_ref, send_ref)
    second_product(grid_ref, flat_ref, hidden_ref, send_ref, second_ref, scratch_ref)
    load.wait()


def keep_b_kernel(weight_hbm, pre_ref, turned_ref, second_ref, keep_ref, weight_ref, weight_sem):
    load = pltpu.make_async_copy(weight_hbm, weight_ref, weight_sem)
    load.start()
    first_product(turned_ref, pre_ref, keep_ref)
    keep_ref[:, pre_ref.shape[1] :] = second_ref[...]
    load.wait()


def shape(*dims):
    return jax.ShapeDtypeStruct(dims, bf16)


def send_a(grid, low, turned_latent, slope, hidden, padded):
    nodes, width = slope.shape
    return pl.pallas_call(
        send_a_kernel,
        in_specs=[smem, vmem, anywhere, anywhere, anywhere, vmem],
        out_specs=[vmem] * 5,
        out_shape=[
            shape(nodes, width),
            shape(256, width + WIDE),
            shape(256, WIDE),
            shape(WIDE, nodes),
            shape(256, nodes),
        ],
        scratch_shapes=[
            pltpu.VMEM((nodes, WIDE), bf16),
            pltpu.VMEM((256, nodes), bf16),
            pltpu.VMEM((4, nodes, 128), bf16),
            pltpu.VMEM((512, WIDE), bf16),
            pltpu.VMEM((nodes, width), bf16),
            pltpu.SemaphoreType.DMA((2,)),
            pltpu.SemaphoreType.DMA((4,)),
            pltpu.SemaphoreType.DMA((nodes // ROWS,)),
        ],
        compiler_params=params(20),
        cost_estimate=cost(nodes * width * (width // 2 + 3 * WIDE), 8 << 20),
        name="send_a",
    )(grid, low, pinned(turned_latent), pinned(slope), pinned(hidden), padded)


def keep_a(grid, turned_latent, hidden, grad_pre, turned_now, second):
    nodes, width = grad_pre.shape
    return pl.pallas_call(
        keep_a_kernel,
        in_specs=[smem, anywhere, anywhere] + [vmem] * 3,
        out_specs=[vmem] * 3,
        out_shape=[shape(256, width + WIDE), shape(256, nodes), shape(4, nodes, 128)],
        scratch_shapes=[pltpu.SemaphoreType.DMA, pltpu.SemaphoreType.DMA((4,))],
        compiler_params=params(12),
        cost_estimate=cost(nodes * width * width // 2, 4 << 20),
        name="keep_a",
    )(grid, pinned(turned_latent), pinned(hidden), grad_pre, turned_now, second)


def send_b(grid, turned_latent, grad_pre, flat, turned_now, hidden_now):
    nodes, width = grad_pre.shape
    return pl.pallas_call(
        send_b_kernel,
        in_specs=[smem, anywhere] + [vmem] * 4,
        out_specs=[vmem] * 3,
        out_shape=[shape(256, width + WIDE), shape(256, WIDE), shape(256, nodes)],
        scratch_shapes=[pltpu.VMEM((512, WIDE), bf16), pltpu.SemaphoreType.DMA],
        compiler_params=params(12),
        cost_estimate=cost(nodes * width * width // 2, 4 << 20),
        name="send_b",
    )(grid, pinned(turned_latent), grad_pre, flat, turned_now, hidden_now)


def keep_b(weight, grad_pre, turned_now, second):
    nodes, width = grad_pre.shape
    return pl.pallas_call(
        keep_b_kernel,
        in_specs=[anywhere] + [vmem] * 3,
        out_specs=[vmem] * 2,
        out_shape=[shape(256, width + WIDE), shape(width, width)],
        scratch_shapes=[pltpu.SemaphoreType.DMA],
        compiler_params=params(12),
        cost_estimate=cost(nodes * width * width // 2, 4 << 20),
        name="keep_b",
    )(pinned(weight), grad_pre, turned_now, second)


def latent_kernel(pre_ref, weight_ref, *refs, begin):
    out_ref, result_ref, sems = refs[-3:]
    width = pre_ref.shape[1]
    stores = []
    for row in range(0, result_ref.shape[0], ROWS):
        rows = slice(begin + row, begin + row + ROWS)
        for start in range(0, width, COLS):
            columns = slice(start, start + COLS)
            result_ref[row : row + ROWS, columns] = lax.dot_general(
                pre_ref[rows, :], weight_ref[columns, :], NT, preferred_element_type=f32
            ).astype(bf16)
        store = pltpu.make_async_copy(
            result_ref.at[pl.ds(row, ROWS)], out_ref.at[pl.ds(begin + row, ROWS)], sems.at[row // ROWS]
        )
        store.start()
        stores.append(store)
    for store in stores:
        store.wait()


def latent_gradient(grad_pre, weight, begin, so_far=None):
    nodes, width = grad_pre.shape
    half = nodes // 2
    more = [] if so_far is None else [so_far]
    return pl.pallas_call(
        functools.partial(latent_kernel, begin=begin),
        in_specs=[vmem, vmem] + [anywhere] * len(more),
        out_specs=anywhere,
        out_shape=pltpu.HBM((nodes, width), bf16),
        input_output_aliases={2: 0} if more else {},
        scratch_shapes=[pltpu.VMEM((half, width), bf16), pltpu.SemaphoreType.DMA((half // ROWS,))],
        compiler_params=params(12),
        cost_estimate=cost(nodes * width * width, 5 << 20),
        name="latent_gradient",
    )(grad_pre, weight, *more)


def finish_kernel(own_ref, *refs, factor):
    *others, first_ref, second_ref = refs
    width, variables = first_ref.shape[1], second_ref.shape[1]
    total = own_ref[...].astype(f32)
    for other in others:
        total = total + other[...].astype(f32)
    total = total * factor
    first_ref[...] = total[:, :width]
    second_ref[...] = total[:, width : width + variables]


def finish(own, others, width, variables, factor):
    rows = own.shape[0]
    return pl.pallas_call(
        functools.partial(finish_kernel, factor=factor),
        in_specs=[vmem] * (1 + len(others)),
        out_specs=[vmem] * 2,
        out_shape=[jax.ShapeDtypeStruct((rows, width), f32), jax.ShapeDtypeStruct((rows, variables), f32)],
        compiler_params=params(8),
        cost_estimate=cost(0, 1 << 20),
        name="finish",
    )(own, *others)


def moved(value, move):
    moves = []
    for member in range(8):
        for grid in range(16):
            y, x_hi, x_lo, z, core = member // 2, member % 2, grid // 8, (grid // 2) % 4, grid % 2
            y, x, z, core = move(y, x_hi * 2 + x_lo, z, core)
            target = (y * 2 + x // 2) * 16 + ((x % 2) * 4 + z) * 2 + core
            moves.append((member * 16 + grid, target))
    return lax.ppermute(value, ("member", "grid"), moves)


def summed(own, others):
    total = own.astype(f32)
    for other in others:
        total = total + other.astype(f32)
    return total


def over_core(send, keep):
    got = moved(send, lambda y, x, z, c: (y, x, z, 1 - c))
    return summed(keep, [got]).reshape(4, 64, send.shape[1])


def up(value):
    return moved(value, lambda y, x, z, c: (y, x, (z + 1) % 4, c))


def down(value):
    return moved(value, lambda y, x, z, c: (y, x, (z + 3) % 4, c))


def over_x(blocks):
    got = [
        moved(blocks[0] if k == 2 else blocks[1], lambda y, x, z, c, k=k: (y, x ^ k, z, c))
        for k in (1, 3, 2)
    ]
    return summed(blocks[0], got).astype(bf16)


def over_y(block):
    return [moved(block, lambda y, x, z, c, k=k: (y ^ k, x, z, c)) for k in (1, 3, 2)]


def body(latents, hidden_weight, output_weight, observed, node_area_weight):
    latent = latents[0]
    members = lax.axis_size("member")
    groups = lax.axis_size("grid")
    nodes, width = latent.shape
    variables = output_weight.shape[1]
    place = lax.axis_index("member").astype(jnp.int32).reshape(1)
    grid = lax.axis_index("grid").astype(jnp.int32).reshape(1)

    forecast, pre, padded = forward(latent, hidden_weight, output_weight.T)
    blocks, pre = lax.optimization_barrier(((0.25 * forecast).astype(f16), pre))
    blocks = lax.all_to_all(blocks, "member", 0, 0, tiled=True)
    hidden, slope = gates(pre)
    blocks, hidden, slope = lax.optimization_barrier((blocks, hidden, slope))
    low = pairs(place, 4.0 * blocks.astype(f32), observed, node_area_weight.reshape(1, nodes))
    low, late_grid = lax.optimization_barrier((low, grid))
    low = lax.all_to_all(low, "member", 0, 0, tiled=True)
    turned_latent = turned(late_grid, latent)
    grad_pre, rows_a, second_a, flat, turned_now = send_a(grid, low, turned_latent, slope, hidden, padded)
    kept_a, turned_now, hidden_now = keep_a(grid, turned_latent, hidden, grad_pre, turned_now, second_a)
    far_up, far_down, near_up, near_down = over_core(rows_a, kept_a).astype(bf16)
    far_up, far_down, near_up, near_down, flat = lax.optimization_barrier((far_up, far_down, near_up, near_down, flat))
    upward, downward = up(far_up), down(far_down)
    from_below, from_above = up(near_up), down(near_down)
    rows_b, second_b, turned_now = send_b(grid, turned_latent, grad_pre, flat, turned_now, hidden_now)
    kept_b, weight_copy = keep_b(hidden_weight, grad_pre, turned_now, second_b)
    above, below, own, other = over_core(rows_b, kept_b)
    above = (above + upward.astype(f32)).astype(bf16)
    below = (below + downward.astype(f32)).astype(bf16)
    above, below, grad_pre = lax.optimization_barrier((above, below, grad_pre))
    grad_latent = latent_gradient(grad_pre, weight_copy, 0)
    own = summed(own, [up(above), from_above])
    other = summed(other, [from_below, down(below)])
    blocks = jnp.stack([own, other]).astype(bf16)
    blocks, grad_latent = lax.optimization_barrier((blocks, grad_latent))
    block, grad_latent = lax.optimization_barrier((over_x(blocks), grad_latent))
    others = over_y(block)
    grad_latent = latent_gradient(grad_pre, weight_copy, nodes // 2, grad_latent)
    *others, grad_latent = lax.optimization_barrier((*others, grad_latent))
    factor = 1.0 / math.sqrt(members * nodes * groups)
    first, second = finish(block, others, width, variables, factor)
    return grad_latent[None], first, second


def solution(mesh):
    in_specs = (P("member", "grid", None), P(), P(), P(None, "grid"), P("grid"))
    out_specs = (P("member", "grid", None), P("grid", None), P("grid", None))
    return jax.shard_map(body, mesh=mesh, in_specs=in_specs, out_specs=out_specs, check_vma=False)
```

```python
import functools
import math

import jax
import jax.numpy as jnp
from jax import lax
from jax.experimental import pallas as pl
from jax.experimental.pallas import tpu as pltpu
from jax.sharding import PartitionSpec as P

smooth_sq = 0.0025
bf16 = jnp.bfloat16
f16 = jnp.float16
f32 = jnp.float32

NT = (((1,), (1,)), ((), ()))
WIDE = 128
TALL = 112
SHARE = 256
ROWS = 512
COLS = 256

vmem = pl.BlockSpec(memory_space=pltpu.VMEM)
smem = pl.BlockSpec(memory_space=pltpu.SMEM)
anywhere = pl.BlockSpec(memory_space=pltpu.HBM)


def params(mib):
    return pltpu.CompilerParams(vmem_limit_bytes=mib * 1024 * 1024)


def cost(flops, nbytes, trans=0):
    return pl.CostEstimate(flops=flops, bytes_accessed=nbytes, transcendentals=trans)


def chunk(ref, start):
    return ref.at[pl.ds(start, ROWS)]


def forward_kernel(
    latent_ref,
    weight_ref,
    out_weight_ref,
    forecast_ref,
    pre_out,
    padded_ref,
    pre_ref,
    hidden_ref,
    latent_copy,
    weight_copy,
    out_weight_copy,
    latent_sems,
    weight_sem,
    out_weight_sem,
    pre_sems,
):
    nodes, width = latent_ref.shape
    variables = out_weight_ref.shape[0]
    weight_load = pltpu.make_async_copy(weight_ref, weight_copy, weight_sem)
    out_weight_load = pltpu.make_async_copy(out_weight_ref, out_weight_copy, out_weight_sem)
    latent_loads = [
        pltpu.make_async_copy(chunk(latent_ref, start), chunk(latent_copy, start), latent_sems.at[start // ROWS])
        for start in range(0, nodes, ROWS)
    ]
    out_weight_load.start()
    weight_load.start()
    for load in latent_loads:
        load.start()
    out_weight_load.wait()
    turned_weight = jnp.concatenate(
        [out_weight_copy[...], jnp.zeros((WIDE - variables, width), bf16)], axis=0
    )
    padded_ref[...] = turned_weight.T
    weight_load.wait()
    stores = []
    for start in range(0, nodes, ROWS):
        rows = slice(start, start + ROWS)
        latent_loads[start // ROWS].wait()
        pre = jnp.dot(latent_copy[rows, :], weight_copy[...], preferred_element_type=f32)
        pre_ref[rows, :] = pre.astype(bf16)
        hidden_ref[rows, :] = (pre * (0.5 * jnp.tanh(0.5 * pre) + 0.5)).astype(bf16)
        store = pltpu.make_async_copy(chunk(pre_ref, start), chunk(pre_out, start), pre_sems.at[start // ROWS])
        store.start()
        stores.append(store)
        for share in range(start // SHARE, (start + ROWS) // SHARE):
            forecast_ref[share] = lax.dot_general(
                turned_weight[:TALL],
                hidden_ref[share * SHARE : (share + 1) * SHARE, :],
                NT,
                preferred_element_type=f32,
            )
    for store in stores:
        store.wait()


def pinned(value):
    return pltpu.with_memory_space_constraint(value, pltpu.HBM)


def forward(latent, weight, out_weight):
    nodes, width = latent.shape
    return pl.pallas_call(
        forward_kernel,
        in_specs=[anywhere] * 3,
        out_specs=[vmem, anywhere, vmem],
        out_shape=[
            jax.ShapeDtypeStruct((nodes // SHARE, TALL, SHARE), f32),
            pltpu.HBM((nodes, width), bf16),
            jax.ShapeDtypeStruct((width, WIDE), bf16),
        ],
        scratch_shapes=[
            pltpu.VMEM((nodes, width), bf16),
            pltpu.VMEM((nodes, width), bf16),
            pltpu.VMEM((nodes, width), bf16),
            pltpu.VMEM((width, width), bf16),
            pltpu.VMEM(out_weight.shape, bf16),
            pltpu.SemaphoreType.DMA((nodes // ROWS,)),
            pltpu.SemaphoreType.DMA,
            pltpu.SemaphoreType.DMA,
            pltpu.SemaphoreType.DMA((nodes // ROWS,)),
        ],
        compiler_params=params(32),
        cost_estimate=cost(2 * nodes * width * (width + WIDE), 20 << 20),
        name="forward",
    )(pinned(latent), pinned(weight), pinned(out_weight))


def gate_kernel(pre_hbm, hidden_out, slope_out, pre_ref, hidden_ref, slope_ref, pre_sems, hidden_sems, slope_sems):
    nodes, width = pre_hbm.shape
    loads = [
        pltpu.make_async_copy(chunk(pre_hbm, start), chunk(pre_ref, start), pre_sems.at[start // ROWS])
        for start in range(0, nodes, ROWS)
    ]
    for load in loads:
        load.start()
    stores = []
    for start in range(0, nodes, ROWS):
        rows = slice(start, start + ROWS)
        loads[start // ROWS].wait()
        for group in range(width // 128):
            columns = slice(group * 128, (group + 1) * 128)
            pre = pre_ref[rows, columns].astype(f32)
            sig = 0.5 * jnp.tanh(0.5 * pre) + 0.5
            hidden = pre * sig
            hidden_ref[group, rows, :] = hidden.astype(bf16)
            slope_ref[rows, columns] = (sig + hidden * (1.0 - sig)).astype(bf16)
        for store in (
            pltpu.make_async_copy(
                hidden_ref.at[:, pl.ds(start, ROWS)], hidden_out.at[:, pl.ds(start, ROWS)], hidden_sems.at[start // ROWS]
            ),
            pltpu.make_async_copy(chunk(slope_ref, start), chunk(slope_out, start), slope_sems.at[start // ROWS]),
        ):
            store.start()
            stores.append(store)
    for store in stores:
        store.wait()


def gates(pre):
    nodes, width = pre.shape
    sems = pltpu.SemaphoreType.DMA((nodes // ROWS,))
    return pl.pallas_call(
        gate_kernel,
        in_specs=[anywhere],
        out_specs=[anywhere] * 2,
        out_shape=[pltpu.HBM((width // 128, nodes, 128), bf16), pltpu.HBM((nodes, width), bf16)],
        scratch_shapes=[
            pltpu.VMEM((nodes, width), bf16),
            pltpu.VMEM((width // 128, nodes, 128), bf16),
            pltpu.VMEM((nodes, width), bf16),
            sems,
            sems,
            sems,
        ],
        compiler_params=params(20),
        cost_estimate=cost(0, 12 << 20),
        name="gates",
    )(pinned(pre))


def slope_function(diff):
    return diff * lax.rsqrt(diff * diff + smooth_sq)


def pair_kernel(place_ref, blocks_ref, observed_ref, area_ref, low_out, here_ref, weight_ref, totals_ref, low_ref, sems):
    members = blocks_ref.shape[0]
    variables = observed_ref.shape[0]
    at = pl.multiple_of(place_ref[0] * SHARE, SHARE)
    loads = [
        pltpu.make_async_copy(observed_ref.at[:, pl.ds(at, SHARE)], here_ref, sems.at[0]),
        pltpu.make_async_copy(area_ref.at[:, pl.ds(at, SHARE)], weight_ref, sems.at[1]),
    ]
    for load in loads:
        load.start()
    for start in range(0, TALL, 16):
        rows = slice(start, start + 16)
        values = [blocks_ref[a, rows, :] for a in range(members)]
        totals = [0.0] * members
        for a in range(members):
            for b in range(a + 1, members):
                slope = slope_function(values[a] - values[b])
                totals[a] = totals[a] + slope
                totals[b] = totals[b] - slope
        for a in range(members):
            totals_ref[a, rows, :] = totals[a]
    for load in loads:
        load.wait()
    stores = [
        pltpu.make_async_copy(
            low_ref.at[:, pl.ds(first, count)], low_out.at[:, pl.ds(first, count)], sems.at[2 + index]
        )
        for index, (first, count) in enumerate(((0, 64), (64, TALL - 64)))
    ]
    area = weight_ref[...]
    for start in range(0, TALL, 16):
        rows = slice(start, start + 16)
        real = min(16, variables - start)
        observed = here_ref[start : start + real, :]
        if real < 16:
            observed = jnp.concatenate([observed, jnp.zeros((16 - real, SHARE), f32)], axis=0)
        for a in range(members):
            own = slope_function(blocks_ref[a, rows, :] - observed)
            low_ref[a, rows, :] = (area * (own - totals_ref[a, rows, :] * (1.0 / (members - 1)))).astype(bf16)
        if start == 48:
            stores[0].start()
    stores[1].start()
    for store in stores:
        store.wait()


def pairs(place, blocks, observed, area):
    members = blocks.shape[0]
    variables = observed.shape[0]
    return pl.pallas_call(
        pair_kernel,
        in_specs=[smem, vmem, anywhere, anywhere],
        out_specs=anywhere,
        out_shape=pltpu.HBM((members, TALL, SHARE), bf16),
        scratch_shapes=[
            pltpu.VMEM((variables, SHARE), f32),
            pltpu.VMEM((1, SHARE), f32),
            pltpu.VMEM((members, TALL, SHARE), f32),
            pltpu.VMEM((members, TALL, SHARE), bf16),
            pltpu.SemaphoreType.DMA((4,)),
        ],
        compiler_params=params(8),
        cost_estimate=cost(4 << 20, 2 << 20),
        name="pairs",
    )(place, blocks, observed, area)


def position(grid_ref):
    grid = grid_ref[0]
    return grid >> 3, (grid >> 1) & 3, grid & 1


PARTS = (((2, 0), (2, 1), (1, 1), (3, 0)), ((1, 0), (3, 1), (0, 0), (0, 1)))


def turn_kernel(grid_ref, latent_ref, turned_ref):
    nodes, width = latent_ref.shape
    x_lo, z, core = position(grid_ref)
    for group in range(8):
        step = (group - z) & 3
        other_x = (group >> 2) ^ x_lo
        odd, back = step & 1, step >> 1
        part = odd * (1 - (other_x ^ back)) + (1 - odd) * (1 - back)
        place = odd * (back + 2 * (1 - part)) + (1 - odd) * (other_x + 2 * part)
        at = part * 512 + place * 64
        first = pl.multiple_of(at + (1 - core) * 256, 64)
        second = pl.multiple_of(at + core * 256, 64)
        for row in range(0, nodes, ROWS):
            columns = slice(row, row + ROWS)
            block = latent_ref[columns, group * 128 : (group + 1) * 128].T
            turned_ref[pl.ds(first, 64), columns] = block[:64]
            turned_ref[pl.ds(second, 64), columns] = block[64:]


def turned(grid, latent):
    nodes, width = latent.shape
    return pl.pallas_call(
        turn_kernel,
        in_specs=[smem, vmem],
        out_specs=vmem,
        out_shape=jax.ShapeDtypeStruct((width, nodes), bf16),
        compiler_params=params(8),
        cost_estimate=cost(0, 8 << 20),
        name="turned",
    )(grid, latent)


def turned_load(turned_hbm, start, turned_ref, sem):
    return pltpu.make_async_copy(turned_hbm.at[pl.ds(start, 256)], turned_ref, sem)


def hidden_loads(part, grid_ref, hidden_hbm, hidden_ref, sems):
    x_lo, z, core = position(grid_ref)
    return [
        pltpu.make_async_copy(
            hidden_hbm.at[(other_x ^ x_lo) * 4 + ((z + step) & 3)], hidden_ref.at[block], sems.at[block]
        )
        for block, (step, other_x) in enumerate(PARTS[part])
    ]


def first_product(turned_ref, pre_ref, out_ref):
    width = pre_ref.shape[1]
    for column in range(0, width, 512):
        columns = slice(column, column + 512)
        part = jnp.dot(turned_ref[...], pre_ref[:, columns], preferred_element_type=f32)
        out_ref[:, columns] = part.astype(bf16)


def second_product(grid_ref, flat_ref, hidden_ref, send_ref, second_ref, scratch_ref):
    width = send_ref.shape[1] - WIDE
    core = position(grid_ref)[2]
    for block in (0, 2):
        columns = jnp.concatenate([hidden_ref[block], hidden_ref[block + 1]], axis=1)
        second = jnp.dot(flat_ref[...], columns, preferred_element_type=f32)
        scratch_ref[block * 128 : (block + 2) * 128, :] = second.T.astype(bf16)
    for block in range(4):
        rows = slice(block * 64, (block + 1) * 64)
        mine = pl.multiple_of(block * 128 + core * 64, 64)
        other = pl.multiple_of(block * 128 + (1 - core) * 64, 64)
        second_ref[rows, :] = scratch_ref[pl.ds(mine, 64), :]
        send_ref[rows, width:] = scratch_ref[pl.ds(other, 64), :]


def send_a_kernel(
    grid_ref,
    low_ref,
    turned_hbm,
    slope_hbm,
    hidden_hbm,
    padded_ref,
    pre_ref,
    send_ref,
    second_ref,
    flat_ref,
    next_turned_ref,
    turn_ref,
    turned_ref,
    hidden_ref,
    scratch_ref,
    slope_ref,
    turned_sems,
    hidden_sems,
    slope_sems,
):
    nodes, width = pre_ref.shape
    slope_loads = [
        pltpu.make_async_copy(
            slope_hbm.at[pl.ds(start, ROWS)], slope_ref.at[pl.ds(start, ROWS)], slope_sems.at[start // ROWS]
        )
        for start in range(0, nodes, ROWS)
    ]
    turned_now = turned_load(turned_hbm, 0, turned_ref, turned_sems.at[0])
    turned_next = turned_load(turned_hbm, 256, next_turned_ref, turned_sems.at[1])
    hidden_now = hidden_loads(0, grid_ref, hidden_hbm, hidden_ref, hidden_sems)
    for load in slope_loads + [turned_now] + hidden_now + [turned_next]:
        load.start()
    for share in range(low_ref.shape[0]):
        columns = slice(share * SHARE, (share + 1) * SHARE)
        low = jnp.concatenate([low_ref[share], jnp.zeros((WIDE - TALL, SHARE), bf16)], axis=0)
        flat_ref[:, columns] = low
        turn_ref[columns, :] = low.T
    for start in range(0, nodes, ROWS):
        rows = slice(start, start + ROWS)
        slope_loads[start // ROWS].wait()
        for column in range(0, width, COLS):
            columns = slice(column, column + COLS)
            grad_hidden = lax.dot_general(turn_ref[rows, :], padded_ref[columns, :], NT, preferred_element_type=f32)
            pre_ref[rows, columns] = (grad_hidden * slope_ref[rows, columns].astype(f32)).astype(bf16)
    turned_now.wait()
    first_product(turned_ref, pre_ref, send_ref)
    for load in hidden_now:
        load.wait()
    second_product(grid_ref, flat_ref, hidden_ref, send_ref, second_ref, scratch_ref)
    turned_next.wait()


def keep_a_kernel(turned_hbm, pre_ref, turned_ref, second_ref, keep_ref, next_turned_ref, turned_sem):
    load = turned_load(turned_hbm, 512, next_turned_ref, turned_sem)
    load.start()
    first_product(turned_ref, pre_ref, keep_ref)
    keep_ref[:, pre_ref.shape[1] :] = second_ref[...]
    load.wait()


def send_b_kernel(
    grid_ref,
    turned_hbm,
    hidden_hbm,
    pre_ref,
    flat_ref,
    turned_ref,
    send_ref,
    second_ref,
    next_turned_ref,
    hidden_ref,
    scratch_ref,
    turned_sem,
    hidden_sems,
):
    loads = hidden_loads(1, grid_ref, hidden_hbm, hidden_ref, hidden_sems)
    loads.append(turned_load(turned_hbm, 768, next_turned_ref, turned_sem))
    for load in loads:
        load.start()
    first_product(turned_ref, pre_ref, send_ref)
    for load in loads[:-1]:
        load.wait()
    second_product(grid_ref, flat_ref, hidden_ref, send_ref, second_ref, scratch_ref)
    loads[-1].wait()


def keep_b_kernel(weight_hbm, pre_ref, turned_ref, second_ref, keep_ref, weight_ref, weight_sem):
    load = pltpu.make_async_copy(weight_hbm, weight_ref, weight_sem)
    load.start()
    first_product(turned_ref, pre_ref, keep_ref)
    keep_ref[:, pre_ref.shape[1] :] = second_ref[...]
    load.wait()


def shape(*dims):
    return jax.ShapeDtypeStruct(dims, bf16)


def send_a(grid, low, turned_latent, slope, hidden, padded):
    nodes, width = slope.shape
    return pl.pallas_call(
        send_a_kernel,
        in_specs=[smem, vmem, anywhere, anywhere, anywhere, vmem],
        out_specs=[vmem] * 5,
        out_shape=[
            shape(nodes, width),
            shape(256, width + WIDE),
            shape(256, WIDE),
            shape(WIDE, nodes),
            shape(256, nodes),
        ],
        scratch_shapes=[
            pltpu.VMEM((nodes, WIDE), bf16),
            pltpu.VMEM((256, nodes), bf16),
            pltpu.VMEM((4, nodes, 128), bf16),
            pltpu.VMEM((512, WIDE), bf16),
            pltpu.VMEM((nodes, width), bf16),
            pltpu.SemaphoreType.DMA((2,)),
            pltpu.SemaphoreType.DMA((4,)),
            pltpu.SemaphoreType.DMA((nodes // ROWS,)),
        ],
        compiler_params=params(20),
        cost_estimate=cost(nodes * width * (width // 2 + 3 * WIDE), 8 << 20),
        name="send_a",
    )(grid, low, pinned(turned_latent), pinned(slope), pinned(hidden), padded)


def keep_a(turned_latent, grad_pre, turned_now, second):
    nodes, width = grad_pre.shape
    return pl.pallas_call(
        keep_a_kernel,
        in_specs=[anywhere] + [vmem] * 3,
        out_specs=[vmem] * 2,
        out_shape=[shape(256, width + WIDE), shape(256, nodes)],
        scratch_shapes=[pltpu.SemaphoreType.DMA],
        compiler_params=params(12),
        cost_estimate=cost(nodes * width * width // 2, 4 << 20),
        name="keep_a",
    )(pinned(turned_latent), grad_pre, turned_now, second)


def send_b(grid, turned_latent, hidden, grad_pre, flat, turned_now):
    nodes, width = grad_pre.shape
    return pl.pallas_call(
        send_b_kernel,
        in_specs=[smem, anywhere, anywhere] + [vmem] * 3,
        out_specs=[vmem] * 3,
        out_shape=[shape(256, width + WIDE), shape(256, WIDE), shape(256, nodes)],
        scratch_shapes=[
            pltpu.VMEM((4, nodes, 128), bf16),
            pltpu.VMEM((512, WIDE), bf16),
            pltpu.SemaphoreType.DMA,
            pltpu.SemaphoreType.DMA((4,)),
        ],
        compiler_params=params(12),
        cost_estimate=cost(nodes * width * width // 2, 4 << 20),
        name="send_b",
    )(grid, pinned(turned_latent), pinned(hidden), grad_pre, flat, turned_now)


def keep_b(weight, grad_pre, turned_now, second):
    nodes, width = grad_pre.shape
    return pl.pallas_call(
        keep_b_kernel,
        in_specs=[anywhere] + [vmem] * 3,
        out_specs=[vmem] * 2,
        out_shape=[shape(256, width + WIDE), shape(width, width)],
        scratch_shapes=[pltpu.SemaphoreType.DMA],
        compiler_params=params(12),
        cost_estimate=cost(nodes * width * width // 2, 4 << 20),
        name="keep_b",
    )(pinned(weight), grad_pre, turned_now, second)


def latent_kernel(pre_ref, weight_ref, *refs, begin):
    out_ref, result_ref, sems = refs[-3:]
    width = pre_ref.shape[1]
    stores = []
    for row in range(0, result_ref.shape[0], ROWS):
        rows = slice(begin + row, begin + row + ROWS)
        for start in range(0, width, COLS):
            columns = slice(start, start + COLS)
            result_ref[row : row + ROWS, columns] = lax.dot_general(
                pre_ref[rows, :], weight_ref[columns, :], NT, preferred_element_type=f32
            ).astype(bf16)
        store = pltpu.make_async_copy(
            result_ref.at[pl.ds(row, ROWS)], out_ref.at[pl.ds(begin + row, ROWS)], sems.at[row // ROWS]
        )
        store.start()
        stores.append(store)
    for store in stores:
        store.wait()


def latent_gradient(grad_pre, weight, begin, so_far=None):
    nodes, width = grad_pre.shape
    half = nodes // 2
    more = [] if so_far is None else [so_far]
    return pl.pallas_call(
        functools.partial(latent_kernel, begin=begin),
        in_specs=[vmem, vmem] + [anywhere] * len(more),
        out_specs=anywhere,
        out_shape=pltpu.HBM((nodes, width), bf16),
        input_output_aliases={2: 0} if more else {},
        scratch_shapes=[pltpu.VMEM((half, width), bf16), pltpu.SemaphoreType.DMA((half // ROWS,))],
        compiler_params=params(12),
        cost_estimate=cost(nodes * width * width, 5 << 20),
        name="latent_gradient",
    )(grad_pre, weight, *more)


def finish_kernel(own_ref, *refs, factor):
    *others, first_ref, second_ref = refs
    width, variables = first_ref.shape[1], second_ref.shape[1]
    total = own_ref[...].astype(f32)
    for other in others:
        total = total + other[...].astype(f32)
    total = total * factor
    first_ref[...] = total[:, :width]
    second_ref[...] = total[:, width : width + variables]


def finish(own, others, width, variables, factor):
    rows = own.shape[0]
    return pl.pallas_call(
        functools.partial(finish_kernel, factor=factor),
        in_specs=[vmem] * (1 + len(others)),
        out_specs=[vmem] * 2,
        out_shape=[jax.ShapeDtypeStruct((rows, width), f32), jax.ShapeDtypeStruct((rows, variables), f32)],
        compiler_params=params(8),
        cost_estimate=cost(0, 1 << 20),
        name="finish",
    )(own, *others)


def moved(value, move):
    moves = []
    for member in range(8):
        for grid in range(16):
            y, x_hi, x_lo, z, core = member // 2, member % 2, grid // 8, (grid // 2) % 4, grid % 2
            y, x, z, core = move(y, x_hi * 2 + x_lo, z, core)
            target = (y * 2 + x // 2) * 16 + ((x % 2) * 4 + z) * 2 + core
            moves.append((member * 16 + grid, target))
    return lax.ppermute(value, ("member", "grid"), moves)


def summed(own, others):
    total = own.astype(f32)
    for other in others:
        total = total + other.astype(f32)
    return total


def over_core(send, keep):
    got = moved(send, lambda y, x, z, c: (y, x, z, 1 - c))
    return summed(keep, [got]).reshape(4, 64, send.shape[1])


def up(value):
    return moved(value, lambda y, x, z, c: (y, x, (z + 1) % 4, c))


def down(value):
    return moved(value, lambda y, x, z, c: (y, x, (z + 3) % 4, c))


def over_x(blocks):
    got = [
        moved(blocks[0] if k == 2 else blocks[1], lambda y, x, z, c, k=k: (y, x ^ k, z, c))
        for k in (1, 3, 2)
    ]
    return summed(blocks[0], got).astype(bf16)


def over_y(block):
    return [moved(block, lambda y, x, z, c, k=k: (y ^ k, x, z, c)) for k in (1, 3, 2)]


def body(latents, hidden_weight, output_weight, observed, node_area_weight):
    latent = latents[0]
    members = lax.axis_size("member")
    groups = lax.axis_size("grid")
    nodes, width = latent.shape
    variables = output_weight.shape[1]
    place = lax.axis_index("member").astype(jnp.int32).reshape(1)
    grid = lax.axis_index("grid").astype(jnp.int32).reshape(1)

    forecast, pre, padded = forward(latent, hidden_weight, output_weight.T)
    blocks, pre = lax.optimization_barrier(((0.25 * forecast).astype(f16), pre))
    blocks = lax.all_to_all(blocks, "member", 0, 0, tiled=True)
    hidden, slope = gates(pre)
    blocks, hidden, slope = lax.optimization_barrier((blocks, hidden, slope))
    low = pairs(place, 4.0 * blocks.astype(f32), observed, node_area_weight.reshape(1, nodes))
    low, late_grid = lax.optimization_barrier((low, grid))
    low = lax.all_to_all(low, "member", 0, 0, tiled=True)
    turned_latent = turned(late_grid, latent)
    grad_pre, rows_a, second_a, flat, turned_now = send_a(grid, low, turned_latent, slope, hidden, padded)
    kept_a, turned_now = keep_a(turned_latent, grad_pre, turned_now, second_a)
    far_up, far_down, near_up, near_down = over_core(rows_a, kept_a).astype(bf16)
    far_up, far_down, near_up, near_down, flat = lax.optimization_barrier((far_up, far_down, near_up, near_down, flat))
    upward, downward = up(far_up), down(far_down)
    from_below, from_above = up(near_up), down(near_down)
    rows_b, second_b, turned_now = send_b(grid, turned_latent, hidden, grad_pre, flat, turned_now)
    kept_b, weight_copy = keep_b(hidden_weight, grad_pre, turned_now, second_b)
    above, below, own, other = over_core(rows_b, kept_b)
    above = (above + upward.astype(f32)).astype(bf16)
    below = (below + downward.astype(f32)).astype(bf16)
    above, below, grad_pre = lax.optimization_barrier((above, below, grad_pre))
    grad_latent = latent_gradient(grad_pre, weight_copy, 0)
    own = summed(own, [up(above), from_above])
    other = summed(other, [from_below, down(below)])
    blocks = jnp.stack([own, other]).astype(bf16)
    blocks, grad_latent = lax.optimization_barrier((blocks, grad_latent))
    grad_latent = latent_gradient(grad_pre, weight_copy, nodes // 2, grad_latent)
    block, grad_latent = lax.optimization_barrier((over_x(blocks), grad_latent))
    factor = 1.0 / math.sqrt(members * nodes * groups)
    first, second = finish(block, over_y(block), width, variables, factor)
    return grad_latent[None], first, second


def solution(mesh):
    in_specs = (P("member", "grid", None), P(), P(), P(None, "grid"), P("grid"))
    out_specs = (P("member", "grid", None), P("grid", None), P("grid", None))
    return jax.shard_map(body, mesh=mesh, in_specs=in_specs, out_specs=out_specs, check_vma=False)
```

```python
import functools
import math

import jax
import jax.numpy as jnp
from jax import lax
from jax.experimental import pallas as pl
from jax.experimental.pallas import tpu as pltpu
from jax.sharding import PartitionSpec as P

smooth_sq = 0.0025
bf16 = jnp.bfloat16
f16 = jnp.float16
f32 = jnp.float32

NT = (((1,), (1,)), ((), ()))
WIDE = 128
TALL = 112
SHARE = 256
ROWS = 512
COLS = 256

vmem = pl.BlockSpec(memory_space=pltpu.VMEM)
smem = pl.BlockSpec(memory_space=pltpu.SMEM)
anywhere = pl.BlockSpec(memory_space=pltpu.HBM)


def params(mib):
    return pltpu.CompilerParams(vmem_limit_bytes=mib * 1024 * 1024)


def cost(flops, nbytes, trans=0):
    return pl.CostEstimate(flops=flops, bytes_accessed=nbytes, transcendentals=trans)


def chunk(ref, start):
    return ref.at[pl.ds(start, ROWS)]


def forward_kernel(
    latent_ref,
    weight_ref,
    out_weight_ref,
    forecast_ref,
    pre_out,
    padded_ref,
    pre_ref,
    hidden_ref,
    latent_copy,
    weight_copy,
    out_weight_copy,
    latent_sems,
    weight_sem,
    out_weight_sem,
    pre_sems,
):
    nodes, width = latent_ref.shape
    variables = out_weight_ref.shape[0]
    weight_load = pltpu.make_async_copy(weight_ref, weight_copy, weight_sem)
    out_weight_load = pltpu.make_async_copy(out_weight_ref, out_weight_copy, out_weight_sem)
    latent_loads = [
        pltpu.make_async_copy(chunk(latent_ref, start), chunk(latent_copy, start), latent_sems.at[start // ROWS])
        for start in range(0, nodes, ROWS)
    ]
    out_weight_load.start()
    weight_load.start()
    for load in latent_loads:
        load.start()
    out_weight_load.wait()
    turned_weight = jnp.concatenate(
        [out_weight_copy[...], jnp.zeros((WIDE - variables, width), bf16)], axis=0
    )
    padded_ref[...] = turned_weight.T
    weight_load.wait()
    stores = []
    for start in range(0, nodes, ROWS):
        rows = slice(start, start + ROWS)
        latent_loads[start // ROWS].wait()
        pre = jnp.dot(latent_copy[rows, :], weight_copy[...], preferred_element_type=f32)
        pre_ref[rows, :] = pre.astype(bf16)
        hidden_ref[rows, :] = (pre * (0.5 * jnp.tanh(0.5 * pre) + 0.5)).astype(bf16)
        store = pltpu.make_async_copy(chunk(pre_ref, start), chunk(pre_out, start), pre_sems.at[start // ROWS])
        store.start()
        stores.append(store)
        for share in range(start // SHARE, (start + ROWS) // SHARE):
            forecast_ref[share] = lax.dot_general(
                turned_weight[:TALL],
                hidden_ref[share * SHARE : (share + 1) * SHARE, :],
                NT,
                preferred_element_type=f32,
            )
    for store in stores:
        store.wait()


def pinned(value):
    return pltpu.with_memory_space_constraint(value, pltpu.HBM)


def forward(latent, weight, out_weight):
    nodes, width = latent.shape
    return pl.pallas_call(
        forward_kernel,
        in_specs=[anywhere] * 3,
        out_specs=[vmem, anywhere, vmem],
        out_shape=[
            jax.ShapeDtypeStruct((nodes // SHARE, TALL, SHARE), f32),
            pltpu.HBM((nodes, width), bf16),
            jax.ShapeDtypeStruct((width, WIDE), bf16),
        ],
        scratch_shapes=[
            pltpu.VMEM((nodes, width), bf16),
            pltpu.VMEM((nodes, width), bf16),
            pltpu.VMEM((nodes, width), bf16),
            pltpu.VMEM((width, width), bf16),
            pltpu.VMEM(out_weight.shape, bf16),
            pltpu.SemaphoreType.DMA((nodes // ROWS,)),
            pltpu.SemaphoreType.DMA,
            pltpu.SemaphoreType.DMA,
            pltpu.SemaphoreType.DMA((nodes // ROWS,)),
        ],
        compiler_params=params(32),
        cost_estimate=cost(2 * nodes * width * (width + WIDE), 20 << 20),
        name="forward",
    )(pinned(latent), pinned(weight), pinned(out_weight))


def gate_kernel(pre_hbm, hidden_out, slope_out, pre_ref, hidden_ref, slope_ref, pre_sems, hidden_sems, slope_sems):
    nodes, width = pre_hbm.shape
    loads = [
        pltpu.make_async_copy(chunk(pre_hbm, start), chunk(pre_ref, start), pre_sems.at[start // ROWS])
        for start in range(0, nodes, ROWS)
    ]
    for load in loads:
        load.start()
    stores = []
    for start in range(0, nodes, ROWS):
        rows = slice(start, start + ROWS)
        loads[start // ROWS].wait()
        for group in range(width // 128):
            columns = slice(group * 128, (group + 1) * 128)
            pre = pre_ref[rows, columns].astype(f32)
            sig = 0.5 * jnp.tanh(0.5 * pre) + 0.5
            hidden = pre * sig
            hidden_ref[group, rows, :] = hidden.astype(bf16)
            slope_ref[rows, columns] = (sig + hidden * (1.0 - sig)).astype(bf16)
        for store in (
            pltpu.make_async_copy(
                hidden_ref.at[:, pl.ds(start, ROWS)], hidden_out.at[:, pl.ds(start, ROWS)], hidden_sems.at[start // ROWS]
            ),
            pltpu.make_async_copy(chunk(slope_ref, start), chunk(slope_out, start), slope_sems.at[start // ROWS]),
        ):
            store.start()
            stores.append(store)
    for store in stores:
        store.wait()


def gates(pre):
    nodes, width = pre.shape
    sems = pltpu.SemaphoreType.DMA((nodes // ROWS,))
    return pl.pallas_call(
        gate_kernel,
        in_specs=[anywhere],
        out_specs=[anywhere] * 2,
        out_shape=[pltpu.HBM((width // 128, nodes, 128), bf16), pltpu.HBM((nodes, width), bf16)],
        scratch_shapes=[
            pltpu.VMEM((nodes, width), bf16),
            pltpu.VMEM((width // 128, nodes, 128), bf16),
            pltpu.VMEM((nodes, width), bf16),
            sems,
            sems,
            sems,
        ],
        compiler_params=params(20),
        cost_estimate=cost(0, 12 << 20),
        name="gates",
    )(pinned(pre))


def slope_function(diff):
    return diff * lax.rsqrt(diff * diff + smooth_sq)


def pair_kernel(place_ref, blocks_ref, observed_ref, area_ref, low_out, here_ref, weight_ref, totals_ref, low_ref, sems):
    members = blocks_ref.shape[0]
    variables = observed_ref.shape[0]
    at = pl.multiple_of(place_ref[0] * SHARE, SHARE)
    loads = [
        pltpu.make_async_copy(observed_ref.at[:, pl.ds(at, SHARE)], here_ref, sems.at[0]),
        pltpu.make_async_copy(area_ref.at[:, pl.ds(at, SHARE)], weight_ref, sems.at[1]),
    ]
    for load in loads:
        load.start()
    for start in range(0, TALL, 16):
        rows = slice(start, start + 16)
        values = [blocks_ref[a, rows, :] for a in range(members)]
        totals = [0.0] * members
        for a in range(members):
            for b in range(a + 1, members):
                slope = slope_function(values[a] - values[b])
                totals[a] = totals[a] + slope
                totals[b] = totals[b] - slope
        for a in range(members):
            totals_ref[a, rows, :] = totals[a]
    for load in loads:
        load.wait()
    stores = [
        pltpu.make_async_copy(
            low_ref.at[:, pl.ds(first, count)], low_out.at[:, pl.ds(first, count)], sems.at[2 + index]
        )
        for index, (first, count) in enumerate(((0, 64), (64, TALL - 64)))
    ]
    area = weight_ref[...]
    for start in range(0, TALL, 16):
        rows = slice(start, start + 16)
        real = min(16, variables - start)
        observed = here_ref[start : start + real, :]
        if real < 16:
            observed = jnp.concatenate([observed, jnp.zeros((16 - real, SHARE), f32)], axis=0)
        for a in range(members):
            own = slope_function(blocks_ref[a, rows, :] - observed)
            low_ref[a, rows, :] = (area * (own - totals_ref[a, rows, :] * (1.0 / (members - 1)))).astype(bf16)
        if start == 48:
            stores[0].start()
    stores[1].start()
    for store in stores:
        store.wait()


def pairs(place, blocks, observed, area):
    members = blocks.shape[0]
    variables = observed.shape[0]
    return pl.pallas_call(
        pair_kernel,
        in_specs=[smem, vmem, anywhere, anywhere],
        out_specs=anywhere,
        out_shape=pltpu.HBM((members, TALL, SHARE), bf16),
        scratch_shapes=[
            pltpu.VMEM((variables, SHARE), f32),
            pltpu.VMEM((1, SHARE), f32),
            pltpu.VMEM((members, TALL, SHARE), f32),
            pltpu.VMEM((members, TALL, SHARE), bf16),
            pltpu.SemaphoreType.DMA((4,)),
        ],
        compiler_params=params(8),
        cost_estimate=cost(4 << 20, 2 << 20),
        name="pairs",
    )(place, blocks, observed, area)


def position(grid_ref):
    grid = grid_ref[0]
    return grid >> 3, (grid >> 1) & 3, grid & 1


PARTS = (((2, 0), (2, 1), (1, 1), (3, 0)), ((1, 0), (3, 1), (0, 0), (0, 1)))


def turn_kernel(grid_ref, latent_ref, turned_ref):
    nodes, width = latent_ref.shape
    x_lo, z, core = position(grid_ref)
    for group in range(8):
        step = (group - z) & 3
        other_x = (group >> 2) ^ x_lo
        odd, back = step & 1, step >> 1
        part = odd * (1 - (other_x ^ back)) + (1 - odd) * (1 - back)
        place = odd * (back + 2 * (1 - part)) + (1 - odd) * (other_x + 2 * part)
        at = part * 512 + place * 64
        first = pl.multiple_of(at + (1 - core) * 256, 64)
        second = pl.multiple_of(at + core * 256, 64)
        for row in range(0, nodes, ROWS):
            columns = slice(row, row + ROWS)
            block = latent_ref[columns, group * 128 : (group + 1) * 128].T
            turned_ref[pl.ds(first, 64), columns] = block[:64]
            turned_ref[pl.ds(second, 64), columns] = block[64:]


def turned(grid, latent):
    nodes, width = latent.shape
    return pl.pallas_call(
        turn_kernel,
        in_specs=[smem, vmem],
        out_specs=vmem,
        out_shape=jax.ShapeDtypeStruct((width, nodes), bf16),
        compiler_params=params(8),
        cost_estimate=cost(0, 8 << 20),
        name="turned",
    )(grid, latent)


def turned_load(turned_hbm, start, turned_ref, sem):
    return pltpu.make_async_copy(turned_hbm.at[pl.ds(start, 256)], turned_ref, sem)


def hidden_loads(part, grid_ref, hidden_hbm, hidden_ref, sems):
    x_lo, z, core = position(grid_ref)
    return [
        pltpu.make_async_copy(
            hidden_hbm.at[(other_x ^ x_lo) * 4 + ((z + step) & 3)], hidden_ref.at[block], sems.at[block]
        )
        for block, (step, other_x) in enumerate(PARTS[part])
    ]


def first_product(turned_ref, pre_ref, out_ref):
    width = pre_ref.shape[1]
    for column in range(0, width, 512):
        columns = slice(column, column + 512)
        part = jnp.dot(turned_ref[...], pre_ref[:, columns], preferred_element_type=f32)
        out_ref[:, columns] = part.astype(bf16)


def second_product(grid_ref, flat_ref, hidden_ref, send_ref, second_ref, scratch_ref):
    width = send_ref.shape[1] - WIDE
    core = position(grid_ref)[2]
    for block in (0, 2):
        columns = jnp.concatenate([hidden_ref[block], hidden_ref[block + 1]], axis=1)
        second = jnp.dot(flat_ref[...], columns, preferred_element_type=f32)
        scratch_ref[block * 128 : (block + 2) * 128, :] = second.T.astype(bf16)
    for block in range(4):
        rows = slice(block * 64, (block + 1) * 64)
        mine = pl.multiple_of(block * 128 + core * 64, 64)
        other = pl.multiple_of(block * 128 + (1 - core) * 64, 64)
        second_ref[rows, :] = scratch_ref[pl.ds(mine, 64), :]
        send_ref[rows, width:] = scratch_ref[pl.ds(other, 64), :]


def send_a_kernel(
    grid_ref,
    low_ref,
    turned_hbm,
    slope_hbm,
    hidden_hbm,
    padded_ref,
    pre_ref,
    send_ref,
    second_ref,
    flat_ref,
    next_turned_ref,
    turn_ref,
    turned_ref,
    hidden_ref,
    scratch_ref,
    slope_ref,
    turned_sems,
    hidden_sems,
    slope_sems,
):
    nodes, width = pre_ref.shape
    slope_loads = [
        pltpu.make_async_copy(
            slope_hbm.at[pl.ds(start, ROWS)], slope_ref.at[pl.ds(start, ROWS)], slope_sems.at[start // ROWS]
        )
        for start in range(0, nodes, ROWS)
    ]
    turned_now = turned_load(turned_hbm, 0, turned_ref, turned_sems.at[0])
    turned_next = turned_load(turned_hbm, 256, next_turned_ref, turned_sems.at[1])
    hidden_now = hidden_loads(0, grid_ref, hidden_hbm, hidden_ref, hidden_sems)
    for load in slope_loads + [turned_now] + hidden_now + [turned_next]:
        load.start()
    for share in range(low_ref.shape[0]):
        columns = slice(share * SHARE, (share + 1) * SHARE)
        low = jnp.concatenate([low_ref[share], jnp.zeros((WIDE - TALL, SHARE), bf16)], axis=0)
        flat_ref[:, columns] = low
        turn_ref[columns, :] = low.T
    for start in range(0, nodes, ROWS):
        rows = slice(start, start + ROWS)
        slope_loads[start // ROWS].wait()
        for column in range(0, width, COLS):
            columns = slice(column, column + COLS)
            grad_hidden = lax.dot_general(turn_ref[rows, :], padded_ref[columns, :], NT, preferred_element_type=f32)
            pre_ref[rows, columns] = (grad_hidden * slope_ref[rows, columns].astype(f32)).astype(bf16)
    turned_now.wait()
    first_product(turned_ref, pre_ref, send_ref)
    for load in hidden_now:
        load.wait()
    second_product(grid_ref, flat_ref, hidden_ref, send_ref, second_ref, scratch_ref)
    turned_next.wait()


def keep_a_kernel(turned_hbm, pre_ref, turned_ref, second_ref, keep_ref, next_turned_ref, last_turned_ref, turned_sems):
    loads = [
        turned_load(turned_hbm, 512, next_turned_ref, turned_sems.at[0]),
        turned_load(turned_hbm, 768, last_turned_ref, turned_sems.at[1]),
    ]
    for load in loads:
        load.start()
    first_product(turned_ref, pre_ref, keep_ref)
    keep_ref[:, pre_ref.shape[1] :] = second_ref[...]
    for load in loads:
        load.wait()


def send_b_kernel(
    grid_ref,
    hidden_hbm,
    pre_ref,
    flat_ref,
    turned_ref,
    send_ref,
    second_ref,
    hidden_ref,
    scratch_ref,
    hidden_sems,
):
    loads = hidden_loads(1, grid_ref, hidden_hbm, hidden_ref, hidden_sems)
    for load in loads:
        load.start()
    first_product(turned_ref, pre_ref, send_ref)
    for load in loads:
        load.wait()
    second_product(grid_ref, flat_ref, hidden_ref, send_ref, second_ref, scratch_ref)


def keep_b_kernel(weight_hbm, pre_ref, turned_ref, second_ref, keep_ref, weight_ref, weight_sem):
    load = pltpu.make_async_copy(weight_hbm, weight_ref, weight_sem)
    load.start()
    first_product(turned_ref, pre_ref, keep_ref)
    keep_ref[:, pre_ref.shape[1] :] = second_ref[...]
    load.wait()


def shape(*dims):
    return jax.ShapeDtypeStruct(dims, bf16)


def send_a(grid, low, turned_latent, slope, hidden, padded):
    nodes, width = slope.shape
    return pl.pallas_call(
        send_a_kernel,
        in_specs=[smem, vmem, anywhere, anywhere, anywhere, vmem],
        out_specs=[vmem] * 5,
        out_shape=[
            shape(nodes, width),
            shape(256, width + WIDE),
            shape(256, WIDE),
            shape(WIDE, nodes),
            shape(256, nodes),
        ],
        scratch_shapes=[
            pltpu.VMEM((nodes, WIDE), bf16),
            pltpu.VMEM((256, nodes), bf16),
            pltpu.VMEM((4, nodes, 128), bf16),
            pltpu.VMEM((512, WIDE), bf16),
            pltpu.VMEM((nodes, width), bf16),
            pltpu.SemaphoreType.DMA((2,)),
            pltpu.SemaphoreType.DMA((4,)),
            pltpu.SemaphoreType.DMA((nodes // ROWS,)),
        ],
        compiler_params=params(20),
        cost_estimate=cost(nodes * width * (width // 2 + 3 * WIDE), 8 << 20),
        name="send_a",
    )(grid, low, pinned(turned_latent), pinned(slope), pinned(hidden), padded)


def keep_a(turned_latent, grad_pre, turned_now, second):
    nodes, width = grad_pre.shape
    return pl.pallas_call(
        keep_a_kernel,
        in_specs=[anywhere] + [vmem] * 3,
        out_specs=[vmem] * 3,
        out_shape=[shape(256, width + WIDE), shape(256, nodes), shape(256, nodes)],
        scratch_shapes=[pltpu.SemaphoreType.DMA((2,))],
        compiler_params=params(12),
        cost_estimate=cost(nodes * width * width // 2, 4 << 20),
        name="keep_a",
    )(pinned(turned_latent), grad_pre, turned_now, second)


def send_b(grid, hidden, grad_pre, flat, turned_now):
    nodes, width = grad_pre.shape
    return pl.pallas_call(
        send_b_kernel,
        in_specs=[smem, anywhere] + [vmem] * 3,
        out_specs=[vmem] * 2,
        out_shape=[shape(256, width + WIDE), shape(256, WIDE)],
        scratch_shapes=[
            pltpu.VMEM((4, nodes, 128), bf16),
            pltpu.VMEM((512, WIDE), bf16),
            pltpu.SemaphoreType.DMA((4,)),
        ],
        compiler_params=params(12),
        cost_estimate=cost(nodes * width * width // 2, 4 << 20),
        name="send_b",
    )(grid, pinned(hidden), grad_pre, flat, turned_now)


def keep_b(weight, grad_pre, turned_now, second):
    nodes, width = grad_pre.shape
    return pl.pallas_call(
        keep_b_kernel,
        in_specs=[anywhere] + [vmem] * 3,
        out_specs=[vmem] * 2,
        out_shape=[shape(256, width + WIDE), shape(width, width)],
        scratch_shapes=[pltpu.SemaphoreType.DMA],
        compiler_params=params(12),
        cost_estimate=cost(nodes * width * width // 2, 4 << 20),
        name="keep_b",
    )(pinned(weight), grad_pre, turned_now, second)


def latent_kernel(pre_ref, weight_ref, *refs, begin):
    out_ref, result_ref, sems = refs[-3:]
    width = pre_ref.shape[1]
    stores = []
    for row in range(0, result_ref.shape[0], ROWS):
        rows = slice(begin + row, begin + row + ROWS)
        for start in range(0, width, COLS):
            columns = slice(start, start + COLS)
            result_ref[row : row + ROWS, columns] = lax.dot_general(
                pre_ref[rows, :], weight_ref[columns, :], NT, preferred_element_type=f32
            ).astype(bf16)
        store = pltpu.make_async_copy(
            result_ref.at[pl.ds(row, ROWS)], out_ref.at[pl.ds(begin + row, ROWS)], sems.at[row // ROWS]
        )
        store.start()
        stores.append(store)
    for store in stores:
        store.wait()


def latent_gradient(grad_pre, weight, begin, so_far=None):
    nodes, width = grad_pre.shape
    half = nodes // 2
    more = [] if so_far is None else [so_far]
    return pl.pallas_call(
        functools.partial(latent_kernel, begin=begin),
        in_specs=[vmem, vmem] + [anywhere] * len(more),
        out_specs=anywhere,
        out_shape=pltpu.HBM((nodes, width), bf16),
        input_output_aliases={2: 0} if more else {},
        scratch_shapes=[pltpu.VMEM((half, width), bf16), pltpu.SemaphoreType.DMA((half // ROWS,))],
        compiler_params=params(12),
        cost_estimate=cost(nodes * width * width, 5 << 20),
        name="latent_gradient",
    )(grad_pre, weight, *more)


def finish_kernel(own_ref, *refs, factor):
    *others, first_ref, second_ref = refs
    width, variables = first_ref.shape[1], second_ref.shape[1]
    total = own_ref[...].astype(f32)
    for other in others:
        total = total + other[...].astype(f32)
    total = total * factor
    first_ref[...] = total[:, :width]
    second_ref[...] = total[:, width : width + variables]


def finish(own, others, width, variables, factor):
    rows = own.shape[0]
    return pl.pallas_call(
        functools.partial(finish_kernel, factor=factor),
        in_specs=[vmem] * (1 + len(others)),
        out_specs=[vmem] * 2,
        out_shape=[jax.ShapeDtypeStruct((rows, width), f32), jax.ShapeDtypeStruct((rows, variables), f32)],
        compiler_params=params(8),
        cost_estimate=cost(0, 1 << 20),
        name="finish",
    )(own, *others)


def moved(value, move):
    moves = []
    for member in range(8):
        for grid in range(16):
            y, x_hi, x_lo, z, core = member // 2, member % 2, grid // 8, (grid // 2) % 4, grid % 2
            y, x, z, core = move(y, x_hi * 2 + x_lo, z, core)
            target = (y * 2 + x // 2) * 16 + ((x % 2) * 4 + z) * 2 + core
            moves.append((member * 16 + grid, target))
    return lax.ppermute(value, ("member", "grid"), moves)


def summed(own, others):
    total = own.astype(f32)
    for other in others:
        total = total + other.astype(f32)
    return total


def over_core(send, keep):
    got = moved(send, lambda y, x, z, c: (y, x, z, 1 - c))
    return summed(keep, [got]).reshape(4, 64, send.shape[1])


def up(value):
    return moved(value, lambda y, x, z, c: (y, x, (z + 1) % 4, c))


def down(value):
    return moved(value, lambda y, x, z, c: (y, x, (z + 3) % 4, c))


def over_x(blocks):
    got = [
        moved(blocks[0] if k == 2 else blocks[1], lambda y, x, z, c, k=k: (y, x ^ k, z, c))
        for k in (1, 3, 2)
    ]
    return summed(blocks[0], got).astype(bf16)


def over_y(block):
    return [moved(block, lambda y, x, z, c, k=k: (y ^ k, x, z, c)) for k in (1, 3, 2)]


def body(latents, hidden_weight, output_weight, observed, node_area_weight):
    latent = latents[0]
    members = lax.axis_size("member")
    groups = lax.axis_size("grid")
    nodes, width = latent.shape
    variables = output_weight.shape[1]
    place = lax.axis_index("member").astype(jnp.int32).reshape(1)
    grid = lax.axis_index("grid").astype(jnp.int32).reshape(1)

    forecast, pre, padded = forward(latent, hidden_weight, output_weight.T)
    blocks, pre = lax.optimization_barrier(((0.25 * forecast).astype(f16), pre))
    blocks = lax.all_to_all(blocks, "member", 0, 0, tiled=True)
    hidden, slope = gates(pre)
    blocks, hidden, slope = lax.optimization_barrier((blocks, hidden, slope))
    low = pairs(place, 4.0 * blocks.astype(f32), observed, node_area_weight.reshape(1, nodes))
    low, late_grid = lax.optimization_barrier((low, grid))
    low = lax.all_to_all(low, "member", 0, 0, tiled=True)
    turned_latent = turned(late_grid, latent)
    grad_pre, rows_a, second_a, flat, turned_now = send_a(grid, low, turned_latent, slope, hidden, padded)
    kept_a, turned_now, turned_last = keep_a(turned_latent, grad_pre, turned_now, second_a)
    far_up, far_down, near_up, near_down = over_core(rows_a, kept_a).astype(bf16)
    far_up, far_down, near_up, near_down, flat = lax.optimization_barrier((far_up, far_down, near_up, near_down, flat))
    upward, downward = up(far_up), down(far_down)
    from_below, from_above = up(near_up), down(near_down)
    rows_b, second_b = send_b(grid, hidden, grad_pre, flat, turned_now)
    kept_b, weight_copy = keep_b(hidden_weight, grad_pre, turned_last, second_b)
    above, below, own, other = over_core(rows_b, kept_b)
    above = (above + upward.astype(f32)).astype(bf16)
    below = (below + downward.astype(f32)).astype(bf16)
    above, below, grad_pre = lax.optimization_barrier((above, below, grad_pre))
    grad_latent = latent_gradient(grad_pre, weight_copy, 0)
    own = summed(own, [up(above), from_above])
    other = summed(other, [from_below, down(below)])
    blocks = jnp.stack([own, other]).astype(bf16)
    blocks, grad_latent = lax.optimization_barrier((blocks, grad_latent))
    grad_latent = latent_gradient(grad_pre, weight_copy, nodes // 2, grad_latent)
    block, grad_latent = lax.optimization_barrier((over_x(blocks), grad_latent))
    factor = 1.0 / math.sqrt(members * nodes * groups)
    first, second = finish(block, over_y(block), width, variables, factor)
    return grad_latent[None], first, second


def solution(mesh):
    in_specs = (P("member", "grid", None), P(), P(), P(None, "grid"), P("grid"))
    out_specs = (P("member", "grid", None), P("grid", None), P("grid", None))
    return jax.shard_map(body, mesh=mesh, in_specs=in_specs, out_specs=out_specs, check_vma=False)
```
